128 devices in a mesh: kv: 8 (over y, core), grp: 16 (over x, z).
Axes of the slice: x: 4, y: 4, z: 4, core: 2. Of those that a mesh axis runs over, the one named last changes fastest.
Arguments:
- queries: bfloat16 [64, 128, 8, 128], P('grp', 'kv'), may hold values from -128 to 128
- new_keys: bfloat16 [64, 8, 8, 128], P('grp', 'kv'), may hold values from -5 to 5
- incoming_values: bfloat16 [64, 8, 8, 128], P('grp', 'kv'), may hold values from -6 to 6
- family: int32 [64], P('grp'), may hold values from 0 to 7
- prefix_table: int32 [8, 2048], P(None, 'grp'), may hold values from 0 to 1023, as said below
- prefix_key_pool: bfloat16 [8, 16384, 16, 128], P('kv', 'grp'), may hold values from -6 to 6
- prefix_value_pool: bfloat16 [8, 16384, 16, 128], P('kv', 'grp'), may hold values from -6 to 6
- suffix_len: int32 [64], P('grp'), may hold values from 1 to 1024, as said below
- suffix_holder: int32 [64, 64], P('grp'), may hold values from 0 to 15, as said below
- suffix_slot: int32 [64, 64], P('grp'), may hold values from 0 to 191, as said below
- suffix_key_pools: bfloat16 [8, 3072, 16, 128], P('kv', 'grp'), may hold values from -8 to 8
- suffix_value_pools: bfloat16 [8, 3072, 16, 128], P('kv', 'grp'), may hold values from -6 to 6
- out_weight: bfloat16 [16384, 16384], P('kv', 'grp'), may hold values from -0.046875 to 0.046875
Outputs:
- attended: bfloat16 [64, 8, 16384], P('grp', None, 'kv')
- mixed: bfloat16 [512, 16384], P('kv', 'grp')
The draws below stay inside these ranges and needn't reach their ends.
Inputs may be any that keep to these rules, and one draw needn't show every extreme that they name: Over the 128 columns of one index of grp, prefix_table holds every number 0 to 1023 exactly once. Page c of row r is live when c * 16 < suffix_len[r]. `suffix_holder`: entries of pages that are not live are 0. `suffix_slot`: A live page of a row of grp index o lies in slots o * 12 to o * 12 + 11 of its holder; no two live pages share a holder and slot; the rows of some grp index have exactly 12 live pages on every holder. Entries of pages that are not live are 0.
All inputs are finite; a program needn't handle non-finite values.
Results may differ from the reference program's by a relative error of at most 0.0095.
Values may be sent and summed in bfloat16 or wider, within the bound.
No kernel may reach another device: no remote copies, remote signals or barrier semaphores. Data moves between devices by JAX's collectives and lax.ppermute only.
A program may use at most 128 MiB of HBM per device.

```python
import math
import jax
import jax.numpy as jnp
from jax import lax

HQ = 128
KEY_HEADS = 8
HEAD_SIZE = 128
D = 16384
GROUP_HEADS = 16
DECODE_STEPS = 8
PAGE_TOKENS = 16
SUFFIX_PAGES = 64
BUSY = 48
FAM = 8
ROW_DEV = 4
ROW_TOTAL = 64
TOKENS = 512
PREFIX_TOKENS = 32768
PRE_PAGES_DEV = 128
PRE_PAGES = 2048
PREFIX_PAGE_POOL = 16384
OWN_PAGES = 192
CAP = 12
SUFFIX_SLOT_POOL = 3072


def suffix_layout(key):
    owners = OWN_PAGES // CAP
    key_total, key_busy, key_shift, key_force, key_fill, key_place = jax.random.split(jax.random.fold_in(key, 7001), 6)
    lowest = max(ROW_DEV, OWN_PAGES // 8)
    highest = OWN_PAGES // 2
    totals = jax.random.randint(key_total, (owners,), lowest, highest + 1)
    busiest = jax.random.randint(key_busy, (), 0, owners)
    is_busy = jnp.arange(owners) == busiest
    totals = jnp.where(is_busy, OWN_PAGES, totals)
    base_pages = totals // ROW_DEV
    remainder = totals % ROW_DEV
    row_index = jnp.arange(ROW_DEV)
    row_pages = base_pages[:, None] + (row_index[None, :] < remainder[:, None]).astype(jnp.int32)
    pair_count = ROW_DEV // 2
    spread_most = jnp.maximum(jnp.minimum(base_pages - 1, SUFFIX_PAGES - base_pages - 1), 0)
    shifts = jax.random.randint(key_shift, (owners, pair_count), 0, spread_most[:, None] + 1)
    changes = jnp.zeros((owners, ROW_DEV), jnp.int32)
    changes = changes.at[:, 0:2 * pair_count:2].set(shifts).at[:, 1:2 * pair_count:2].set(-shifts)
    row_pages = row_pages + changes
    chosen = jax.random.randint(key_force, (), 0, pair_count)
    forced_long = is_busy[:, None] & (row_index == 2 * chosen)[None, :]
    forced_short = is_busy[:, None] & (row_index == 2 * chosen + 1)[None, :]
    row_pages = jnp.where(forced_long, SUFFIX_PAGES, jnp.where(forced_short, 2 * BUSY - SUFFIX_PAGES, row_pages))
    last_fill = jax.random.randint(key_fill, (owners, ROW_DEV), 1, PAGE_TOKENS + 1)
    last_fill = jnp.where(forced_long, PAGE_TOKENS, last_fill)
    lengths = (row_pages - 1) * PAGE_TOKENS + last_fill
    first_page = jnp.cumsum(row_pages, axis=1) - row_pages
    columns = jnp.arange(SUFFIX_PAGES)
    ordinal = first_page[:, :, None] + columns[None, None, :]
    is_live = columns[None, None, :] < row_pages[:, :, None]
    shuffles = jax.vmap(lambda subkey: jax.random.permutation(subkey, OWN_PAGES))(jax.random.split(key_place, owners))
    flat_order = jnp.clip(ordinal, 0, OWN_PAGES - 1).reshape(owners, ROW_DEV * SUFFIX_PAGES)
    location = jnp.take_along_axis(shuffles, flat_order, axis=1).reshape(owners, ROW_DEV, SUFFIX_PAGES)
    holders = jnp.where(is_live, location % owners, 0)
    slots = jnp.where(is_live, jnp.arange(owners)[:, None, None] * CAP + location // owners, 0)
    return (lengths.reshape(owners * ROW_DEV), holders.reshape(owners * ROW_DEV, SUFFIX_PAGES), slots.reshape(owners * ROW_DEV, SUFFIX_PAGES))


def query_layout(key):
    key_stack = jax.random.fold_in(key, 301)
    key_rows = jax.random.fold_in(key, 303)
    gaussian_portion = jnp.clip(jax.random.normal(key_stack, (ROW_TOTAL, KEY_HEADS, DECODE_STEPS, HEAD_SIZE)), -4.0, 4.0)
    newest_keys = gaussian_portion
    chosen_rows = jax.random.randint(key_rows, (ROW_TOTAL,), 0, 4) == 0
    second_step = jnp.where(chosen_rows[:, None, None, None], newest_keys[:, :, 1:2, :], newest_keys[:, :, 1:2, :])
    joined = jnp.clip(jnp.concatenate([newest_keys[:, :, 0:1, :], second_step, newest_keys[:, :, 2:, :]], axis=2), -5.0, 5.0)
    return joined


def draw_new_keys(key, part):
    new_keys = query_layout(key)
    return new_keys.astype(jnp.bfloat16)


def draw_queries(key, part):
    new_keys = query_layout(key)
    key = jax.random.fold_in(key, 43)
    key_base, key_scale = jax.random.split(key, 2)
    spread = jnp.exp(jax.random.uniform(key_scale, (ROW_TOTAL, HQ, DECODE_STEPS), minval=math.log(1.5), maxval=math.log(3.0)))
    own_keys = jnp.repeat(new_keys, GROUP_HEADS, axis=1)
    noise = jnp.clip(jax.random.normal(key_base, (ROW_TOTAL, HQ, DECODE_STEPS, HEAD_SIZE)), -4.0, 4.0)
    final_output = noise * spread[..., None] + own_keys
    return jnp.clip(final_output, -128.0, 128.0).astype(jnp.bfloat16)


def draw_prefix_table(key, part):
    key = jax.random.fold_in(key, 23)
    devices = PRE_PAGES // PRE_PAGES_DEV
    shuffles = jax.vmap(lambda subkey: jax.random.permutation(subkey, FAM * PRE_PAGES_DEV))(jax.random.split(key, devices))
    page_table = shuffles.reshape(devices, FAM, PRE_PAGES_DEV).transpose(1, 0, 2).reshape(FAM, PRE_PAGES)
    return page_table


def draw_suffix_len(key, part):
    lengths, holders, slots = suffix_layout(key)
    return lengths


def draw_suffix_holder(key, part):
    lengths, holders, slots = suffix_layout(key)
    return holders


def draw_suffix_slot(key, part):
    lengths, holders, slots = suffix_layout(key)
    return slots


def place_ends(array, rng, least, top_value):
    extent = array.shape
    place = [jax.random.randint(jax.random.fold_in(rng, axis), (), 0, extent[axis]) for axis in range(len(extent))]
    array = array.at[tuple(place)].set(least)
    longest = extent.index(max(extent))
    place[longest] = (place[longest] + 1) % extent[longest]
    return array.at[tuple(place)].set(top_value)


def block_levels(stream_key, extent, cuts, low, high):
    loudness = 1.0
    for axis_at, blocks in cuts:
        steps = jax.random.uniform(jax.random.fold_in(jax.random.fold_in(stream_key, 6), axis_at), (blocks,), jnp.float32, low / len(cuts), high / len(cuts))
        loudness = loudness * jnp.repeat(jnp.exp(steps), extent[axis_at] // blocks).reshape((-1,) + (1,) * (len(extent) - 1 - axis_at))
    return loudness


def bell_draw(key, dims, deviation, limit, cuts=(), kind=jnp.bfloat16):
    factor_of = block_levels(key, dims, cuts, -0.22, 0.18) if cuts else 1.0
    drawn = jax.random.normal(key, dims, jnp.float32) * deviation * factor_of
    return jnp.minimum(jnp.maximum(drawn, -limit), limit).astype(kind)


def setup_inputs(seed: int = 0) -> dict:
    key_list = jax.random.split(jax.random.key(seed), 14)
    return {
        "queries": draw_queries(jax.random.fold_in(key_list[13], 71), 0),
        "new_keys": draw_new_keys(jax.random.fold_in(key_list[13], 71), 0),
        "incoming_values": bell_draw(key_list[2], (ROW_TOTAL, KEY_HEADS, DECODE_STEPS, HEAD_SIZE), 1.0, 6.0, ((0, 16), (1, 8))),
        "family": place_ends(jax.random.randint(key_list[3], (ROW_TOTAL,), 0, FAM), jax.random.fold_in(key_list[3], 1), 0, FAM - 1).astype(jnp.int32),
        "prefix_table": draw_prefix_table(jax.random.fold_in(key_list[13], 71), 0),
        "prefix_key_pool": bell_draw(key_list[5], (KEY_HEADS, PREFIX_PAGE_POOL, PAGE_TOKENS, HEAD_SIZE), 1.0, 6.0, ((0, 8), (1, 16))),
        "prefix_value_pool": bell_draw(key_list[6], (KEY_HEADS, PREFIX_PAGE_POOL, PAGE_TOKENS, HEAD_SIZE), 1.0, 6.0, ((0, 8), (1, 16))),
        "suffix_len": draw_suffix_len(jax.random.fold_in(key_list[13], 71), 0),
        "suffix_holder": draw_suffix_holder(jax.random.fold_in(key_list[13], 71), 0),
        "suffix_slot": draw_suffix_slot(jax.random.fold_in(key_list[13], 71), 0),
        "suffix_key_pools": bell_draw(key_list[10], (KEY_HEADS, SUFFIX_SLOT_POOL, PAGE_TOKENS, HEAD_SIZE), 1.4, 8.0, ((0, 8), (1, 16))),
        "suffix_value_pools": bell_draw(key_list[11], (KEY_HEADS, SUFFIX_SLOT_POOL, PAGE_TOKENS, HEAD_SIZE), 1.0, 6.0, ((0, 8), (1, 16))),
        "out_weight": bell_draw(key_list[12], (HQ * HEAD_SIZE, D), (HQ * HEAD_SIZE) ** -0.5, 0.046875, ((0, 8), (1, 16))),
    }


def reference(queries, new_keys, incoming_values, family, prefix_table, prefix_key_pool, prefix_value_pool, suffix_len, suffix_holder, suffix_slot, suffix_key_pools, suffix_value_pools, out_weight):
    page_block = jnp.arange(PRE_PAGES, dtype=jnp.int32) // PRE_PAGES_DEV
    pool_index = (page_block[None, :] * (FAM * PRE_PAGES_DEV) + prefix_table).astype(jnp.int32)
    score_scale = 1.0 / math.sqrt(HEAD_SIZE)
    query_feature_width = GROUP_HEADS * DECODE_STEPS
    step_of_query = jnp.tile(jnp.arange(DECODE_STEPS, dtype=jnp.int32), GROUP_HEADS)
    new_mask = jnp.arange(DECODE_STEPS, dtype=jnp.int32)[None, :] <= step_of_query[:, None]
    token_index = jnp.arange(SUFFIX_PAGES * PAGE_TOKENS, dtype=jnp.int32)
    prefix_mask = jnp.ones((query_feature_width, PREFIX_TOKENS), dtype=jnp.bool_)

    def one_row(inputs):
        single_query_row, key_new, value_new, family_id, length, holder_row, slot_row = inputs
        prefix_row_list = pool_index[family_id]
        key_prefix_random = prefix_key_pool[:, prefix_row_list].reshape(KEY_HEADS, PREFIX_TOKENS, HEAD_SIZE)
        value_prefix_random = prefix_value_pool[:, prefix_row_list].reshape(KEY_HEADS, PREFIX_TOKENS, HEAD_SIZE)
        suffix_row_list = (holder_row * OWN_PAGES + slot_row).astype(jnp.int32)
        key_suffix_random = suffix_key_pools[:, suffix_row_list].reshape(KEY_HEADS, SUFFIX_PAGES * PAGE_TOKENS, HEAD_SIZE)
        value_suffix_random = suffix_value_pools[:, suffix_row_list].reshape(KEY_HEADS, SUFFIX_PAGES * PAGE_TOKENS, HEAD_SIZE)
        key_all = jnp.concatenate([key_prefix_random, key_suffix_random, key_new], axis=1).astype(jnp.float32)
        value_all = jnp.concatenate([value_prefix_random, value_suffix_random, value_new], axis=1).astype(jnp.float32)
        query_tensor = single_query_row.reshape(KEY_HEADS, query_feature_width, HEAD_SIZE).astype(jnp.float32)
        scores = jnp.einsum('jqd,jkd->jqk', query_tensor, key_all, precision=lax.Precision.HIGHEST) * score_scale
        suffix_mask = jnp.broadcast_to((token_index < length)[None, :], (query_feature_width, SUFFIX_PAGES * PAGE_TOKENS))
        key_mask = jnp.concatenate([prefix_mask, suffix_mask, new_mask], axis=1)
        scores = jnp.where(key_mask[None], scores, -jnp.inf)
        row_peak = lax.optimization_barrier(jnp.max(scores, axis=-1, keepdims=True))
        weight = jnp.exp(scores - row_peak)
        weight_total = lax.optimization_barrier(jnp.sum(weight, axis=-1, keepdims=True))
        rounded = lax.optimization_barrier(weight.astype(jnp.bfloat16)).astype(jnp.float32)
        summed_output = jnp.einsum('jqk,jkd->jqd', rounded, value_all, precision=lax.Precision.HIGHEST)
        final_output = (summed_output / weight_total).reshape(KEY_HEADS, GROUP_HEADS, DECODE_STEPS, HEAD_SIZE).transpose(2, 0, 1, 3)
        return final_output.reshape(DECODE_STEPS, HQ * HEAD_SIZE).astype(jnp.bfloat16)
    attended = lax.map(one_row, (queries, new_keys, incoming_values, family, suffix_len, suffix_holder, suffix_slot))
    mixed = jnp.dot(attended.reshape(TOKENS, HQ * HEAD_SIZE), out_weight, preferred_element_type=jnp.float32).astype(jnp.bfloat16)
    return (attended, mixed)
```

```python
import functools
import math

import jax
import jax.numpy as jnp
from jax import lax
from jax.experimental import pallas as pl
from jax.experimental.pallas import tpu as pltpu
from jax.sharding import PartitionSpec as P

F32 = jnp.float32
BF16 = jnp.bfloat16
I32 = jnp.int32
NT = (((1,), (1,)), ((), ()))
TN = (((0,), (0,)), ((), ()))
LOG2E = math.log2(math.e)
NEG = -1e30
MIB = 1024 * 1024
GROUP = 2
KEY_BLOCK = 1024
KEY_SUB = 512


def vmem_spec():
    return pl.BlockSpec(memory_space=pltpu.VMEM)


def smem_spec():
    return pl.BlockSpec(memory_space=pltpu.SMEM)


def params(mib):
    return pltpu.CompilerParams(vmem_limit_bytes=mib * MIB)


def pack_kernel(
    base_ref, family_ref, length_ref, holder_ref, slot_ref, query_ref, out_ref, meta_ref, *, cap, page_len
):
    devices, _, lanes = out_ref.shape
    rows, pages = holder_ref.shape
    query = query_ref[...]
    for g in range(devices):
        out_ref[g, : query.shape[0], :] = query
    base = base_ref[0]
    holder_of = lax.broadcasted_iota(I32, (devices, lanes), 0)
    lane = lax.broadcasted_iota(I32, (devices, lanes), 1)
    counts = jnp.zeros((devices, lanes), F32)
    for r in range(rows):
        counts = jnp.where(lane == rows * cap + r, family_ref[r].astype(F32), counts)
    meta_ref[...] = counts
    for r in range(rows):
        length = length_ref[r]

        def add_page(c, carry):
            place = r * cap + slot_ref[r, c] - base
            live = jnp.clip(length - c * page_len, 0, page_len)
            hit = (lane == place) & (holder_of == holder_ref[r, c]) & (live > 0)
            meta_ref[...] = jnp.where(hit, live.astype(F32), meta_ref[...])
            return carry

        lax.fori_loop(0, pages, add_page, 0, unroll=4)
    meta = meta_ref[...]
    tile_row = lax.broadcasted_iota(I32, (16, lanes), 0)
    for g in range(devices):
        tile = jnp.where(tile_row == 0, jnp.broadcast_to(meta[g : g + 1, :], (16, lanes)), 0.0)
        out_ref[g, query.shape[0] :, :] = tile.astype(BF16)


def arrange_kernel(table_ref, key_ref, value_ref, suffix_value_ref, key_out, value_out, suffix_out, page_ref):
    pages = key_ref.shape[0]
    fams = key_out.shape[0]
    per_fam = pages // fams
    page_len, head_dim = key_ref.shape[1:]
    block_pages = 128 // page_len

    for f in range(fams):

        def move_block(b, carry):
            for i in range(block_pages):
                page = table_ref[f, b * block_pages + i]
                at = pl.multiple_of(b * 128 + i * page_len, page_len)
                key_out[f, pl.ds(at, page_len), :] = key_ref[page]
                page_ref[i * page_len : (i + 1) * page_len, :] = value_ref[page]
            turned = page_ref[...].T
            value_out[f, :, pl.ds(pl.multiple_of(b * 128, 128), 128)] = turned
            return carry

        lax.fori_loop(0, per_fam // block_pages, move_block, 0)
    for g in range(suffix_value_ref.shape[0]):
        suffix_out[g] = suffix_value_ref[g].T


def attend_kernel(
    meta_ref,
    recv_ref,
    key_ref,
    value_ref,
    suffix_key_ref,
    suffix_value_ref,
    out_ref,
    score_a,
    score_b,
    top_a,
    top_b,
    score_s,
    lse_ref,
    pair_ref,
    wait_ref,
    *,
    rows_dev,
    cap,
    page_len,
    width,
):
    devices = recv_ref.shape[0]
    rows = devices * rows_dev
    fams, prefix, head_dim = key_ref.shape
    span = GROUP * width
    scale = LOG2E / math.sqrt(head_dim)
    blocks = prefix // KEY_BLOCK
    subs = KEY_BLOCK // KEY_SUB
    buffers = ((score_a, top_a), (score_b, top_b))
    suffix = cap * page_len

    for f in range(fams):
        wait_ref[f] = -1

    def pair_row(r, n):
        fam = meta_ref[r // rows_dev, rows_dev * cap + r % rows_dev]
        first = wait_ref[fam]
        full = first >= 0
        pair_ref[n, 0] = fam
        pair_ref[n, 1] = first
        pair_ref[n, 2] = r
        wait_ref[fam] = jnp.where(full, -1, r)
        return n + full.astype(I32)

    groups = lax.fori_loop(0, rows, pair_row, 0)
    for f in range(fams):
        left = wait_ref[f]
        pair_ref[groups, 0] = f
        pair_ref[groups, 1] = left
        pair_ref[groups, 2] = left
        groups = groups + (left >= 0).astype(I32)

    def load_queries(g):
        parts = []
        for i in range(GROUP):
            r = pair_ref[g, 1 + i]
            at = pl.multiple_of((r % rows_dev) * width, width)
            parts.append(recv_ref[r // rows_dev, pl.ds(at, width), :])
        return jnp.concatenate(parts, axis=0)

    def fold_max(scores):
        return jnp.max(scores.reshape(scores.shape[0] // 8, 8, scores.shape[1]), axis=0)

    def fold_sum(values):
        return jnp.sum(values.reshape(values.shape[0] // 8, 8, values.shape[1]), axis=0)

    def score_sub(query, fam, block, sub, into):
        at = block * KEY_BLOCK + sub * KEY_SUB
        scores = lax.dot_general(
            key_ref[fam, at : at + KEY_SUB, :], query, NT, preferred_element_type=F32
        )
        into[0][sub * KEY_SUB : (sub + 1) * KEY_SUB, :] = scores
        return fold_max(scores)

    first_query = load_queries(0)
    first_fam = pair_ref[0, 0]
    top = None
    for s in range(subs):
        peak = score_sub(first_query, first_fam, 0, s, buffers[0])
        top = peak if top is None else jnp.maximum(top, peak)
    top_a[...] = top
    lse_ref[...] = jnp.zeros_like(lse_ref)
    token = lax.broadcasted_iota(I32, (page_len, width), 0)

    def attend_group(g, carry):
        fam = pair_ref[g, 0]
        after = jnp.minimum(g + 1, groups - 1)
        next_fam = pair_ref[after, 0]
        query = load_queries(g)
        next_query = load_queries(after)
        tops = []
        for i in range(GROUP):
            r = pair_ref[g, 1 + i]
            owner = r // rows_dev
            scores = lax.dot_general(
                suffix_key_ref[owner],
                query[i * width : (i + 1) * width, :],
                NT,
                preferred_element_type=F32,
            )
            masked = []
            for p in range(cap):
                live = meta_ref[owner, (r % rows_dev) * cap + p]
                masked.append(
                    jnp.where(token < live, scores[p * page_len : (p + 1) * page_len, :], NEG)
                )
            masked = jnp.concatenate(masked, axis=0)
            score_s[:, i * width : (i + 1) * width] = masked
            tops.append(fold_max(masked))
        suffix_top = jnp.concatenate(tops, axis=1)
        peak = total = acc = None
        for b in range(blocks):
            now, later = buffers[b % 2], buffers[(b + 1) % 2]
            block_top = now[1][...]
            if b == 0:
                block_top = jnp.maximum(block_top, suffix_top)
            block_peak = jnp.max(block_top, axis=0, keepdims=True) * scale
            if peak is None:
                new_peak = block_peak
            else:
                new_peak = jnp.maximum(peak, block_peak)
                factor = jnp.exp2(peak - new_peak)
                total = total * factor
                acc = acc * factor
            peak = new_peak
            top = None
            for s in range(subs):
                if b + 1 < blocks:
                    sub_top = score_sub(query, fam, b + 1, s, later)
                else:
                    sub_top = score_sub(next_query, next_fam, 0, s, later)
                top = sub_top if top is None else jnp.maximum(top, sub_top)
                weight = jnp.exp2(now[0][s * KEY_SUB : (s + 1) * KEY_SUB, :] * scale - peak)
                sub_total = fold_sum(weight)
                total = sub_total if total is None else total + sub_total
                at = b * KEY_BLOCK + s * KEY_SUB
                part = jnp.dot(
                    value_ref[fam, :, at : at + KEY_SUB],
                    weight.astype(BF16),
                    preferred_element_type=F32,
                )
                acc = part if acc is None else acc + part
            later[1][...] = top
            if b == 0:
                weight = jnp.exp2(score_s[...] * scale - peak)
                total = total + fold_sum(weight)
                weight = weight.astype(BF16)
                parts = []
                for i in range(GROUP):
                    owner = pair_ref[g, 1 + i] // rows_dev
                    parts.append(
                        jnp.dot(
                            suffix_value_ref[owner],
                            weight[:, i * width : (i + 1) * width],
                            preferred_element_type=F32,
                        )
                    )
                acc = acc + jnp.concatenate(parts, axis=1)
        total = jnp.sum(total, axis=0, keepdims=True)
        lse = peak + jnp.log2(total)
        high = lse.astype(BF16).astype(F32)
        middle = (lse - high).astype(BF16).astype(F32)
        low = lse - high - middle
        acc = (acc * (1.0 / total)).astype(BF16)
        for i in range(GROUP):
            r = pair_ref[g, 1 + i]
            owner, at = r // rows_dev, r % rows_dev
            cols = slice(i * width, (i + 1) * width)
            out_ref[owner, pl.ds(pl.multiple_of(at * head_dim, head_dim), head_dim), :] = acc[:, cols]
            lse_ref[owner, pl.ds(at, 1), :] = high[:, cols]
            lse_ref[owner, pl.ds(rows_dev + at, 1), :] = middle[:, cols]
            lse_ref[owner, pl.ds(2 * rows_dev + at, 1), :] = low[:, cols]
        return carry

    lax.fori_loop(0, groups, attend_group, 0)
    out_ref[:, rows_dev * head_dim :, :] = lse_ref[...].astype(BF16)


def merge_kernel(recv_ref, query_ref, key_ref, value_ref, out_ref, send_ref, *, steps):
    devices = recv_ref.shape[0]
    rows = key_ref.shape[0]
    head_dim = recv_ref.shape[2]
    width = query_ref.shape[0] // rows
    scale = LOG2E / math.sqrt(head_dim)
    tail = recv_ref[:, rows * head_dim :, :].astype(F32)
    fresh = lax.broadcasted_iota(I32, (steps, width), 0)
    step = lax.broadcasted_iota(I32, (steps, width), 1) % steps
    for r in range(rows):
        scores = lax.dot_general(
            key_ref[r], query_ref[r * width : (r + 1) * width, :], NT, preferred_element_type=F32
        )
        scores = jnp.where(fresh <= step, scores * scale, NEG)
        new_peak = jnp.max(scores, axis=0, keepdims=True)
        weight = jnp.exp2(scores - new_peak)
        new_total = jnp.sum(weight, axis=0, keepdims=True)
        new_acc = lax.dot_general(
            value_ref[r], weight.astype(BF16), TN, preferred_element_type=F32
        )
        lse = tail[:, r, :] + tail[:, rows + r, :] + tail[:, 2 * rows + r, :]
        peak = jnp.maximum(jnp.max(lse, axis=0, keepdims=True), new_peak)
        share = jnp.exp2(lse - peak)
        new_share = jnp.exp2(new_peak - peak)
        total = jnp.sum(share, axis=0, keepdims=True) + new_share * new_total
        acc = new_acc * new_share
        for g in range(devices):
            part = recv_ref[g, r * head_dim : (r + 1) * head_dim, :].astype(F32)
            acc = acc + part * share[g : g + 1, :]
        turned = (acc * (1.0 / total)).T.astype(BF16)
        for h in range(width // steps):
            tile = turned[h * steps : (h + 1) * steps, :]
            cols = slice(h * head_dim, (h + 1) * head_dim)
            out_ref[r, :, cols] = tile
            for g in range(devices):
                send_ref[g, r * steps : (r + 1) * steps, cols] = tile


def on_device(
    queries,
    new_keys,
    incoming_values,
    family,
    prefix_table,
    prefix_key_pool,
    prefix_value_pool,
    suffix_len,
    suffix_holder,
    suffix_slot,
    suffix_key_pools,
    suffix_value_pools,
    out_weight,
):
    devices = lax.axis_size("grp")
    heads = lax.axis_size("kv")
    row_dev, local_heads, steps, head_dim = queries.shape
    width = local_heads * steps
    fams, pages_dev = prefix_table.shape
    page_len = prefix_key_pool.shape[2]
    own_pages = suffix_key_pools.shape[1]
    cap = own_pages // devices
    suffix = cap * page_len
    rows = row_dev * devices
    flat_query = queries.reshape(row_dev * width, head_dim)
    sent_rows = row_dev * width + 16
    base = (lax.axis_index("grp") * cap).astype(I32).reshape(1)

    packed = pl.pallas_call(
        functools.partial(pack_kernel, cap=cap, page_len=page_len),
        out_shape=jax.ShapeDtypeStruct((devices, sent_rows, head_dim), BF16),
        in_specs=[smem_spec()] * 5 + [vmem_spec()],
        out_specs=vmem_spec(),
        scratch_shapes=[pltpu.VMEM((devices, head_dim), F32)],
        compiler_params=params(8),
        name="pack",
    )(base, family, suffix_len, suffix_holder, suffix_slot, flat_query)

    recv = lax.all_to_all(packed, "grp", 0, 0, tiled=True)

    sorted_keys, sorted_values, turned_suffix = pl.pallas_call(
        arrange_kernel,
        out_shape=[
            jax.ShapeDtypeStruct((fams, pages_dev * page_len, head_dim), BF16),
            jax.ShapeDtypeStruct((fams, head_dim, pages_dev * page_len), BF16),
            jax.ShapeDtypeStruct((devices, head_dim, suffix), BF16),
        ],
        in_specs=[smem_spec()] + [vmem_spec()] * 3,
        out_specs=[vmem_spec()] * 3,
        scratch_shapes=[pltpu.VMEM((128, head_dim), BF16)],
        compiler_params=params(24),
        name="arrange",
        cost_estimate=pl.CostEstimate(flops=0, bytes_accessed=20 * MIB, transcendentals=0),
    )(
        prefix_table,
        prefix_key_pool[0],
        prefix_value_pool[0],
        suffix_value_pools.reshape(devices, suffix, head_dim),
    )

    meta = recv[:, row_dev * width, :].astype(I32)
    span = GROUP * width
    most_groups = rows // GROUP + fams + 1
    partial = pl.pallas_call(
        functools.partial(attend_kernel, rows_dev=row_dev, cap=cap, page_len=page_len, width=width),
        out_shape=jax.ShapeDtypeStruct((devices, row_dev * head_dim + 16, width), BF16),
        in_specs=[smem_spec()] + [vmem_spec()] * 5,
        out_specs=vmem_spec(),
        scratch_shapes=[
            pltpu.VMEM((KEY_BLOCK, span), F32),
            pltpu.VMEM((KEY_BLOCK, span), F32),
            pltpu.VMEM((8, span), F32),
            pltpu.VMEM((8, span), F32),
            pltpu.VMEM((suffix, span), F32),
            pltpu.VMEM((devices, 16, width), F32),
            pltpu.SMEM((most_groups, 3), I32),
            pltpu.SMEM((fams,), I32),
        ],
        compiler_params=params(40),
        name="attend",
        cost_estimate=pl.CostEstimate(
            flops=4 * rows * width * pages_dev * page_len * head_dim,
            bytes_accessed=14 * MIB,
            transcendentals=rows * width * pages_dev * page_len,
        ),
    )(
        meta,
        recv,
        sorted_keys,
        sorted_values,
        suffix_key_pools.reshape(devices, suffix, head_dim),
        turned_suffix,
    )

    returned = lax.all_to_all(partial, "grp", 0, 0, tiled=True)

    attended, spread = pl.pallas_call(
        functools.partial(merge_kernel, steps=steps),
        out_shape=[
            jax.ShapeDtypeStruct((row_dev, steps, local_heads * head_dim), BF16),
            jax.ShapeDtypeStruct((devices, row_dev * steps, local_heads * head_dim), BF16),
        ],
        in_specs=[vmem_spec()] * 4,
        out_specs=[vmem_spec()] * 2,
        compiler_params=params(12),
        name="merge",
    )(returned, flat_query, new_keys[:, 0], incoming_values[:, 0])

    tokens = lax.all_to_all(spread, "grp", 0, 0, tiled=True)
    tokens = tokens.reshape(rows * steps, local_heads * head_dim)
    product = jnp.dot(tokens, out_weight, preferred_element_type=F32).astype(BF16)
    shares = lax.all_to_all(
        product.reshape(heads, rows * steps // heads, out_weight.shape[1]), "kv", 0, 0, tiled=True
    )
    mixed = jnp.sum(shares.astype(F32), axis=0).astype(BF16)
    return (attended, mixed)


def solution(mesh):
    in_specs = (
        P("grp", "kv", None, None),
        P("grp", "kv", None, None),
        P("grp", "kv", None, None),
        P("grp"),
        P(None, "grp"),
        P("kv", "grp", None, None),
        P("kv", "grp", None, None),
        P("grp"),
        P("grp", None),
        P("grp", None),
        P("kv", "grp", None, None),
        P("kv", "grp", None, None),
        P("kv", "grp"),
    )
    out_specs = (P("grp", None, "kv"), P("kv", "grp"))
    return jax.shard_map(
        on_device, mesh=mesh, in_specs=in_specs, out_specs=out_specs, check_vma=False
    )
```

```python
import functools
import math

import jax
import jax.numpy as jnp
from jax import lax
from jax.experimental import pallas as pl
from jax.experimental.pallas import tpu as pltpu
from jax.sharding import PartitionSpec as P

F32 = jnp.float32
BF16 = jnp.bfloat16
I32 = jnp.int32
NT = (((1,), (1,)), ((), ()))
TN = (((0,), (0,)), ((), ()))
LOG2E = math.log2(math.e)
NEG = -1e30
MIB = 1024 * 1024
GROUP = 2
KEY_BLOCK = 1024
KEY_SUB = 512


def vmem_spec():
    return pl.BlockSpec(memory_space=pltpu.VMEM)


def smem_spec():
    return pl.BlockSpec(memory_space=pltpu.SMEM)


def any_spec():
    return pl.BlockSpec(memory_space=pl.ANY)


def in_hbm(x):
    return pltpu.with_memory_space_constraint(x, pltpu.HBM)


def params(mib):
    return pltpu.CompilerParams(vmem_limit_bytes=mib * MIB)


def pack_kernel(
    base_ref,
    family_ref,
    length_ref,
    holder_ref,
    slot_ref,
    query_ref,
    out_ref,
    *,
    cap,
    page_len,
):
    devices, sent, lanes = out_ref.shape
    rows, pages = holder_ref.shape
    body = sent - 16
    for g in range(devices):
        out_ref[g, :body, :] = query_ref[:body, :]
    base = base_ref[0]
    holder_of = lax.broadcasted_iota(I32, (devices, lanes), 0)
    lane = lax.broadcasted_iota(I32, (devices, lanes), 1)
    meta = jnp.zeros((devices, lanes), I32)
    for r in range(rows):
        meta = jnp.where(lane == rows * cap + r, family_ref[r], meta)
    place_of = holder_of * lanes + lane
    for r in range(rows):
        length = length_ref[r]

        def add_page(c, meta):
            live = jnp.clip(length - c * page_len, 0, page_len)
            place = holder_ref[r, c] * lanes + r * cap + slot_ref[r, c] - base
            place = jnp.where(live > 0, place, -1)
            return jnp.where(place_of == place, live, meta)

        meta = lax.fori_loop(0, pages, add_page, meta, unroll=8)
    meta = meta.astype(F32)
    tile_row = lax.broadcasted_iota(I32, (16, lanes), 0)
    for g in range(devices):
        tile = jnp.where(tile_row == 0, jnp.broadcast_to(meta[g : g + 1, :], (16, lanes)), 0.0)
        out_ref[g, body:, :] = tile.astype(BF16)


def arrange_kernel(core_ref, table_ref, *refs, turn):
    @pl.when(core_ref[0] == turn)
    def _():
        arrange_pages(table_ref, *refs[:3], *refs[-11:])


def arrange_pages(
    table_ref,
    key_hbm,
    value_hbm,
    suffix_value_hbm,
    key_out,
    value_out,
    suffix_out,
    key_ref,
    value_ref,
    suffix_ref,
    key_done,
    value_done,
    suffix_done,
    in_sems,
    out_sems,
):
    pages, page_len, head_dim = key_ref.shape
    fams = key_done.shape[0]
    per_fam = pages // fams
    span = 256
    block = span // page_len

    loads = [
        pltpu.make_async_copy(src, dst, in_sems.at[i])
        for i, (src, dst) in enumerate(
            ((value_hbm, value_ref), (key_hbm, key_ref), (suffix_value_hbm, suffix_ref))
        )
    ]
    for load in loads:
        load.start()
    row = lax.broadcasted_iota(I32, (head_dim, head_dim), 0)
    column = lax.broadcasted_iota(I32, (head_dim, head_dim), 1)
    identity = (row == column).astype(F32).astype(BF16)

    def turn(values):
        return lax.dot_general(identity, values, NT, preferred_element_type=F32).astype(BF16)

    stores = []
    loads[0].wait()
    for f in range(fams):

        def turn_block(b, carry):
            listed = [table_ref[f, b * block + i] for i in range(block)]
            values = jnp.concatenate([value_ref[page] for page in listed], axis=0)
            value_done[f, :, pl.ds(pl.multiple_of(b * span, span), span)] = turn(values)
            return carry

        lax.fori_loop(0, per_fam // block, turn_block, 0, unroll=4)
        stores.append(
            pltpu.make_async_copy(value_done.at[f], value_out.at[f], out_sems.at[f])
        )
        stores[-1].start()
    loads[1].wait()
    for f in range(fams):

        def move_block(b, carry):
            for i in range(block):
                at = pl.multiple_of(b * span + i * page_len, page_len)
                key_done[f, pl.ds(at, page_len), :] = key_ref[table_ref[f, b * block + i]]
            return carry

        lax.fori_loop(0, per_fam // block, move_block, 0, unroll=2)
        stores.append(
            pltpu.make_async_copy(key_done.at[f], key_out.at[f], out_sems.at[fams + f])
        )
        stores[-1].start()
    loads[2].wait()
    for g in range(suffix_ref.shape[0]):
        suffix_done[g] = turn(suffix_ref[g])
    stores.append(pltpu.make_async_copy(suffix_done, suffix_out, out_sems.at[2 * fams]))
    stores[-1].start()
    for store in stores:
        store.wait()


def attend_kernel(
    meta_ref,
    recv_ref,
    key_hbm,
    value_hbm,
    suffix_key_hbm,
    suffix_value_hbm,
    out_ref,
    key_ref,
    value_ref,
    suffix_key_ref,
    suffix_value_ref,
    score_a,
    score_b,
    top_a,
    top_b,
    score_s,
    top_s,
    lse_ref,
    pair_ref,
    count_ref,
    sems,
    key_sems,
    value_sems,
    *,
    first_row,
    rows_here,
    rows_dev,
    cap,
    page_len,
    width,
):
    devices = out_ref.shape[0]
    rows = devices * rows_here
    fams, prefix, head_dim = key_ref.shape
    scale = LOG2E / math.sqrt(head_dim)
    blocks = prefix // KEY_BLOCK
    subs = KEY_BLOCK // KEY_SUB
    buffers = ((score_a, top_a), (score_b, top_b))

    def key_load(f):
        return pltpu.make_async_copy(key_hbm.at[f], key_ref.at[f], key_sems.at[f])

    def value_load(f):
        return pltpu.make_async_copy(value_hbm.at[f], value_ref.at[f], value_sems.at[f])

    suffix_loads = [
        pltpu.make_async_copy(suffix_key_hbm, suffix_key_ref, sems.at[0]),
        pltpu.make_async_copy(suffix_value_hbm, suffix_value_ref, sems.at[1]),
    ]
    key_load(0).start()
    suffix_loads[0].start()
    value_load(0).start()
    suffix_loads[1].start()
    for f in range(1, fams):
        key_load(f).start()
        value_load(f).start()

    def row_family(r):
        return meta_ref[r // rows_here, rows_dev * cap + first_row + r % rows_here]

    for f in range(fams):
        count_ref[0, f] = 0

    def count_row(r, carry):
        fam = row_family(r)
        count_ref[0, fam] = count_ref[0, fam] + 1
        return carry

    lax.fori_loop(0, rows, count_row, 0, unroll=4)
    groups = 0
    for f in range(fams):
        count_ref[1, f] = 2 * groups
        groups = groups + (count_ref[0, f] + 1) // 2

    def place_row(r, carry):
        fam = row_family(r)
        at = count_ref[1, fam]
        count_ref[1, fam] = at + 1
        pair_ref[at // 2, 0] = fam
        pair_ref[at // 2, 1 + at % 2] = r

        @pl.when(at % 2 == 0)
        def _():
            pair_ref[at // 2, 2] = r

        return carry

    lax.fori_loop(0, rows, place_row, 0, unroll=4)
    count_ref[0, 0] = 0

    def families_to(fam):
        def one(f, carry):
            key_load(f).wait()
            value_load(f).wait()
            return carry

        lax.fori_loop(count_ref[0, 0], fam + 1, one, 0)
        count_ref[0, 0] = jnp.maximum(count_ref[0, 0], fam + 1)

    tail = rows_here * head_dim
    lse_ref[...] = jnp.zeros_like(lse_ref)

    def load_queries(g):
        parts = []
        for i in range(GROUP):
            r = pair_ref[g, 1 + i]
            at = pl.multiple_of((r % rows_here) * width, width)
            parts.append(recv_ref[r // rows_here, pl.ds(at, width), :])
        return jnp.concatenate(parts, axis=0)

    def fold_max(scores):
        return jnp.max(scores.reshape(scores.shape[0] // 8, 8, scores.shape[1]), axis=0)

    def fold_sum(values):
        return jnp.sum(values.reshape(values.shape[0] // 8, 8, values.shape[1]), axis=0)

    def score_sub(query, fam, block, sub, into):
        at = block * KEY_BLOCK + sub * KEY_SUB
        scores = lax.dot_general(
            key_ref[fam, at : at + KEY_SUB, :], query, NT, preferred_element_type=F32
        )
        into[0][sub * KEY_SUB : (sub + 1) * KEY_SUB, :] = scores
        return fold_max(scores)

    token = lax.broadcasted_iota(I32, (page_len, width), 0)

    def score_suffix(query, g):
        for i in range(GROUP):
            r = pair_ref[g, 1 + i]
            owner = r // rows_here
            first_live = (first_row + r % rows_here) * cap
            cols = slice(i * width, (i + 1) * width)
            scores = lax.dot_general(
                suffix_key_ref[owner], query[cols, :], NT, preferred_element_type=F32
            )
            masked = jnp.concatenate(
                [
                    jnp.where(
                        token < meta_ref[owner, first_live + p],
                        scores[p * page_len : (p + 1) * page_len, :],
                        NEG,
                    )
                    for p in range(cap)
                ],
                axis=0,
            )
            score_s[:, cols] = masked
            top_s[:, cols] = fold_max(masked)

    first_query = load_queries(0)
    first_fam = pair_ref[0, 0]
    families_to(first_fam)
    suffix_loads[0].wait()
    top = None
    for s in range(subs):
        sub_top = score_sub(first_query, first_fam, 0, s, buffers[0])
        top = sub_top if top is None else jnp.maximum(top, sub_top)
    top_a[...] = top
    score_suffix(first_query, 0)
    suffix_loads[1].wait()

    def attend_group(g, carry):
        fam = pair_ref[g, 0]
        after = jnp.minimum(g + 1, groups - 1)
        next_fam = pair_ref[after, 0]
        families_to(next_fam)
        query = load_queries(g)
        next_query = load_queries(after)
        peak = total = acc = None
        for b in range(blocks):
            now, later = buffers[b % 2], buffers[(b + 1) % 2]
            block_top = now[1][...]
            if b == 0:
                block_top = jnp.maximum(block_top, top_s[...])
            block_peak = jnp.max(block_top, axis=0, keepdims=True) * scale
            if peak is None:
                new_peak = block_peak
            else:
                new_peak = jnp.maximum(peak, block_peak)
                factor = jnp.exp2(peak - new_peak)
                total = total * factor
                acc = acc * factor
            peak = new_peak
            if b == 0:
                weight = jnp.exp2(score_s[...] * scale - peak)
                total = fold_sum(weight)
                weight = weight.astype(BF16)
                acc = jnp.concatenate(
                    [
                        jnp.dot(
                            suffix_value_ref[pair_ref[g, 1 + i] // rows_here],
                            weight[:, i * width : (i + 1) * width],
                            preferred_element_type=F32,
                        )
                        for i in range(GROUP)
                    ],
                    axis=1,
                )
            top = None
            for s in range(subs):
                if b + 1 < blocks:
                    sub_top = score_sub(query, fam, b + 1, s, later)
                else:
                    sub_top = score_sub(next_query, next_fam, 0, s, later)
                top = sub_top if top is None else jnp.maximum(top, sub_top)
                weight = jnp.exp2(now[0][s * KEY_SUB : (s + 1) * KEY_SUB, :] * scale - peak)
                total = total + fold_sum(weight)
                at = b * KEY_BLOCK + s * KEY_SUB
                acc = acc + jnp.dot(
                    value_ref[fam, :, at : at + KEY_SUB],
                    weight.astype(BF16),
                    preferred_element_type=F32,
                )
            later[1][...] = top
        score_suffix(next_query, after)
        total = jnp.sum(total, axis=0, keepdims=True)
        lse = peak + jnp.log2(total)
        high = lse.astype(BF16).astype(F32)
        middle = (lse - high).astype(BF16).astype(F32)
        low = lse - high - middle
        acc = (acc * (1.0 / total)).astype(BF16)
        for i in range(GROUP):
            r = pair_ref[g, 1 + i]
            owner, at = r // rows_here, r % rows_here
            cols = slice(i * width, (i + 1) * width)
            out_ref[owner, pl.ds(pl.multiple_of(at * head_dim, head_dim), head_dim), :] = acc[:, cols]
            lse_ref[owner, pl.ds(at, 1), :] = high[:, cols]
            lse_ref[owner, pl.ds(rows_dev + at, 1), :] = middle[:, cols]
            lse_ref[owner, pl.ds(2 * rows_dev + at, 1), :] = low[:, cols]
        return carry

    lax.fori_loop(0, groups, attend_group, 0)
    families_to(fams - 1)
    out_ref[:, tail:, :] = lse_ref[...].astype(BF16)


def merge_kernel(
    recv_ref,
    query_ref,
    key_ref,
    value_ref,
    out_ref,
    send_ref,
):
    devices, _, head_dim = recv_ref.shape
    rows, steps, _ = out_ref.shape
    width = query_ref.shape[0] // rows
    scale = LOG2E / math.sqrt(head_dim)
    tail = recv_ref[:, rows * head_dim :, :].astype(F32)
    fresh = lax.broadcasted_iota(I32, (steps, width), 0)
    step = lax.broadcasted_iota(I32, (steps, width), 1) % steps
    for r in range(rows):
        scores = lax.dot_general(
            key_ref[r],
            query_ref[r * width : (r + 1) * width, :],
            NT,
            preferred_element_type=F32,
        )
        scores = jnp.where(fresh <= step, scores * scale, NEG)
        new_peak = jnp.max(scores, axis=0, keepdims=True)
        weight = jnp.exp2(scores - new_peak)
        new_total = jnp.sum(weight, axis=0, keepdims=True)
        new_acc = lax.dot_general(
            value_ref[r], weight.astype(BF16), TN, preferred_element_type=F32
        )
        lse = tail[:, r, :] + tail[:, rows + r, :] + tail[:, 2 * rows + r, :]
        peak = jnp.maximum(jnp.max(lse, axis=0, keepdims=True), new_peak)
        share = jnp.exp2(lse - peak)
        new_share = jnp.exp2(new_peak - peak)
        total = jnp.sum(share, axis=0, keepdims=True) + new_share * new_total
        acc = new_acc * new_share
        for g in range(devices):
            part = recv_ref[g, r * head_dim : (r + 1) * head_dim, :].astype(F32)
            acc = acc + part * share[g : g + 1, :]
        turned = (acc * (1.0 / total)).T.astype(BF16)
        for h in range(width // steps):
            tile = turned[h * steps : (h + 1) * steps, :]
            cols = slice(h * head_dim, (h + 1) * head_dim)
            out_ref[r, :, cols] = tile
            for g in range(devices):
                send_ref[g, r * steps : (r + 1) * steps, cols] = tile


def project_kernel(core_ref, *refs):
    token_refs, weight_ref, away_ref, own_ref = refs[:-3], *refs[-3:]
    chips, tokens_out, columns = own_ref.shape
    groups = token_refs[0].shape[2]
    step = 256
    for side, out_ref in ((1 - core_ref[0], away_ref), (core_ref[0], own_ref)):
        for c in range(columns // step):
            cols = slice(c * step, (c + 1) * step)
            at = 0
            for token_ref in token_refs:
                steps, features = token_ref.shape[3:]
                tokens = jnp.concatenate([token_ref[y, side] for y in range(chips)], axis=0)
                part = jnp.dot(
                    tokens.reshape(-1, features), weight_ref[:, cols], preferred_element_type=F32
                )
                part = part.astype(out_ref.dtype).reshape(chips, groups, steps, step)
                for g in range(groups):
                    row = g * (tokens_out // groups) + at
                    out_ref[:, row : row + steps, cols] = part[:, g]
                at += steps


def on_device(
    queries,
    new_keys,
    incoming_values,
    family,
    prefix_table,
    prefix_key_pool,
    prefix_value_pool,
    suffix_len,
    suffix_holder,
    suffix_slot,
    suffix_key_pools,
    suffix_value_pools,
    out_weight,
):
    devices = lax.axis_size("grp")
    heads = lax.axis_size("kv")
    row_dev, local_heads, steps, head_dim = queries.shape
    width = local_heads * steps
    features = local_heads * head_dim
    fams, pages_dev = prefix_table.shape
    page_len = prefix_key_pool.shape[2]
    prefix_dev = pages_dev * page_len
    own_pages = suffix_key_pools.shape[1]
    cap = own_pages // devices
    suffix = cap * page_len
    columns = out_weight.shape[1]
    core = lax.axis_index("kv") % 2
    chip = lax.axis_index("kv") // 2
    chips = heads // 2
    flat_query = queries.reshape(row_dev * width, head_dim)
    base = (lax.axis_index("grp") * cap).astype(I32).reshape(1)

    def pack():
        return pl.pallas_call(
            functools.partial(pack_kernel, cap=cap, page_len=page_len),
            out_shape=jax.ShapeDtypeStruct((devices, row_dev * width + 16, head_dim), BF16),
            in_specs=[smem_spec()] * 5 + [vmem_spec()],
            out_specs=vmem_spec(),
            compiler_params=params(8),
            name="pack",
        )(
            base,
            in_hbm(family),
            in_hbm(suffix_len),
            in_hbm(suffix_holder),
            in_hbm(suffix_slot),
            in_hbm(flat_query),
        )

    def arrange(turn, before=()):
        shapes = [
            (fams, prefix_dev, head_dim),
            (fams, head_dim, prefix_dev),
            (devices, head_dim, suffix),
        ]
        return pl.pallas_call(
            functools.partial(arrange_kernel, turn=turn),
            out_shape=[pltpu.HBM(shape, BF16) for shape in shapes],
            in_specs=[smem_spec()] * 2 + [any_spec()] * (3 + len(before)),
            out_specs=[any_spec()] * 3,
            input_output_aliases={5 + i: i for i in range(len(before))},
            scratch_shapes=[
                pltpu.VMEM(prefix_key_pool.shape[1:], BF16),
                pltpu.VMEM(prefix_value_pool.shape[1:], BF16),
                pltpu.VMEM((devices, suffix, head_dim), BF16),
            ]
            + [pltpu.VMEM(shape, BF16) for shape in shapes]
            + [
                pltpu.SemaphoreType.DMA((3,)),
                pltpu.SemaphoreType.DMA((2 * fams + 1,)),
            ],
            compiler_params=params(24),
            name=f"arrange_{turn}",
            cost_estimate=pl.CostEstimate(flops=0, bytes_accessed=20 * MIB, transcendentals=0),
        )(
            core.astype(I32).reshape(1),
            in_hbm(prefix_table),
            in_hbm(prefix_key_pool[0]),
            in_hbm(prefix_value_pool[0]),
            in_hbm(suffix_value_pools.reshape(devices, suffix, head_dim)),
            *[in_hbm(x) for x in before],
        )

    def attend(first, n, meta, recv, pages):
        span = GROUP * width
        rows = devices * n
        keys, values, suffix_values = pages
        kernel = functools.partial(
            attend_kernel,
            first_row=first,
            rows_here=n,
            rows_dev=row_dev,
            cap=cap,
            page_len=page_len,
            width=width,
        )
        scratch = [
            pltpu.VMEM(keys.shape, BF16),
            pltpu.VMEM(values.shape, BF16),
            pltpu.VMEM((devices, suffix, head_dim), BF16),
            pltpu.VMEM(suffix_values.shape, BF16),
            pltpu.VMEM((KEY_BLOCK, span), F32),
            pltpu.VMEM((KEY_BLOCK, span), F32),
            pltpu.VMEM((8, span), F32),
            pltpu.VMEM((8, span), F32),
            pltpu.VMEM((suffix, span), F32),
            pltpu.VMEM((8, span), F32),
            pltpu.VMEM((devices, 16, width), F32),
            pltpu.SMEM((rows // GROUP + fams + 1, 3), I32),
            pltpu.SMEM((2, fams), I32),
            pltpu.SemaphoreType.DMA((2,)),
            pltpu.SemaphoreType.DMA((fams,)),
            pltpu.SemaphoreType.DMA((fams,)),
        ]
        return pl.pallas_call(
            kernel,
            out_shape=jax.ShapeDtypeStruct((devices, n * head_dim + 16, width), BF16),
            in_specs=[smem_spec(), vmem_spec()] + [any_spec()] * 4,
            out_specs=vmem_spec(),
            scratch_shapes=scratch,
            compiler_params=params(40),
            name=f"attend_{first}",
            cost_estimate=pl.CostEstimate(
                flops=8 * rows * width * prefix_dev * head_dim,
                bytes_accessed=14 * MIB,
                transcendentals=rows * width * prefix_dev,
            ),
        )(
            meta,
            recv,
            in_hbm(keys),
            in_hbm(values),
            in_hbm(suffix_key_pools.reshape(devices, suffix, head_dim)),
            in_hbm(suffix_values),
        )

    def merge(returned):
        return pl.pallas_call(
            merge_kernel,
            out_shape=[
                jax.ShapeDtypeStruct((row_dev, steps, features), BF16),
                jax.ShapeDtypeStruct((devices, row_dev * steps, features), BF16),
            ],
            in_specs=[vmem_spec()] * 4,
            out_specs=[vmem_spec()] * 2,
            compiler_params=params(12),
            name="merge",
        )(returned, flat_query, new_keys[:, 0], incoming_values[:, 0])


    def project(tokens):
        block = sum(t.shape[2] * t.shape[3] for t in tokens)
        return pl.pallas_call(
            project_kernel,
            out_shape=[
                jax.ShapeDtypeStruct((chips, block, columns), BF16),
                jax.ShapeDtypeStruct((chips, block, columns), F32),
            ],
            in_specs=[smem_spec()] + [vmem_spec()] * (len(tokens) + 1),
            out_specs=[vmem_spec()] * 2,
            compiler_params=params(16),
            name="project",
        )(core.astype(I32).reshape(1), *tokens, out_weight)

    def chip_perm(shift):
        return [(y * 2 + c, (y + shift) % chips * 2 + c) for y in range(chips) for c in range(2)]

    def project_and_sum(tokens):
        away, own = project(
            [t.reshape(chips, 2, devices // heads, -1, features) for t in tokens]
        )
        partner = [(y * 2 + c, y * 2 + 1 - c) for y in range(chips) for c in range(2)]
        arrived = lax.ppermute(away, "kv", partner)
        both = own + arrived.astype(F32)
        total = lax.dynamic_index_in_dim(both, chip, 0, keepdims=False)
        for shift in range(1, chips):
            part = lax.dynamic_index_in_dim(both, (chip + shift) % chips, 0, keepdims=False)
            part = lax.ppermute(part.astype(BF16), "kv", chip_perm(shift))
            total = total + part.astype(F32)
        return total.astype(BF16)

    def exchange(x):
        return lax.all_to_all(x, "grp", 0, 0, tiled=True)

    packed, *pages = lax.optimization_barrier((pack(), *arrange(0)))
    recv = exchange(packed)
    pages = arrange(1, pages)
    meta = recv[:, row_dev * width, :].astype(I32)
    attended, spread = merge(exchange(attend(0, row_dev, meta, recv, pages)))
    mixed = project_and_sum([exchange(spread)])
    return (attended, mixed)


def solution(mesh):
    in_specs = (
        P("grp", "kv", None, None),
        P("grp", "kv", None, None),
        P("grp", "kv", None, None),
        P("grp"),
        P(None, "grp"),
        P("kv", "grp", None, None),
        P("kv", "grp", None, None),
        P("grp"),
        P("grp", None),
        P("grp", None),
        P("kv", "grp", None, None),
        P("kv", "grp", None, None),
        P("kv", "grp"),
    )
    out_specs = (P("grp", None, "kv"), P("kv", "grp"))
    return jax.shard_map(
        on_device, mesh=mesh, in_specs=in_specs, out_specs=out_specs, check_vma=False
    )
```

```python
import functools
import math

import jax
import jax.numpy as jnp
from jax import lax
from jax.experimental import pallas as pl
from jax.experimental.pallas import tpu as pltpu
from jax.sharding import PartitionSpec as P

F32 = jnp.float32
BF16 = jnp.bfloat16
I32 = jnp.int32
NT = (((1,), (1,)), ((), ()))
TN = (((0,), (0,)), ((), ()))
LOG2E = math.log2(math.e)
NEG = -1e30
MIB = 1024 * 1024
GROUP = 2
KEY_BLOCK = 1024
KEY_SUB = 512
UNIT = 4


def vmem_spec():
    return pl.BlockSpec(memory_space=pltpu.VMEM)


def smem_spec():
    return pl.BlockSpec(memory_space=pltpu.SMEM)


def any_spec():
    return pl.BlockSpec(memory_space=pl.ANY)


def in_hbm(x):
    return pltpu.with_memory_space_constraint(x, pltpu.HBM)


def params(mib):
    return pltpu.CompilerParams(vmem_limit_bytes=mib * MIB)


def list_pages(base, family_ref, length_ref, holder_ref, slot_ref, devices, cap, page_len):
    rows, pages = holder_ref.shape
    lanes = 128
    holder_of = lax.broadcasted_iota(I32, (devices, lanes), 0)
    lane = lax.broadcasted_iota(I32, (devices, lanes), 1)
    listed = jnp.full((devices, lanes), -1, I32)
    for r in range(rows):
        listed = jnp.where(lane == rows * cap + r, family_ref[r], listed)
        length = length_ref[r]

        def add_page(c, carry):
            listed, count = carry
            live = jnp.clip(length - c * page_len, 0, page_len)
            holder = jnp.where(live > 0, holder_ref[r, c], -1)
            entry = (slot_ref[r, c] - base) * page_len + live - 1
            here = holder_of == holder
            listed = jnp.where(here & (lane == count), entry, listed)
            return listed, count + here.astype(I32)

        start = jnp.full((devices, lanes), r * cap, I32)
        listed, _ = lax.fori_loop(0, pages, add_page, (listed, start), unroll=8)
    return listed


def arrange_pages(
    table_ref, loads, key_ref, value_ref, key_done, value_done, key_out, value_out, sems
):
    pages, page_len, head_dim = key_ref.shape
    fams = key_done.shape[0]
    per_fam = pages // fams
    span = 256
    block = span // page_len
    row = lax.broadcasted_iota(I32, (head_dim, head_dim), 0)
    column = lax.broadcasted_iota(I32, (head_dim, head_dim), 1)
    identity = (row == column).astype(F32).astype(BF16)
    stores = []
    loads[0].wait()
    for f in range(fams):

        def turn_block(b, carry):
            listed = [table_ref[f, b * block + i] for i in range(block)]
            values = jnp.concatenate([value_ref[page] for page in listed], axis=0)
            turned = lax.dot_general(identity, values, NT, preferred_element_type=F32)
            value_done[f, :, pl.ds(pl.multiple_of(b * span, span), span)] = turned.astype(BF16)
            return carry

        lax.fori_loop(0, per_fam // block, turn_block, 0, unroll=4)
        stores.append(pltpu.make_async_copy(value_done.at[f], value_out.at[f], sems.at[f]))
        stores[-1].start()
    loads[1].wait()
    for f in range(fams):

        def move_block(b, carry):
            for i in range(block):
                at = pl.multiple_of(b * span + i * page_len, page_len)
                key_done[f, pl.ds(at, page_len), :] = key_ref[table_ref[f, b * block + i]]
            return carry

        lax.fori_loop(0, per_fam // block, move_block, 0, unroll=2)
        stores.append(pltpu.make_async_copy(key_done.at[f], key_out.at[f], sems.at[fams + f]))
        stores[-1].start()
    for store in stores:
        store.wait()


def prepare_kernel(
    place_ref,
    table_hbm,
    key_hbm,
    value_hbm,
    family_hbm,
    length_hbm,
    holder_hbm,
    slot_hbm,
    query_hbm,
    packed_out,
    key_out,
    value_out,
    table_ref,
    key_ref,
    value_ref,
    key_done,
    value_done,
    family_ref,
    length_ref,
    holder_ref,
    slot_ref,
    query_ref,
    tile_ref,
    small_sems,
    sent_sems,
    in_sems,
    out_sems,
    *,
    cap,
    page_len,
):
    devices, _, lanes = packed_out.shape
    body = query_ref.shape[0]
    first = place_ref[0] == 0
    small = [
        pltpu.make_async_copy(src, dst, small_sems.at[i])
        for i, (src, dst) in enumerate(
            (
                (family_hbm, family_ref),
                (length_hbm, length_ref),
                (holder_hbm, holder_ref),
                (slot_hbm, slot_ref),
                (query_hbm, query_ref),
                (table_hbm, table_ref),
            )
        )
    ]
    for load in small:
        load.start()
    loads = [
        pltpu.make_async_copy(value_hbm, value_ref, in_sems.at[0]),
        pltpu.make_async_copy(key_hbm, key_ref, in_sems.at[1]),
    ]

    @pl.when(first)
    def _():
        for load in loads:
            load.start()

    sent = [
        pltpu.make_async_copy(
            query_ref, packed_out.at[g, pl.ds(0, body), :], sent_sems.at[g]
        )
        for g in range(devices)
    ]
    small[4].wait()
    for copy in sent:
        copy.start()
    for i in (0, 1, 2, 3, 5):
        small[i].wait()
    listed = list_pages(
        place_ref[1], family_ref, length_ref, holder_ref, slot_ref, devices, cap, page_len
    ).astype(F32)
    tile_row = lax.broadcasted_iota(I32, (16, lanes), 0)
    for g in range(devices):
        tile = jnp.where(tile_row == 0, jnp.broadcast_to(listed[g : g + 1, :], (16, lanes)), 0.0)
        tile_ref[g] = tile.astype(BF16)
    tiles = pltpu.make_async_copy(
        tile_ref, packed_out.at[:, pl.ds(body, 16), :], sent_sems.at[devices]
    )
    tiles.start()

    @pl.when(first)
    def _():
        arrange_pages(
            table_ref,
            loads,
            key_ref,
            value_ref,
            key_done,
            value_done,
            key_out,
            value_out,
            out_sems,
        )

    for copy in sent:
        copy.wait()
    tiles.wait()


def arrange_kernel(
    place_ref,
    table_ref,
    key_hbm,
    value_hbm,
    key_before,
    value_before,
    key_out,
    value_out,
    key_ref,
    value_ref,
    key_done,
    value_done,
    in_sems,
    out_sems,
):
    @pl.when(place_ref[0] == 1)
    def _():
        loads = [
            pltpu.make_async_copy(value_hbm, value_ref, in_sems.at[0]),
            pltpu.make_async_copy(key_hbm, key_ref, in_sems.at[1]),
        ]
        for load in loads:
            load.start()
        arrange_pages(
            table_ref,
            loads,
            key_ref,
            value_ref,
            key_done,
            value_done,
            key_out,
            value_out,
            out_sems,
        )


def attend_kernel(
    meta_ref,
    recv_ref,
    key_hbm,
    value_hbm,
    suffix_key_hbm,
    suffix_value_hbm,
    out_ref,
    key_ref,
    value_ref,
    suffix_key_ref,
    suffix_value_ref,
    score_a,
    score_b,
    top_a,
    top_b,
    score_s,
    top_s,
    lse_ref,
    pair_ref,
    count_ref,
    many_ref,
    sems,
    key_sems,
    value_sems,
    *,
    rows_dev,
    cap,
    page_len,
    width,
):
    devices = out_ref.shape[0]
    rows = devices * rows_dev
    fams, prefix, head_dim = key_ref.shape
    scale = LOG2E / math.sqrt(head_dim)
    blocks = prefix // KEY_BLOCK
    subs = KEY_BLOCK // KEY_SUB
    buffers = ((score_a, top_a), (score_b, top_b))

    def key_load(f):
        return pltpu.make_async_copy(key_hbm.at[f], key_ref.at[f], key_sems.at[f])

    def value_load(f):
        return pltpu.make_async_copy(value_hbm.at[f], value_ref.at[f], value_sems.at[f])

    suffix_loads = [
        pltpu.make_async_copy(suffix_key_hbm, suffix_key_ref, sems.at[0]),
        pltpu.make_async_copy(suffix_value_hbm, suffix_value_ref, sems.at[1]),
    ]
    key_load(0).start()
    suffix_loads[0].start()
    value_load(0).start()
    suffix_loads[1].start()
    for f in range(1, fams):
        key_load(f).start()
        value_load(f).start()

    def row_family(r):
        return meta_ref[r // rows_dev, rows_dev * cap + r % rows_dev]

    for f in range(fams):
        count_ref[0, f] = 0

    def count_row(r, n):
        fam = row_family(r)
        count_ref[0, fam] = count_ref[0, fam] + 1
        many_ref[n] = r
        return n + (meta_ref[r // rows_dev, (r % rows_dev) * cap + UNIT] >= 0).astype(I32)

    many = lax.fori_loop(0, rows, count_row, 0, unroll=4)
    groups = 0
    for f in range(fams):
        count_ref[1, f] = 2 * groups
        groups = groups + (count_ref[0, f] + 1) // 2

    def place_row(r, carry):
        fam = row_family(r)
        at = count_ref[1, fam]
        count_ref[1, fam] = at + 1
        pair_ref[at // 2, 0] = fam
        pair_ref[at // 2, 1 + at % 2] = r

        @pl.when(at % 2 == 0)
        def _():
            pair_ref[at // 2, 2] = r

        return carry

    lax.fori_loop(0, rows, place_row, 0, unroll=4)
    count_ref[0, 0] = 0

    def families_to(fam):
        def one(f, carry):
            key_load(f).wait()
            value_load(f).wait()
            return carry

        lax.fori_loop(count_ref[0, 0], fam + 1, one, 0)
        count_ref[0, 0] = jnp.maximum(count_ref[0, 0], fam + 1)

    tail = rows_dev * head_dim
    lse_ref[...] = jnp.zeros_like(lse_ref)

    def load_queries(g):
        parts = []
        for i in range(GROUP):
            r = pair_ref[g, 1 + i]
            at = pl.multiple_of((r % rows_dev) * width, width)
            parts.append(recv_ref[r // rows_dev, pl.ds(at, width), :])
        return jnp.concatenate(parts, axis=0)

    def fold_max(scores):
        return jnp.max(scores.reshape(scores.shape[0] // 8, 8, scores.shape[1]), axis=0)

    def fold_sum(values):
        return jnp.sum(values.reshape(values.shape[0] // 8, 8, values.shape[1]), axis=0)

    def score_sub(query, fam, block, sub, into):
        at = block * KEY_BLOCK + sub * KEY_SUB
        scores = lax.dot_general(
            key_ref[fam, at : at + KEY_SUB, :], query, NT, preferred_element_type=F32
        )
        into[0][sub * KEY_SUB : (sub + 1) * KEY_SUB, :] = scores
        return fold_max(scores)

    token = lax.broadcasted_iota(I32, (page_len, width), 0)

    def listed_pages(r, unit):
        owner = r // rows_dev
        found = []
        for p in range(UNIT):
            entry = meta_ref[owner, (r % rows_dev) * cap + unit * UNIT + p]
            live = jnp.where(entry >= 0, entry % page_len + 1, 0)
            found.append((owner * cap + jnp.maximum(entry, 0) // page_len, live))
        return found

    def pair_pages(g):
        found = []
        for i in range(GROUP):
            found += listed_pages(pair_ref[g, 1 + i], 0)
        return found

    def suffix_scores(query, pages):
        keys = jnp.concatenate([suffix_key_ref[page] for page, _ in pages], axis=0)
        return lax.dot_general(keys, query, NT, preferred_element_type=F32)

    def suffix_part(weight, pages):
        values = jnp.concatenate([suffix_value_ref[page] for page, _ in pages], axis=0)
        return lax.dot_general(values, weight.astype(BF16), TN, preferred_element_type=F32)

    def score_suffix(query, pages):
        scores = suffix_scores(query, pages)
        dead = jnp.full((page_len, width), NEG, F32)
        tops = []
        for i in range(GROUP):
            cols = slice(i * width, (i + 1) * width)
            top = None
            for p, (_, live) in enumerate(pages):
                at = slice(p * page_len, (p + 1) * page_len)
                if p // UNIT != i:
                    score_s[at, cols] = dead
                    continue
                part = jnp.where(token < live, scores[at, cols], NEG)
                score_s[at, cols] = part
                sub_top = fold_max(part)
                top = sub_top if top is None else jnp.maximum(top, sub_top)
            tops.append(top)
        top_s[...] = jnp.concatenate(tops, axis=1)

    first_query = load_queries(0)
    first_fam = pair_ref[0, 0]
    families_to(first_fam)
    suffix_loads[0].wait()
    top = None
    for s in range(subs):
        sub_top = score_sub(first_query, first_fam, 0, s, buffers[0])
        top = sub_top if top is None else jnp.maximum(top, sub_top)
    top_a[...] = top
    score_suffix(first_query, pair_pages(0))
    suffix_loads[1].wait()

    def attend_group(g, carry):
        fam = pair_ref[g, 0]
        after = jnp.minimum(g + 1, groups - 1)
        next_fam = pair_ref[after, 0]
        families_to(next_fam)
        query = load_queries(g)
        next_query = load_queries(after)
        peak = total = acc = None
        for b in range(blocks):
            now, later = buffers[b % 2], buffers[(b + 1) % 2]
            block_top = now[1][...]
            if b == 0:
                block_top = jnp.maximum(block_top, top_s[...])
            block_peak = jnp.max(block_top, axis=0, keepdims=True) * scale
            if peak is None:
                new_peak = block_peak
            else:
                new_peak = jnp.maximum(peak, block_peak)
                factor = jnp.exp2(peak - new_peak)
                total = total * factor
                acc = acc * factor
            peak = new_peak
            if b == 0:
                weight = jnp.exp2(score_s[...] * scale - peak)
                total = fold_sum(weight)
                acc = suffix_part(weight, pair_pages(g))
            if b + 1 == blocks:
                score_suffix(next_query, pair_pages(after))
            top = None
            for s in range(subs):
                if b + 1 < blocks:
                    sub_top = score_sub(query, fam, b + 1, s, later)
                else:
                    sub_top = score_sub(next_query, next_fam, 0, s, later)
                top = sub_top if top is None else jnp.maximum(top, sub_top)
                weight = jnp.exp2(now[0][s * KEY_SUB : (s + 1) * KEY_SUB, :] * scale - peak)
                total = total + fold_sum(weight)
                at = b * KEY_BLOCK + s * KEY_SUB
                acc = acc + jnp.dot(
                    value_ref[fam, :, at : at + KEY_SUB],
                    weight.astype(BF16),
                    preferred_element_type=F32,
                )
            later[1][...] = top
        total = jnp.sum(total, axis=0, keepdims=True)
        lse = peak + jnp.log2(total)
        acc = (acc * (1.0 / total)).astype(BF16)
        for i in range(GROUP):
            cols = slice(i * width, (i + 1) * width)
            put_row(pair_ref[g, 1 + i], acc[:, cols], lse[:, cols])
        return carry

    def row_place(r):
        return pl.ds(pl.multiple_of((r % rows_dev) * head_dim, head_dim), head_dim)

    def put_row(r, acc, lse):
        owner, at = r // rows_dev, r % rows_dev
        high = lse.astype(BF16).astype(F32)
        middle = (lse - high).astype(BF16).astype(F32)
        out_ref[owner, row_place(r), :] = acc
        lse_ref[owner, pl.ds(at, 1), :] = high
        lse_ref[owner, pl.ds(rows_dev + at, 1), :] = middle
        lse_ref[owner, pl.ds(2 * rows_dev + at, 1), :] = lse - high - middle

    def more_suffix(r, unit):
        owner, at = r // rows_dev, r % rows_dev
        begin = pl.multiple_of(at * width, width)
        pages = listed_pages(r, unit)
        scores = suffix_scores(recv_ref[owner, pl.ds(begin, width), :], pages)
        scores = jnp.concatenate(
            [
                jnp.where(token < live, scores[p * page_len : (p + 1) * page_len, :], NEG)
                for p, (_, live) in enumerate(pages)
            ],
            axis=0,
        )
        lse = (
            lse_ref[owner, pl.ds(at, 1), :]
            + lse_ref[owner, pl.ds(rows_dev + at, 1), :]
            + lse_ref[owner, pl.ds(2 * rows_dev + at, 1), :]
        )
        peak = jnp.maximum(lse, jnp.max(scores, axis=0, keepdims=True) * scale)
        weight = jnp.exp2(scores * scale - peak)
        factor = jnp.exp2(lse - peak)
        total = factor + jnp.sum(weight, axis=0, keepdims=True)
        acc = out_ref[owner, row_place(r), :].astype(F32) * factor + suffix_part(weight, pages)
        put_row(r, (acc * (1.0 / total)).astype(BF16), peak + jnp.log2(total))

    def finish_row(n, carry):
        r = many_ref[n]
        for unit in range(1, cap // UNIT):

            @pl.when(meta_ref[r // rows_dev, (r % rows_dev) * cap + unit * UNIT] >= 0)
            def _():
                more_suffix(r, unit)

        return carry

    lax.fori_loop(0, groups, attend_group, 0)
    families_to(fams - 1)
    lax.fori_loop(0, many, finish_row, 0)
    out_ref[:, tail:, :] = lse_ref[...].astype(BF16)


def merge_kernel(
    recv_ref,
    query_ref,
    key_ref,
    value_ref,
    out_ref,
    send_ref,
):
    devices, _, head_dim = recv_ref.shape
    rows, steps, _ = out_ref.shape
    width = query_ref.shape[0] // rows
    scale = LOG2E / math.sqrt(head_dim)
    tail = recv_ref[:, rows * head_dim :, :].astype(F32)
    fresh = lax.broadcasted_iota(I32, (steps, width), 0)
    step = lax.broadcasted_iota(I32, (steps, width), 1) % steps
    for r in range(rows):
        scores = lax.dot_general(
            key_ref[r],
            query_ref[r * width : (r + 1) * width, :],
            NT,
            preferred_element_type=F32,
        )
        scores = jnp.where(fresh <= step, scores * scale, NEG)
        new_peak = jnp.max(scores, axis=0, keepdims=True)
        weight = jnp.exp2(scores - new_peak)
        new_total = jnp.sum(weight, axis=0, keepdims=True)
        new_acc = lax.dot_general(
            value_ref[r], weight.astype(BF16), TN, preferred_element_type=F32
        )
        lse = tail[:, r, :] + tail[:, rows + r, :] + tail[:, 2 * rows + r, :]
        peak = jnp.maximum(jnp.max(lse, axis=0, keepdims=True), new_peak)
        share = jnp.exp2(lse - peak)
        new_share = jnp.exp2(new_peak - peak)
        total = jnp.sum(share, axis=0, keepdims=True) + new_share * new_total
        acc = new_acc * new_share
        for g in range(devices):
            part = recv_ref[g, r * head_dim : (r + 1) * head_dim, :].astype(F32)
            acc = acc + part * share[g : g + 1, :]
        turned = (acc * (1.0 / total)).T.astype(BF16)
        for h in range(width // steps):
            tile = turned[h * steps : (h + 1) * steps, :]
            cols = slice(h * head_dim, (h + 1) * head_dim)
            out_ref[r, :, cols] = tile
            for g in range(devices):
                send_ref[g, r * steps : (r + 1) * steps, cols] = tile


def project_kernel(core_ref, *refs):
    token_refs, weight_ref, away_ref, own_ref = refs[:-3], *refs[-3:]
    chips, tokens_out, columns = own_ref.shape
    groups = token_refs[0].shape[2]
    step = 256
    for side, out_ref in ((1 - core_ref[0], away_ref), (core_ref[0], own_ref)):
        for c in range(columns // step):
            cols = slice(c * step, (c + 1) * step)
            at = 0
            for token_ref in token_refs:
                steps, features = token_ref.shape[3:]
                tokens = jnp.concatenate([token_ref[y, side] for y in range(chips)], axis=0)
                part = jnp.dot(
                    tokens.reshape(-1, features), weight_ref[:, cols], preferred_element_type=F32
                )
                part = part.astype(out_ref.dtype).reshape(chips, groups, steps, step)
                for g in range(groups):
                    row = g * (tokens_out // groups) + at
                    out_ref[:, row : row + steps, cols] = part[:, g]
                at += steps


def on_device(
    queries,
    new_keys,
    incoming_values,
    family,
    prefix_table,
    prefix_key_pool,
    prefix_value_pool,
    suffix_len,
    suffix_holder,
    suffix_slot,
    suffix_key_pools,
    suffix_value_pools,
    out_weight,
):
    devices = lax.axis_size("grp")
    heads = lax.axis_size("kv")
    row_dev, local_heads, steps, head_dim = queries.shape
    width = local_heads * steps
    features = local_heads * head_dim
    fams, pages_dev = prefix_table.shape
    page_len = prefix_key_pool.shape[2]
    prefix_dev = pages_dev * page_len
    own_pages = suffix_key_pools.shape[1]
    cap = own_pages // devices
    columns = out_weight.shape[1]
    core = lax.axis_index("kv") % 2
    chip = lax.axis_index("kv") // 2
    chips = heads // 2
    flat_query = queries.reshape(row_dev * width, head_dim)

    place = jnp.stack([core, lax.axis_index("grp") * cap]).astype(I32)
    key_shape = (fams, prefix_dev, head_dim)
    value_shape = (fams, head_dim, prefix_dev)
    page_scratch = [
        pltpu.VMEM(prefix_key_pool.shape[1:], BF16),
        pltpu.VMEM(prefix_value_pool.shape[1:], BF16),
        pltpu.VMEM(key_shape, BF16),
        pltpu.VMEM(value_shape, BF16),
    ]
    page_operands = [
        in_hbm(prefix_table),
        in_hbm(prefix_key_pool[0]),
        in_hbm(prefix_value_pool[0]),
    ]

    def prepare():
        return pl.pallas_call(
            functools.partial(prepare_kernel, cap=cap, page_len=page_len),
            out_shape=[
                pltpu.HBM((devices, row_dev * width + 16, head_dim), BF16),
                pltpu.HBM(key_shape, BF16),
                pltpu.HBM(value_shape, BF16),
            ],
            in_specs=[smem_spec()] + [any_spec()] * 8,
            out_specs=[any_spec()] * 3,
            scratch_shapes=[pltpu.SMEM(prefix_table.shape, I32)]
            + page_scratch
            + [
                pltpu.SMEM(family.shape, I32),
                pltpu.SMEM(suffix_len.shape, I32),
                pltpu.SMEM(suffix_holder.shape, I32),
                pltpu.SMEM(suffix_slot.shape, I32),
                pltpu.VMEM(flat_query.shape, BF16),
                pltpu.VMEM((devices, 16, head_dim), BF16),
                pltpu.SemaphoreType.DMA((6,)),
                pltpu.SemaphoreType.DMA((devices + 1,)),
                pltpu.SemaphoreType.DMA((2,)),
                pltpu.SemaphoreType.DMA((2 * fams,)),
            ],
            compiler_params=params(24),
            name="prepare",
        )(
            place,
            *page_operands,
            in_hbm(family),
            in_hbm(suffix_len),
            in_hbm(suffix_holder),
            in_hbm(suffix_slot),
            in_hbm(flat_query),
        )

    def arrange(before):
        return pl.pallas_call(
            arrange_kernel,
            out_shape=[pltpu.HBM(key_shape, BF16), pltpu.HBM(value_shape, BF16)],
            in_specs=[smem_spec()] * 2 + [any_spec()] * 4,
            out_specs=[any_spec()] * 2,
            input_output_aliases={4: 0, 5: 1},
            scratch_shapes=page_scratch
            + [
                pltpu.SemaphoreType.DMA((2,)),
                pltpu.SemaphoreType.DMA((2 * fams,)),
            ],
            compiler_params=params(24),
            name="arrange",
            cost_estimate=pl.CostEstimate(flops=0, bytes_accessed=20 * MIB, transcendentals=0),
        )(place, *page_operands, *[in_hbm(x) for x in before])

    def attend(meta, recv, pages):
        span = GROUP * width
        rows = devices * row_dev
        keys, values = pages
        kernel = functools.partial(
            attend_kernel,
            rows_dev=row_dev,
            cap=cap,
            page_len=page_len,
            width=width,
        )
        scratch = [
            pltpu.VMEM(keys.shape, BF16),
            pltpu.VMEM(values.shape, BF16),
            pltpu.VMEM(suffix_key_pools.shape[1:], BF16),
            pltpu.VMEM(suffix_value_pools.shape[1:], BF16),
            pltpu.VMEM((KEY_BLOCK, span), F32),
            pltpu.VMEM((KEY_BLOCK, span), F32),
            pltpu.VMEM((8, span), F32),
            pltpu.VMEM((8, span), F32),
            pltpu.VMEM((GROUP * UNIT * page_len, span), F32),
            pltpu.VMEM((8, span), F32),
            pltpu.VMEM((devices, 16, width), F32),
            pltpu.SMEM((rows // GROUP + fams + 1, 3), I32),
            pltpu.SMEM((2, fams), I32),
            pltpu.SMEM((rows + 1,), I32),
            pltpu.SemaphoreType.DMA((2,)),
            pltpu.SemaphoreType.DMA((fams,)),
            pltpu.SemaphoreType.DMA((fams,)),
        ]
        return pl.pallas_call(
            kernel,
            out_shape=jax.ShapeDtypeStruct((devices, row_dev * head_dim + 16, width), BF16),
            in_specs=[smem_spec(), vmem_spec()] + [any_spec()] * 4,
            out_specs=vmem_spec(),
            scratch_shapes=scratch,
            compiler_params=params(40),
            name="attend",
            cost_estimate=pl.CostEstimate(
                flops=8 * rows * width * prefix_dev * head_dim,
                bytes_accessed=14 * MIB,
                transcendentals=rows * width * prefix_dev,
            ),
        )(
            meta,
            recv,
            in_hbm(keys),
            in_hbm(values),
            in_hbm(suffix_key_pools[0]),
            in_hbm(suffix_value_pools[0]),
        )

    def merge(returned):
        return pl.pallas_call(
            merge_kernel,
            out_shape=[
                jax.ShapeDtypeStruct((row_dev, steps, features), BF16),
                jax.ShapeDtypeStruct((devices, row_dev * steps, features), BF16),
            ],
            in_specs=[vmem_spec()] * 4,
            out_specs=[vmem_spec()] * 2,
            compiler_params=params(12),
            name="merge",
        )(returned, flat_query, new_keys[:, 0], incoming_values[:, 0])


    def project(tokens):
        block = sum(t.shape[2] * t.shape[3] for t in tokens)
        return pl.pallas_call(
            project_kernel,
            out_shape=[
                jax.ShapeDtypeStruct((chips, block, columns), BF16),
                jax.ShapeDtypeStruct((chips, block, columns), F32),
            ],
            in_specs=[smem_spec()] + [vmem_spec()] * (len(tokens) + 1),
            out_specs=[vmem_spec()] * 2,
            compiler_params=params(16),
            name="project",
        )(core.astype(I32).reshape(1), *tokens, out_weight)

    def chip_perm(shift):
        return [(y * 2 + c, (y + shift) % chips * 2 + c) for y in range(chips) for c in range(2)]

    def project_and_sum(tokens):
        away, own = project(
            [t.reshape(chips, 2, devices // heads, -1, features) for t in tokens]
        )
        partner = [(y * 2 + c, y * 2 + 1 - c) for y in range(chips) for c in range(2)]
        arrived = lax.ppermute(away, "kv", partner)
        both = own + arrived.astype(F32)
        total = lax.dynamic_index_in_dim(both, chip, 0, keepdims=False)
        for shift in range(1, chips):
            part = lax.dynamic_index_in_dim(both, (chip + shift) % chips, 0, keepdims=False)
            part = lax.ppermute(part.astype(BF16), "kv", chip_perm(shift))
            total = total + part.astype(F32)
        return total.astype(BF16)

    def exchange(x):
        return lax.all_to_all(x, "grp", 0, 0, tiled=True)

    packed, *pages = prepare()
    recv = exchange(packed)
    pages = arrange(pages)
    meta = recv[:, row_dev * width, :].astype(I32)
    attended, spread = merge(exchange(attend(meta, recv, pages)))
    mixed = project_and_sum([exchange(spread)])
    return (attended, mixed)


def solution(mesh):
    in_specs = (
        P("grp", "kv", None, None),
        P("grp", "kv", None, None),
        P("grp", "kv", None, None),
        P("grp"),
        P(None, "grp"),
        P("kv", "grp", None, None),
        P("kv", "grp", None, None),
        P("grp"),
        P("grp", None),
        P("grp", None),
        P("kv", "grp", None, None),
        P("kv", "grp", None, None),
        P("kv", "grp"),
    )
    out_specs = (P("grp", None, "kv"), P("kv", "grp"))
    return jax.shard_map(
        on_device, mesh=mesh, in_specs=in_specs, out_specs=out_specs, check_vma=False
    )
```

```python
import functools
import math

import jax
import jax.numpy as jnp
from jax import lax
from jax.experimental import pallas as pl
from jax.experimental.pallas import tpu as pltpu
from jax.sharding import PartitionSpec as P

F32 = jnp.float32
BF16 = jnp.bfloat16
I32 = jnp.int32
NT = (((1,), (1,)), ((), ()))
TN = (((0,), (0,)), ((), ()))
LOG2E = math.log2(math.e)
NEG = -1e30
MIB = 1024 * 1024
GROUP = 2
KEY_BLOCK = 1024
KEY_SUB = 512
UNIT = 4


def vmem_spec():
    return pl.BlockSpec(memory_space=pltpu.VMEM)


def smem_spec():
    return pl.BlockSpec(memory_space=pltpu.SMEM)


def any_spec():
    return pl.BlockSpec(memory_space=pl.ANY)


def in_hbm(x):
    return pltpu.with_memory_space_constraint(x, pltpu.HBM)


def params(mib):
    return pltpu.CompilerParams(vmem_limit_bytes=mib * MIB)


def list_pages(base, family_ref, length_ref, holder_ref, slot_ref, devices, cap, page_len):
    rows, pages = holder_ref.shape
    lanes = 128
    holder_of = lax.broadcasted_iota(I32, (devices, lanes), 0)
    lane = lax.broadcasted_iota(I32, (devices, lanes), 1)
    listed = jnp.full((devices, lanes), -1, I32)
    for r in range(rows):
        listed = jnp.where(lane == rows * cap + r, family_ref[r], listed)
        length = length_ref[r]

        def add_page(c, carry):
            listed, count = carry
            live = jnp.clip(length - c * page_len, 0, page_len)
            holder = jnp.where(live > 0, holder_ref[r, c], -1)
            entry = (slot_ref[r, c] - base) * page_len + live - 1
            here = holder_of == holder
            listed = jnp.where(here & (lane == count), entry, listed)
            return listed, count + here.astype(I32)

        start = jnp.full((devices, lanes), r * cap, I32)
        listed, _ = lax.fori_loop(0, pages, add_page, (listed, start), unroll=8)
    return listed


def arrange_pages(
    table_ref, loads, key_ref, value_ref, key_done, value_done, key_out, value_out, sems
):
    pages, page_len, head_dim = key_ref.shape
    fams = key_done.shape[0]
    per_fam = pages // fams
    span = 256
    block = span // page_len
    row = lax.broadcasted_iota(I32, (head_dim, head_dim), 0)
    column = lax.broadcasted_iota(I32, (head_dim, head_dim), 1)
    identity = (row == column).astype(F32).astype(BF16)
    stores = []
    loads[0].wait()
    for f in range(fams):

        def turn_block(b, carry):
            listed = [table_ref[f, b * block + i] for i in range(block)]
            values = jnp.concatenate([value_ref[page] for page in listed], axis=0)
            turned = lax.dot_general(identity, values, NT, preferred_element_type=F32)
            value_done[f, :, pl.ds(pl.multiple_of(b * span, span), span)] = turned.astype(BF16)
            return carry

        lax.fori_loop(0, per_fam // block, turn_block, 0, unroll=4)
        stores.append(pltpu.make_async_copy(value_done.at[f], value_out.at[f], sems.at[f]))
        stores[-1].start()
    loads[1].wait()
    for f in range(fams):

        def move_block(b, carry):
            for i in range(block):
                at = pl.multiple_of(b * span + i * page_len, page_len)
                key_done[f, pl.ds(at, page_len), :] = key_ref[table_ref[f, b * block + i]]
            return carry

        lax.fori_loop(0, per_fam // block, move_block, 0, unroll=2)
        stores.append(pltpu.make_async_copy(key_done.at[f], key_out.at[f], sems.at[fams + f]))
        stores[-1].start()
    for store in stores:
        store.wait()


def prepare_kernel(
    place_ref,
    table_hbm,
    key_hbm,
    value_hbm,
    family_hbm,
    length_hbm,
    holder_hbm,
    slot_hbm,
    query_hbm,
    packed_out,
    key_out,
    value_out,
    table_ref,
    key_ref,
    value_ref,
    key_done,
    value_done,
    family_ref,
    length_ref,
    holder_ref,
    slot_ref,
    query_ref,
    tile_ref,
    small_sems,
    sent_sems,
    in_sems,
    out_sems,
    *,
    cap,
    page_len,
):
    devices, _, lanes = packed_out.shape
    body = query_ref.shape[0]
    first = place_ref[0] == 0
    small = [
        pltpu.make_async_copy(src, dst, small_sems.at[i])
        for i, (src, dst) in enumerate(
            (
                (family_hbm, family_ref),
                (length_hbm, length_ref),
                (holder_hbm, holder_ref),
                (slot_hbm, slot_ref),
                (query_hbm, query_ref),
                (table_hbm, table_ref),
            )
        )
    ]
    for load in small:
        load.start()
    loads = [
        pltpu.make_async_copy(value_hbm, value_ref, in_sems.at[0]),
        pltpu.make_async_copy(key_hbm, key_ref, in_sems.at[1]),
    ]

    @pl.when(first)
    def _():
        for load in loads:
            load.start()

    sent = [
        pltpu.make_async_copy(
            query_ref, packed_out.at[g, pl.ds(0, body), :], sent_sems.at[g]
        )
        for g in range(devices)
    ]
    small[4].wait()
    for copy in sent:
        copy.start()
    for i in (0, 1, 2, 3, 5):
        small[i].wait()
    listed = list_pages(
        place_ref[1], family_ref, length_ref, holder_ref, slot_ref, devices, cap, page_len
    ).astype(F32)
    tile_row = lax.broadcasted_iota(I32, (16, lanes), 0)
    for g in range(devices):
        tile = jnp.where(tile_row == 0, jnp.broadcast_to(listed[g : g + 1, :], (16, lanes)), 0.0)
        tile_ref[g] = tile.astype(BF16)
    tiles = pltpu.make_async_copy(
        tile_ref, packed_out.at[:, pl.ds(body, 16), :], sent_sems.at[devices]
    )
    tiles.start()

    @pl.when(first)
    def _():
        arrange_pages(
            table_ref,
            loads,
            key_ref,
            value_ref,
            key_done,
            value_done,
            key_out,
            value_out,
            out_sems,
        )

    for copy in sent:
        copy.wait()
    tiles.wait()


def arrange_kernel(
    place_ref,
    table_ref,
    key_hbm,
    value_hbm,
    key_before,
    value_before,
    key_out,
    value_out,
    key_ref,
    value_ref,
    key_done,
    value_done,
    in_sems,
    out_sems,
):
    @pl.when(place_ref[0] == 1)
    def _():
        loads = [
            pltpu.make_async_copy(value_hbm, value_ref, in_sems.at[0]),
            pltpu.make_async_copy(key_hbm, key_ref, in_sems.at[1]),
        ]
        for load in loads:
            load.start()
        arrange_pages(
            table_ref,
            loads,
            key_ref,
            value_ref,
            key_done,
            value_done,
            key_out,
            value_out,
            out_sems,
        )


def attend_kernel(
    meta_ref,
    recv_ref,
    key_hbm,
    value_hbm,
    suffix_key_hbm,
    suffix_value_hbm,
    out_ref,
    key_ref,
    value_ref,
    suffix_key_ref,
    suffix_value_ref,
    score_a,
    score_b,
    top_a,
    top_b,
    score_s,
    top_s,
    lse_ref,
    pair_ref,
    count_ref,
    many_ref,
    sems,
    key_sems,
    value_sems,
    *,
    rows_dev,
    cap,
    page_len,
    width,
):
    devices = out_ref.shape[0]
    rows = devices * rows_dev
    fams, prefix, head_dim = key_ref.shape
    scale = LOG2E / math.sqrt(head_dim)
    blocks = prefix // KEY_BLOCK
    subs = KEY_BLOCK // KEY_SUB
    buffers = ((score_a, top_a), (score_b, top_b))

    def key_load(f):
        return pltpu.make_async_copy(key_hbm.at[f], key_ref.at[f], key_sems.at[f])

    def value_load(f):
        return pltpu.make_async_copy(value_hbm.at[f], value_ref.at[f], value_sems.at[f])

    suffix_loads = [
        pltpu.make_async_copy(suffix_key_hbm, suffix_key_ref, sems.at[0]),
        pltpu.make_async_copy(suffix_value_hbm, suffix_value_ref, sems.at[1]),
    ]
    key_load(0).start()
    suffix_loads[0].start()
    value_load(0).start()
    suffix_loads[1].start()
    for f in range(1, fams):
        key_load(f).start()
        value_load(f).start()

    def row_family(r):
        return meta_ref[r // rows_dev, rows_dev * cap + r % rows_dev]

    for f in range(fams):
        count_ref[0, f] = 0

    def count_row(r, n):
        fam = row_family(r)
        count_ref[0, fam] = count_ref[0, fam] + 1
        many_ref[n] = r
        return n + (meta_ref[r // rows_dev, (r % rows_dev) * cap + UNIT] >= 0).astype(I32)

    many = lax.fori_loop(0, rows, count_row, 0, unroll=4)
    groups = 0
    for f in range(fams):
        count_ref[1, f] = 2 * groups
        groups = groups + (count_ref[0, f] + 1) // 2

    def place_row(r, carry):
        fam = row_family(r)
        at = count_ref[1, fam]
        count_ref[1, fam] = at + 1
        pair_ref[at // 2, 0] = fam
        pair_ref[at // 2, 1 + at % 2] = r

        @pl.when(at % 2 == 0)
        def _():
            pair_ref[at // 2, 2] = r

        return carry

    lax.fori_loop(0, rows, place_row, 0, unroll=4)
    count_ref[0, 0] = 0

    def families_to(fam):
        def one(f, carry):
            key_load(f).wait()
            value_load(f).wait()
            return carry

        lax.fori_loop(count_ref[0, 0], fam + 1, one, 0)
        count_ref[0, 0] = jnp.maximum(count_ref[0, 0], fam + 1)

    tail = rows_dev * head_dim
    lse_ref[...] = jnp.zeros_like(lse_ref)

    def load_queries(g):
        parts = []
        for i in range(GROUP):
            r = pair_ref[g, 1 + i]
            at = pl.multiple_of((r % rows_dev) * width, width)
            parts.append(recv_ref[r // rows_dev, pl.ds(at, width), :])
        return jnp.concatenate(parts, axis=0)

    def fold_max(scores):
        return jnp.max(scores.reshape(scores.shape[0] // 8, 8, scores.shape[1]), axis=0)

    def fold_sum(values):
        return jnp.sum(values.reshape(values.shape[0] // 8, 8, values.shape[1]), axis=0)

    def score_sub(query, fam, block, sub, into):
        at = block * KEY_BLOCK + sub * KEY_SUB
        scores = lax.dot_general(
            key_ref[fam, at : at + KEY_SUB, :], query, NT, preferred_element_type=F32
        )
        into[0][sub * KEY_SUB : (sub + 1) * KEY_SUB, :] = scores
        return fold_max(scores)

    token = lax.broadcasted_iota(I32, (page_len, width), 0)

    def listed_pages(r, unit):
        owner = r // rows_dev
        found = []
        for p in range(UNIT):
            entry = meta_ref[owner, (r % rows_dev) * cap + unit * UNIT + p]
            live = jnp.where(entry >= 0, entry % page_len + 1, 0)
            found.append((owner * cap + jnp.maximum(entry, 0) // page_len, live))
        return found

    def pair_pages(g):
        found = []
        for i in range(GROUP):
            found += listed_pages(pair_ref[g, 1 + i], 0)
        return found

    def suffix_scores(query, pages):
        keys = jnp.concatenate([suffix_key_ref[page] for page, _ in pages], axis=0)
        return lax.dot_general(keys, query, NT, preferred_element_type=F32)

    def suffix_part(weight, pages):
        values = jnp.concatenate([suffix_value_ref[page] for page, _ in pages], axis=0)
        return lax.dot_general(values, weight.astype(BF16), TN, preferred_element_type=F32)

    def score_suffix(query, pages):
        scores = suffix_scores(query, pages)
        dead = jnp.full((page_len, width), NEG, F32)
        tops = []
        for i in range(GROUP):
            cols = slice(i * width, (i + 1) * width)
            top = None
            for p, (_, live) in enumerate(pages):
                at = slice(p * page_len, (p + 1) * page_len)
                if p // UNIT != i:
                    score_s[at, cols] = dead
                    continue
                part = jnp.where(token < live, scores[at, cols], NEG)
                score_s[at, cols] = part
                sub_top = fold_max(part)
                top = sub_top if top is None else jnp.maximum(top, sub_top)
            tops.append(top)
        top_s[...] = jnp.concatenate(tops, axis=1)

    first_query = load_queries(0)
    first_fam = pair_ref[0, 0]
    families_to(first_fam)
    suffix_loads[0].wait()
    top = None
    for s in range(subs):
        sub_top = score_sub(first_query, first_fam, 0, s, buffers[0])
        top = sub_top if top is None else jnp.maximum(top, sub_top)
    top_a[...] = top
    score_suffix(first_query, pair_pages(0))
    suffix_loads[1].wait()

    def attend_group(g, carry):
        fam = pair_ref[g, 0]
        after = jnp.minimum(g + 1, groups - 1)
        next_fam = pair_ref[after, 0]
        families_to(next_fam)
        query = load_queries(g)
        next_query = load_queries(after)
        peak = total = acc = pending = None

        def value_part(at, weight):
            return jnp.dot(
                value_ref[fam, :, at : at + KEY_SUB], weight, preferred_element_type=F32
            )

        for b in range(blocks):
            now, later = buffers[b % 2], buffers[(b + 1) % 2]
            block_top = now[1][...]
            if b == 0:
                block_top = jnp.maximum(block_top, top_s[...])
            block_peak = jnp.max(block_top, axis=0, keepdims=True) * scale
            if peak is None:
                new_peak = block_peak
            else:
                new_peak = jnp.maximum(peak, block_peak)
                factor = jnp.exp2(peak - new_peak)
                total = total * factor
                acc = (acc + value_part(*pending)) * factor
                pending = None
            peak = new_peak
            if b == 0:
                weight = jnp.exp2(score_s[...] * scale - peak)
                total = fold_sum(weight)
                acc = suffix_part(weight, pair_pages(g))
            if b + 1 == blocks:
                score_suffix(next_query, pair_pages(after))
            top = None
            for s in range(subs):
                if b + 1 < blocks:
                    sub_top = score_sub(query, fam, b + 1, s, later)
                else:
                    sub_top = score_sub(next_query, next_fam, 0, s, later)
                top = sub_top if top is None else jnp.maximum(top, sub_top)
                if pending is not None:
                    acc = acc + value_part(*pending)
                weight = jnp.exp2(now[0][s * KEY_SUB : (s + 1) * KEY_SUB, :] * scale - peak)
                total = total + fold_sum(weight)
                pending = (b * KEY_BLOCK + s * KEY_SUB, weight.astype(BF16))
            later[1][...] = top
        acc = acc + value_part(*pending)
        total = jnp.sum(total, axis=0, keepdims=True)
        lse = peak + jnp.log2(total)
        acc = (acc * (1.0 / total)).astype(BF16)
        for i in range(GROUP):
            cols = slice(i * width, (i + 1) * width)
            put_row(pair_ref[g, 1 + i], acc[:, cols], lse[:, cols])
        return carry

    def row_place(r):
        return pl.ds(pl.multiple_of((r % rows_dev) * head_dim, head_dim), head_dim)

    def put_row(r, acc, lse):
        owner, at = r // rows_dev, r % rows_dev
        high = lse.astype(BF16).astype(F32)
        middle = (lse - high).astype(BF16).astype(F32)
        out_ref[owner, row_place(r), :] = acc
        lse_ref[owner, pl.ds(at, 1), :] = high
        lse_ref[owner, pl.ds(rows_dev + at, 1), :] = middle
        lse_ref[owner, pl.ds(2 * rows_dev + at, 1), :] = lse - high - middle

    def more_suffix(r, unit):
        owner, at = r // rows_dev, r % rows_dev
        begin = pl.multiple_of(at * width, width)
        pages = listed_pages(r, unit)
        scores = suffix_scores(recv_ref[owner, pl.ds(begin, width), :], pages)
        scores = jnp.concatenate(
            [
                jnp.where(token < live, scores[p * page_len : (p + 1) * page_len, :], NEG)
                for p, (_, live) in enumerate(pages)
            ],
            axis=0,
        )
        lse = (
            lse_ref[owner, pl.ds(at, 1), :]
            + lse_ref[owner, pl.ds(rows_dev + at, 1), :]
            + lse_ref[owner, pl.ds(2 * rows_dev + at, 1), :]
        )
        peak = jnp.maximum(lse, jnp.max(scores, axis=0, keepdims=True) * scale)
        weight = jnp.exp2(scores * scale - peak)
        factor = jnp.exp2(lse - peak)
        total = factor + jnp.sum(weight, axis=0, keepdims=True)
        acc = out_ref[owner, row_place(r), :].astype(F32) * factor + suffix_part(weight, pages)
        put_row(r, (acc * (1.0 / total)).astype(BF16), peak + jnp.log2(total))

    def finish_row(n, carry):
        r = many_ref[n]
        for unit in range(1, cap // UNIT):

            @pl.when(meta_ref[r // rows_dev, (r % rows_dev) * cap + unit * UNIT] >= 0)
            def _():
                more_suffix(r, unit)

        return carry

    lax.fori_loop(0, groups, attend_group, 0)
    families_to(fams - 1)
    lax.fori_loop(0, many, finish_row, 0)
    out_ref[:, tail:, :] = lse_ref[...].astype(BF16)


def merge_kernel(
    recv_ref,
    query_ref,
    key_ref,
    value_ref,
    out_ref,
    send_ref,
):
    devices, _, head_dim = recv_ref.shape
    rows, steps, _ = out_ref.shape
    width = query_ref.shape[0] // rows
    scale = LOG2E / math.sqrt(head_dim)
    tail = recv_ref[:, rows * head_dim :, :].astype(F32)
    fresh = lax.broadcasted_iota(I32, (steps, width), 0)
    step = lax.broadcasted_iota(I32, (steps, width), 1) % steps
    for r in range(rows):
        scores = lax.dot_general(
            key_ref[r],
            query_ref[r * width : (r + 1) * width, :],
            NT,
            preferred_element_type=F32,
        )
        scores = jnp.where(fresh <= step, scores * scale, NEG)
        new_peak = jnp.max(scores, axis=0, keepdims=True)
        weight = jnp.exp2(scores - new_peak)
        new_total = jnp.sum(weight, axis=0, keepdims=True)
        new_acc = lax.dot_general(
            value_ref[r], weight.astype(BF16), TN, preferred_element_type=F32
        )
        lse = tail[:, r, :] + tail[:, rows + r, :] + tail[:, 2 * rows + r, :]
        peak = jnp.maximum(jnp.max(lse, axis=0, keepdims=True), new_peak)
        share = jnp.exp2(lse - peak)
        new_share = jnp.exp2(new_peak - peak)
        total = jnp.sum(share, axis=0, keepdims=True) + new_share * new_total
        acc = new_acc * new_share
        for g in range(devices):
            part = recv_ref[g, r * head_dim : (r + 1) * head_dim, :].astype(F32)
            acc = acc + part * share[g : g + 1, :]
        turned = (acc * (1.0 / total)).T.astype(BF16)
        for h in range(width // steps):
            tile = turned[h * steps : (h + 1) * steps, :]
            cols = slice(h * head_dim, (h + 1) * head_dim)
            out_ref[r, :, cols] = tile
            for g in range(devices):
                send_ref[g, r * steps : (r + 1) * steps, cols] = tile


def project_kernel(core_ref, *refs):
    token_refs, weight_ref, away_ref, own_ref = refs[:-3], *refs[-3:]
    chips, tokens_out, columns = own_ref.shape
    groups = token_refs[0].shape[2]
    step = 256
    for side, out_ref in ((1 - core_ref[0], away_ref), (core_ref[0], own_ref)):
        for c in range(columns // step):
            cols = slice(c * step, (c + 1) * step)
            at = 0
            for token_ref in token_refs:
                steps, features = token_ref.shape[3:]
                tokens = jnp.concatenate([token_ref[y, side] for y in range(chips)], axis=0)
                part = jnp.dot(
                    tokens.reshape(-1, features), weight_ref[:, cols], preferred_element_type=F32
                )
                part = part.astype(out_ref.dtype).reshape(chips, groups, steps, step)
                for g in range(groups):
                    row = g * (tokens_out // groups) + at
                    out_ref[:, row : row + steps, cols] = part[:, g]
                at += steps


def on_device(
    queries,
    new_keys,
    incoming_values,
    family,
    prefix_table,
    prefix_key_pool,
    prefix_value_pool,
    suffix_len,
    suffix_holder,
    suffix_slot,
    suffix_key_pools,
    suffix_value_pools,
    out_weight,
):
    devices = lax.axis_size("grp")
    heads = lax.axis_size("kv")
    row_dev, local_heads, steps, head_dim = queries.shape
    width = local_heads * steps
    features = local_heads * head_dim
    fams, pages_dev = prefix_table.shape
    page_len = prefix_key_pool.shape[2]
    prefix_dev = pages_dev * page_len
    own_pages = suffix_key_pools.shape[1]
    cap = own_pages // devices
    columns = out_weight.shape[1]
    core = lax.axis_index("kv") % 2
    chip = lax.axis_index("kv") // 2
    chips = heads // 2
    flat_query = queries.reshape(row_dev * width, head_dim)

    place = jnp.stack([core, lax.axis_index("grp") * cap]).astype(I32)
    key_shape = (fams, prefix_dev, head_dim)
    value_shape = (fams, head_dim, prefix_dev)
    page_scratch = [
        pltpu.VMEM(prefix_key_pool.shape[1:], BF16),
        pltpu.VMEM(prefix_value_pool.shape[1:], BF16),
        pltpu.VMEM(key_shape, BF16),
        pltpu.VMEM(value_shape, BF16),
    ]
    page_operands = [
        in_hbm(prefix_table),
        in_hbm(prefix_key_pool[0]),
        in_hbm(prefix_value_pool[0]),
    ]

    def prepare():
        return pl.pallas_call(
            functools.partial(prepare_kernel, cap=cap, page_len=page_len),
            out_shape=[
                pltpu.HBM((devices, row_dev * width + 16, head_dim), BF16),
                pltpu.HBM(key_shape, BF16),
                pltpu.HBM(value_shape, BF16),
            ],
            in_specs=[smem_spec()] + [any_spec()] * 8,
            out_specs=[any_spec()] * 3,
            scratch_shapes=[pltpu.SMEM(prefix_table.shape, I32)]
            + page_scratch
            + [
                pltpu.SMEM(family.shape, I32),
                pltpu.SMEM(suffix_len.shape, I32),
                pltpu.SMEM(suffix_holder.shape, I32),
                pltpu.SMEM(suffix_slot.shape, I32),
                pltpu.VMEM(flat_query.shape, BF16),
                pltpu.VMEM((devices, 16, head_dim), BF16),
                pltpu.SemaphoreType.DMA((6,)),
                pltpu.SemaphoreType.DMA((devices + 1,)),
                pltpu.SemaphoreType.DMA((2,)),
                pltpu.SemaphoreType.DMA((2 * fams,)),
            ],
            compiler_params=params(24),
            name="prepare",
        )(
            place,
            *page_operands,
            in_hbm(family),
            in_hbm(suffix_len),
            in_hbm(suffix_holder),
            in_hbm(suffix_slot),
            in_hbm(flat_query),
        )

    def arrange(before):
        return pl.pallas_call(
            arrange_kernel,
            out_shape=[pltpu.HBM(key_shape, BF16), pltpu.HBM(value_shape, BF16)],
            in_specs=[smem_spec()] * 2 + [any_spec()] * 4,
            out_specs=[any_spec()] * 2,
            input_output_aliases={4: 0, 5: 1},
            scratch_shapes=page_scratch
            + [
                pltpu.SemaphoreType.DMA((2,)),
                pltpu.SemaphoreType.DMA((2 * fams,)),
            ],
            compiler_params=params(24),
            name="arrange",
            cost_estimate=pl.CostEstimate(flops=0, bytes_accessed=20 * MIB, transcendentals=0),
        )(place, *page_operands, *[in_hbm(x) for x in before])

    def attend(meta, recv, pages):
        span = GROUP * width
        rows = devices * row_dev
        keys, values = pages
        kernel = functools.partial(
            attend_kernel,
            rows_dev=row_dev,
            cap=cap,
            page_len=page_len,
            width=width,
        )
        scratch = [
            pltpu.VMEM(keys.shape, BF16),
            pltpu.VMEM(values.shape, BF16),
            pltpu.VMEM(suffix_key_pools.shape[1:], BF16),
            pltpu.VMEM(suffix_value_pools.shape[1:], BF16),
            pltpu.VMEM((KEY_BLOCK, span), F32),
            pltpu.VMEM((KEY_BLOCK, span), F32),
            pltpu.VMEM((8, span), F32),
            pltpu.VMEM((8, span), F32),
            pltpu.VMEM((GROUP * UNIT * page_len, span), F32),
            pltpu.VMEM((8, span), F32),
            pltpu.VMEM((devices, 16, width), F32),
            pltpu.SMEM((rows // GROUP + fams + 1, 3), I32),
            pltpu.SMEM((2, fams), I32),
            pltpu.SMEM((rows + 1,), I32),
            pltpu.SemaphoreType.DMA((2,)),
            pltpu.SemaphoreType.DMA((fams,)),
            pltpu.SemaphoreType.DMA((fams,)),
        ]
        return pl.pallas_call(
            kernel,
            out_shape=jax.ShapeDtypeStruct((devices, row_dev * head_dim + 16, width), BF16),
            in_specs=[smem_spec(), vmem_spec()] + [any_spec()] * 4,
            out_specs=vmem_spec(),
            scratch_shapes=scratch,
            compiler_params=params(40),
            name="attend",
            cost_estimate=pl.CostEstimate(
                flops=8 * rows * width * prefix_dev * head_dim,
                bytes_accessed=14 * MIB,
                transcendentals=rows * width * prefix_dev,
            ),
        )(
            meta,
            recv,
            in_hbm(keys),
            in_hbm(values),
            in_hbm(suffix_key_pools[0]),
            in_hbm(suffix_value_pools[0]),
        )

    def merge(returned):
        return pl.pallas_call(
            merge_kernel,
            out_shape=[
                jax.ShapeDtypeStruct((row_dev, steps, features), BF16),
                jax.ShapeDtypeStruct((devices, row_dev * steps, features), BF16),
            ],
            in_specs=[vmem_spec()] * 4,
            out_specs=[vmem_spec()] * 2,
            compiler_params=params(12),
            name="merge",
        )(returned, flat_query, new_keys[:, 0], incoming_values[:, 0])


    def project(tokens):
        block = sum(t.shape[2] * t.shape[3] for t in tokens)
        return pl.pallas_call(
            project_kernel,
            out_shape=[
                jax.ShapeDtypeStruct((chips, block, columns), BF16),
                jax.ShapeDtypeStruct((chips, block, columns), F32),
            ],
            in_specs=[smem_spec()] + [vmem_spec()] * (len(tokens) + 1),
            out_specs=[vmem_spec()] * 2,
            compiler_params=params(16),
            name="project",
        )(core.astype(I32).reshape(1), *tokens, out_weight)

    def chip_perm(shift):
        return [(y * 2 + c, (y + shift) % chips * 2 + c) for y in range(chips) for c in range(2)]

    def project_and_sum(tokens):
        away, own = project(
            [t.reshape(chips, 2, devices // heads, -1, features) for t in tokens]
        )
        partner = [(y * 2 + c, y * 2 + 1 - c) for y in range(chips) for c in range(2)]
        arrived = lax.ppermute(away, "kv", partner)
        both = own + arrived.astype(F32)
        total = lax.dynamic_index_in_dim(both, chip, 0, keepdims=False)
        for shift in sorted(range(1, chips), key=lambda d: -min(d, chips - d)):
            part = lax.dynamic_index_in_dim(both, (chip + shift) % chips, 0, keepdims=False)
            part = lax.ppermute(part.astype(BF16), "kv", chip_perm(shift))
            total = total + part.astype(F32)
        return total.astype(BF16)

    def exchange(x):
        return lax.all_to_all(x, "grp", 0, 0, tiled=True)

    packed, *pages = prepare()
    recv = exchange(packed)
    pages = arrange(pages)
    meta = recv[:, row_dev * width, :].astype(I32)
    attended, spread = merge(exchange(attend(meta, recv, pages)))
    mixed = project_and_sum([exchange(spread)])
    return (attended, mixed)


def solution(mesh):
    in_specs = (
        P("grp", "kv", None, None),
        P("grp", "kv", None, None),
        P("grp", "kv", None, None),
        P("grp"),
        P(None, "grp"),
        P("kv", "grp", None, None),
        P("kv", "grp", None, None),
        P("grp"),
        P("grp", None),
        P("grp", None),
        P("kv", "grp", None, None),
        P("kv", "grp", None, None),
        P("kv", "grp"),
    )
    out_specs = (P("grp", None, "kv"), P("kv", "grp"))
    return jax.shard_map(
        on_device, mesh=mesh, in_specs=in_specs, out_specs=out_specs, check_vma=False
    )
```

```python
import functools
import math

import jax
import jax.numpy as jnp
from jax import lax
from jax.experimental import pallas as pl
from jax.experimental.pallas import tpu as pltpu
from jax.sharding import PartitionSpec as P

F32 = jnp.float32
BF16 = jnp.bfloat16
I32 = jnp.int32
NT = (((1,), (1,)), ((), ()))
TN = (((0,), (0,)), ((), ()))
LOG2E = math.log2(math.e)
NEG = -1e30
MIB = 1024 * 1024
GROUP = 2
KEY_BLOCK = 1024
KEY_SUB = 512
UNIT = 4


def vmem_spec():
    return pl.BlockSpec(memory_space=pltpu.VMEM)


def smem_spec():
    return pl.BlockSpec(memory_space=pltpu.SMEM)


def any_spec():
    return pl.BlockSpec(memory_space=pl.ANY)


def in_hbm(x):
    return pltpu.with_memory_space_constraint(x, pltpu.HBM)


def params(mib):
    return pltpu.CompilerParams(vmem_limit_bytes=mib * MIB)


def list_pages(base, family_ref, length_ref, holder_ref, slot_ref, devices, cap, page_len):
    rows, pages = holder_ref.shape
    lanes = 128
    holder_of = lax.broadcasted_iota(I32, (devices, lanes), 0)
    lane = lax.broadcasted_iota(I32, (devices, lanes), 1)
    listed = jnp.full((devices, lanes), -1, I32)
    for r in range(rows):
        listed = jnp.where(lane == rows * cap + r, family_ref[r], listed)
        length = length_ref[r]

        def add_page(c, carry):
            listed, count = carry
            live = jnp.clip(length - c * page_len, 0, page_len)
            holder = jnp.where(live > 0, holder_ref[r, c], -1)
            entry = (slot_ref[r, c] - base) * page_len + live - 1
            here = holder_of == holder
            listed = jnp.where(here & (lane == count), entry, listed)
            return listed, count + here.astype(I32)

        start = jnp.full((devices, lanes), r * cap, I32)
        listed, _ = lax.fori_loop(0, pages, add_page, (listed, start), unroll=8)
    return listed


def arrange_pages(
    table_ref, loads, key_ref, value_ref, key_done, value_done, key_out, value_out, sems, unroll
):
    pages, page_len, head_dim = key_ref.shape
    fams = key_done.shape[0]
    per_fam = pages // fams
    span = 256
    block = span // page_len
    row = lax.broadcasted_iota(I32, (head_dim, head_dim), 0)
    column = lax.broadcasted_iota(I32, (head_dim, head_dim), 1)
    identity = (row == column).astype(F32).astype(BF16)
    stores = []
    loads[0].wait()
    for f in range(fams):

        def turn_block(b, carry):
            listed = [table_ref[f, b * block + i] for i in range(block)]
            values = jnp.concatenate([value_ref[page] for page in listed], axis=0)
            turned = lax.dot_general(identity, values, NT, preferred_element_type=F32)
            value_done[f, :, pl.ds(pl.multiple_of(b * span, span), span)] = turned.astype(BF16)
            return carry

        lax.fori_loop(0, per_fam // block, turn_block, 0, unroll=2 * unroll)
        stores.append(pltpu.make_async_copy(value_done.at[f], value_out.at[f], sems.at[f]))
        stores[-1].start()
    loads[1].wait()
    for f in range(fams):

        def move_block(b, carry):
            for i in range(block):
                at = pl.multiple_of(b * span + i * page_len, page_len)
                key_done[f, pl.ds(at, page_len), :] = key_ref[table_ref[f, b * block + i]]
            return carry

        lax.fori_loop(0, per_fam // block, move_block, 0, unroll=unroll)
        stores.append(pltpu.make_async_copy(key_done.at[f], key_out.at[f], sems.at[fams + f]))
        stores[-1].start()
    for store in stores:
        store.wait()


def prepare_kernel(
    place_ref,
    table_hbm,
    key_hbm,
    value_hbm,
    family_hbm,
    length_hbm,
    holder_hbm,
    slot_hbm,
    query_hbm,
    packed_out,
    key_out,
    value_out,
    table_ref,
    key_ref,
    value_ref,
    key_done,
    value_done,
    family_ref,
    length_ref,
    holder_ref,
    slot_ref,
    query_ref,
    tile_ref,
    small_sems,
    sent_sems,
    in_sems,
    out_sems,
    *,
    cap,
    page_len,
):
    devices, _, lanes = packed_out.shape
    body = query_ref.shape[0]
    first = place_ref[0] == 0
    small = [
        pltpu.make_async_copy(src, dst, small_sems.at[i])
        for i, (src, dst) in enumerate(
            (
                (family_hbm, family_ref),
                (length_hbm, length_ref),
                (holder_hbm, holder_ref),
                (slot_hbm, slot_ref),
                (query_hbm, query_ref),
                (table_hbm, table_ref),
            )
        )
    ]
    for load in small:
        load.start()
    loads = [
        pltpu.make_async_copy(value_hbm, value_ref, in_sems.at[0]),
        pltpu.make_async_copy(key_hbm, key_ref, in_sems.at[1]),
    ]

    @pl.when(first)
    def _():
        for load in loads:
            load.start()

    sent = [
        pltpu.make_async_copy(
            query_ref, packed_out.at[g, pl.ds(0, body), :], sent_sems.at[g]
        )
        for g in range(devices)
    ]
    small[4].wait()
    for copy in sent:
        copy.start()
    for i in (0, 1, 2, 3, 5):
        small[i].wait()
    listed = list_pages(
        place_ref[1], family_ref, length_ref, holder_ref, slot_ref, devices, cap, page_len
    ).astype(F32)
    tile_row = lax.broadcasted_iota(I32, (16, lanes), 0)
    for g in range(devices):
        tile = jnp.where(tile_row == 0, jnp.broadcast_to(listed[g : g + 1, :], (16, lanes)), 0.0)
        tile_ref[g] = tile.astype(BF16)
    tiles = pltpu.make_async_copy(
        tile_ref, packed_out.at[:, pl.ds(body, 16), :], sent_sems.at[devices]
    )
    tiles.start()

    @pl.when(first)
    def _():
        arrange_pages(
            table_ref,
            loads,
            key_ref,
            value_ref,
            key_done,
            value_done,
            key_out,
            value_out,
            out_sems,
            2,
        )

    for copy in sent:
        copy.wait()
    tiles.wait()


def arrange_kernel(
    place_ref,
    table_ref,
    key_hbm,
    value_hbm,
    key_before,
    value_before,
    key_out,
    value_out,
    key_ref,
    value_ref,
    key_done,
    value_done,
    in_sems,
    out_sems,
):
    @pl.when(place_ref[0] == 1)
    def _():
        loads = [
            pltpu.make_async_copy(value_hbm, value_ref, in_sems.at[0]),
            pltpu.make_async_copy(key_hbm, key_ref, in_sems.at[1]),
        ]
        for load in loads:
            load.start()
        arrange_pages(
            table_ref,
            loads,
            key_ref,
            value_ref,
            key_done,
            value_done,
            key_out,
            value_out,
            out_sems,
            4,
        )


def attend_kernel(
    place_ref,
    meta_ref,
    recv_ref,
    key_hbm,
    value_hbm,
    suffix_key_hbm,
    suffix_value_hbm,
    own_ref,
    out_ref,
    key_ref,
    value_ref,
    suffix_key_ref,
    suffix_value_ref,
    score_a,
    score_b,
    top_a,
    top_b,
    score_s,
    top_s,
    lse_ref,
    pair_ref,
    count_ref,
    many_ref,
    sems,
    key_sems,
    value_sems,
    *,
    rows_dev,
    cap,
    page_len,
    width,
):
    devices = out_ref.shape[0]
    rows = devices * rows_dev
    me = place_ref[1] // cap
    owner_base = me if own_ref is None else 0
    fams, prefix, head_dim = key_ref.shape
    scale = LOG2E / math.sqrt(head_dim)
    blocks = prefix // KEY_BLOCK
    subs = KEY_BLOCK // KEY_SUB
    buffers = ((score_a, top_a), (score_b, top_b))

    def key_load(f):
        return pltpu.make_async_copy(key_hbm.at[f], key_ref.at[f], key_sems.at[f])

    def value_load(f):
        return pltpu.make_async_copy(value_hbm.at[f], value_ref.at[f], value_sems.at[f])

    suffix_loads = [
        pltpu.make_async_copy(suffix_key_hbm, suffix_key_ref, sems.at[0]),
        pltpu.make_async_copy(suffix_value_hbm, suffix_value_ref, sems.at[1]),
    ]
    key_load(0).start()
    suffix_loads[0].start()
    value_load(0).start()
    suffix_loads[1].start()
    for f in range(1, fams):
        key_load(f).start()
        value_load(f).start()

    def row_family(r):
        return meta_ref[r // rows_dev, rows_dev * cap + r % rows_dev]

    for f in range(fams):
        count_ref[0, f] = 0

    def is_taken(r):
        return True if own_ref is None else r // rows_dev != me

    def count_row(r, n):
        fam = row_family(r)
        taken = is_taken(r)
        count_ref[0, fam] = count_ref[0, fam] + jnp.int32(taken)
        many_ref[n] = r
        more = meta_ref[r // rows_dev, (r % rows_dev) * cap + UNIT] >= 0
        return n + (taken & more).astype(I32)

    many = lax.fori_loop(0, rows, count_row, 0, unroll=4)
    groups = 0
    for f in range(fams):
        count_ref[1, f] = 2 * groups
        groups = groups + (count_ref[0, f] + 1) // 2

    def place_row(r, carry):
        @pl.when(is_taken(r))
        def _():
            fam = row_family(r)
            at = count_ref[1, fam]
            count_ref[1, fam] = at + 1
            pair_ref[at // 2, 0] = fam
            pair_ref[at // 2, 1 + at % 2] = r

            @pl.when(at % 2 == 0)
            def _():
                pair_ref[at // 2, 2] = r

        return carry

    lax.fori_loop(0, rows, place_row, 0, unroll=4)
    count_ref[0, 0] = 0

    def families_to(fam):
        def one(f, carry):
            key_load(f).wait()
            value_load(f).wait()
            return carry

        lax.fori_loop(count_ref[0, 0], fam + 1, one, 0)
        count_ref[0, 0] = jnp.maximum(count_ref[0, 0], fam + 1)

    tail = rows_dev * head_dim
    lse_ref[...] = jnp.zeros_like(lse_ref)

    def load_queries(g):
        parts = []
        for i in range(GROUP):
            r = pair_ref[g, 1 + i]
            at = pl.multiple_of((r % rows_dev) * width, width)
            parts.append(recv_ref[r // rows_dev, pl.ds(at, width), :])
        return jnp.concatenate(parts, axis=0)

    def fold_max(scores):
        return jnp.max(scores.reshape(scores.shape[0] // 8, 8, scores.shape[1]), axis=0)

    def fold_sum(values):
        return jnp.sum(values.reshape(values.shape[0] // 8, 8, values.shape[1]), axis=0)

    def score_sub(query, fam, block, sub, into):
        at = block * KEY_BLOCK + sub * KEY_SUB
        scores = lax.dot_general(
            key_ref[fam, at : at + KEY_SUB, :], query, NT, preferred_element_type=F32
        )
        into[0][sub * KEY_SUB : (sub + 1) * KEY_SUB, :] = scores
        return fold_max(scores)

    token = lax.broadcasted_iota(I32, (page_len, width), 0)

    def listed_pages(r, unit):
        owner = r // rows_dev
        found = []
        for p in range(UNIT):
            entry = meta_ref[owner, (r % rows_dev) * cap + unit * UNIT + p]
            live = jnp.where(entry >= 0, entry % page_len + 1, 0)
            page = (owner_base + owner) * cap + jnp.maximum(entry, 0) // page_len
            found.append((page, live))
        return found

    def pair_pages(g):
        found = []
        for i in range(GROUP):
            found += listed_pages(pair_ref[g, 1 + i], 0)
        return found

    def suffix_scores(query, pages):
        keys = jnp.concatenate([suffix_key_ref[page] for page, _ in pages], axis=0)
        return lax.dot_general(keys, query, NT, preferred_element_type=F32)

    def suffix_part(weight, pages):
        values = jnp.concatenate([suffix_value_ref[page] for page, _ in pages], axis=0)
        return lax.dot_general(values, weight.astype(BF16), TN, preferred_element_type=F32)

    def score_suffix(query, pages):
        scores = suffix_scores(query, pages)
        dead = jnp.full((page_len, width), NEG, F32)
        tops = []
        for i in range(GROUP):
            cols = slice(i * width, (i + 1) * width)
            top = None
            for p, (_, live) in enumerate(pages):
                at = slice(p * page_len, (p + 1) * page_len)
                if p // UNIT != i:
                    score_s[at, cols] = dead
                    continue
                part = jnp.where(token < live, scores[at, cols], NEG)
                score_s[at, cols] = part
                sub_top = fold_max(part)
                top = sub_top if top is None else jnp.maximum(top, sub_top)
            tops.append(top)
        top_s[...] = jnp.concatenate(tops, axis=1)

    first_query = load_queries(0)
    first_fam = pair_ref[0, 0]
    families_to(first_fam)
    suffix_loads[0].wait()
    top = None
    for s in range(subs):
        sub_top = score_sub(first_query, first_fam, 0, s, buffers[0])
        top = sub_top if top is None else jnp.maximum(top, sub_top)
    top_a[...] = top
    score_suffix(first_query, pair_pages(0))
    suffix_loads[1].wait()

    def attend_group(g, carry):
        fam = pair_ref[g, 0]
        after = jnp.minimum(g + 1, groups - 1)
        next_fam = pair_ref[after, 0]
        families_to(next_fam)
        query = load_queries(g)
        next_query = load_queries(after)
        peak = total = acc = pending = None

        def value_part(at, weight):
            return jnp.dot(
                value_ref[fam, :, at : at + KEY_SUB], weight, preferred_element_type=F32
            )

        for b in range(blocks):
            now, later = buffers[b % 2], buffers[(b + 1) % 2]
            block_top = now[1][...]
            if b == 0:
                block_top = jnp.maximum(block_top, top_s[...])
            block_peak = jnp.max(block_top, axis=0, keepdims=True) * scale
            if peak is None:
                new_peak = block_peak
            else:
                new_peak = jnp.maximum(peak, block_peak)
                factor = jnp.exp2(peak - new_peak)
                total = total * factor
                acc = (acc + value_part(*pending)) * factor
                pending = None
            peak = new_peak
            if b == 0:
                weight = jnp.exp2(score_s[...] * scale - peak)
                total = fold_sum(weight)
                acc = suffix_part(weight, pair_pages(g))
            if b + 1 == blocks:
                score_suffix(next_query, pair_pages(after))
            top = None
            for s in range(subs):
                if b + 1 < blocks:
                    sub_top = score_sub(query, fam, b + 1, s, later)
                else:
                    sub_top = score_sub(next_query, next_fam, 0, s, later)
                top = sub_top if top is None else jnp.maximum(top, sub_top)
                if pending is not None:
                    acc = acc + value_part(*pending)
                weight = jnp.exp2(now[0][s * KEY_SUB : (s + 1) * KEY_SUB, :] * scale - peak)
                total = total + fold_sum(weight)
                pending = (b * KEY_BLOCK + s * KEY_SUB, weight.astype(BF16))
            later[1][...] = top
        acc = acc + value_part(*pending)
        total = jnp.sum(total, axis=0, keepdims=True)
        lse = peak + jnp.log2(total)
        acc = (acc * (1.0 / total)).astype(BF16)
        for i in range(GROUP):
            cols = slice(i * width, (i + 1) * width)
            put_row(pair_ref[g, 1 + i], acc[:, cols], lse[:, cols])
        return carry

    def row_place(r):
        return pl.ds(pl.multiple_of((r % rows_dev) * head_dim, head_dim), head_dim)

    def put_row(r, acc, lse):
        owner, at = r // rows_dev, r % rows_dev
        high = lse.astype(BF16).astype(F32)
        middle = (lse - high).astype(BF16).astype(F32)
        out_ref[owner, row_place(r), :] = acc
        lse_ref[owner, pl.ds(at, 1), :] = high
        lse_ref[owner, pl.ds(rows_dev + at, 1), :] = middle
        lse_ref[owner, pl.ds(2 * rows_dev + at, 1), :] = lse - high - middle

    def more_suffix(r, unit):
        owner, at = r // rows_dev, r % rows_dev
        begin = pl.multiple_of(at * width, width)
        pages = listed_pages(r, unit)
        scores = suffix_scores(recv_ref[owner, pl.ds(begin, width), :], pages)
        scores = jnp.concatenate(
            [
                jnp.where(token < live, scores[p * page_len : (p + 1) * page_len, :], NEG)
                for p, (_, live) in enumerate(pages)
            ],
            axis=0,
        )
        lse = (
            lse_ref[owner, pl.ds(at, 1), :]
            + lse_ref[owner, pl.ds(rows_dev + at, 1), :]
            + lse_ref[owner, pl.ds(2 * rows_dev + at, 1), :]
        )
        peak = jnp.maximum(lse, jnp.max(scores, axis=0, keepdims=True) * scale)
        weight = jnp.exp2(scores * scale - peak)
        factor = jnp.exp2(lse - peak)
        total = factor + jnp.sum(weight, axis=0, keepdims=True)
        acc = out_ref[owner, row_place(r), :].astype(F32) * factor + suffix_part(weight, pages)
        put_row(r, (acc * (1.0 / total)).astype(BF16), peak + jnp.log2(total))

    def finish_row(n, carry):
        r = many_ref[n]
        for unit in range(1, cap // UNIT):

            @pl.when(meta_ref[r // rows_dev, (r % rows_dev) * cap + unit * UNIT] >= 0)
            def _():
                more_suffix(r, unit)

        return carry

    lax.fori_loop(0, groups, attend_group, 0)
    families_to(fams - 1)
    lax.fori_loop(0, many, finish_row, 0)
    out_ref[:, tail:, :] = lse_ref[...].astype(BF16)
    if own_ref is not None:
        out_ref[me] = own_ref[0]


def merge_kernel(
    recv_ref,
    query_ref,
    key_ref,
    value_ref,
    out_ref,
    send_ref,
):
    devices, _, head_dim = recv_ref.shape
    rows, steps, _ = out_ref.shape
    width = query_ref.shape[0] // rows
    scale = LOG2E / math.sqrt(head_dim)
    tail = recv_ref[:, rows * head_dim :, :].astype(F32)
    fresh = lax.broadcasted_iota(I32, (steps, width), 0)
    step = lax.broadcasted_iota(I32, (steps, width), 1) % steps
    for r in range(rows):
        scores = lax.dot_general(
            key_ref[r],
            query_ref[r * width : (r + 1) * width, :],
            NT,
            preferred_element_type=F32,
        )
        scores = jnp.where(fresh <= step, scores * scale, NEG)
        new_peak = jnp.max(scores, axis=0, keepdims=True)
        weight = jnp.exp2(scores - new_peak)
        new_total = jnp.sum(weight, axis=0, keepdims=True)
        new_acc = lax.dot_general(
            value_ref[r], weight.astype(BF16), TN, preferred_element_type=F32
        )
        lse = tail[:, r, :] + tail[:, rows + r, :] + tail[:, 2 * rows + r, :]
        peak = jnp.maximum(jnp.max(lse, axis=0, keepdims=True), new_peak)
        share = jnp.exp2(lse - peak)
        new_share = jnp.exp2(new_peak - peak)
        total = jnp.sum(share, axis=0, keepdims=True) + new_share * new_total
        acc = new_acc * new_share
        for g in range(devices):
            part = recv_ref[g, r * head_dim : (r + 1) * head_dim, :].astype(F32)
            acc = acc + part * share[g : g + 1, :]
        turned = (acc * (1.0 / total)).T.astype(BF16)
        for h in range(width // steps):
            tile = turned[h * steps : (h + 1) * steps, :]
            cols = slice(h * head_dim, (h + 1) * head_dim)
            out_ref[r, :, cols] = tile
            for g in range(devices):
                send_ref[g, r * steps : (r + 1) * steps, cols] = tile


def project_kernel(core_ref, *refs):
    token_refs, weight_ref, away_ref, own_ref = refs[:-3], *refs[-3:]
    chips, tokens_out, columns = own_ref.shape
    groups = token_refs[0].shape[2]
    step = 256
    for side, out_ref in ((1 - core_ref[0], away_ref), (core_ref[0], own_ref)):
        for c in range(columns // step):
            cols = slice(c * step, (c + 1) * step)
            at = 0
            for token_ref in token_refs:
                steps, features = token_ref.shape[3:]
                tokens = jnp.concatenate([token_ref[y, side] for y in range(chips)], axis=0)
                part = jnp.dot(
                    tokens.reshape(-1, features), weight_ref[:, cols], preferred_element_type=F32
                )
                part = part.astype(out_ref.dtype).reshape(chips, groups, steps, step)
                for g in range(groups):
                    row = g * (tokens_out // groups) + at
                    out_ref[:, row : row + steps, cols] = part[:, g]
                at += steps


def on_device(
    queries,
    new_keys,
    incoming_values,
    family,
    prefix_table,
    prefix_key_pool,
    prefix_value_pool,
    suffix_len,
    suffix_holder,
    suffix_slot,
    suffix_key_pools,
    suffix_value_pools,
    out_weight,
):
    devices = lax.axis_size("grp")
    heads = lax.axis_size("kv")
    row_dev, local_heads, steps, head_dim = queries.shape
    width = local_heads * steps
    features = local_heads * head_dim
    fams, pages_dev = prefix_table.shape
    page_len = prefix_key_pool.shape[2]
    prefix_dev = pages_dev * page_len
    own_pages = suffix_key_pools.shape[1]
    cap = own_pages // devices
    columns = out_weight.shape[1]
    core = lax.axis_index("kv") % 2
    chip = lax.axis_index("kv") // 2
    chips = heads // 2
    flat_query = queries.reshape(row_dev * width, head_dim)

    place = jnp.stack([core, lax.axis_index("grp") * cap]).astype(I32)
    key_shape = (fams, prefix_dev, head_dim)
    value_shape = (fams, head_dim, prefix_dev)
    page_scratch = [
        pltpu.VMEM(prefix_key_pool.shape[1:], BF16),
        pltpu.VMEM(prefix_value_pool.shape[1:], BF16),
        pltpu.VMEM(key_shape, BF16),
        pltpu.VMEM(value_shape, BF16),
    ]
    page_operands = [
        in_hbm(prefix_table),
        in_hbm(prefix_key_pool[0]),
        in_hbm(prefix_value_pool[0]),
    ]

    def prepare():
        return pl.pallas_call(
            functools.partial(prepare_kernel, cap=cap, page_len=page_len),
            out_shape=[
                pltpu.HBM((devices, row_dev * width + 16, head_dim), BF16),
                pltpu.HBM(key_shape, BF16),
                pltpu.HBM(value_shape, BF16),
            ],
            in_specs=[smem_spec()] + [any_spec()] * 8,
            out_specs=[any_spec()] * 3,
            scratch_shapes=[pltpu.SMEM(prefix_table.shape, I32)]
            + page_scratch
            + [
                pltpu.SMEM(family.shape, I32),
                pltpu.SMEM(suffix_len.shape, I32),
                pltpu.SMEM(suffix_holder.shape, I32),
                pltpu.SMEM(suffix_slot.shape, I32),
                pltpu.VMEM(flat_query.shape, BF16),
                pltpu.VMEM((devices, 16, head_dim), BF16),
                pltpu.SemaphoreType.DMA((6,)),
                pltpu.SemaphoreType.DMA((devices + 1,)),
                pltpu.SemaphoreType.DMA((2,)),
                pltpu.SemaphoreType.DMA((2 * fams,)),
            ],
            compiler_params=params(24),
            name="prepare",
        )(
            place,
            *page_operands,
            in_hbm(family),
            in_hbm(suffix_len),
            in_hbm(suffix_holder),
            in_hbm(suffix_slot),
            in_hbm(flat_query),
        )

    def arrange(before):
        return pl.pallas_call(
            arrange_kernel,
            out_shape=[pltpu.HBM(key_shape, BF16), pltpu.HBM(value_shape, BF16)],
            in_specs=[smem_spec()] * 2 + [any_spec()] * 4,
            out_specs=[any_spec()] * 2,
            input_output_aliases={4: 0, 5: 1},
            scratch_shapes=page_scratch
            + [
                pltpu.SemaphoreType.DMA((2,)),
                pltpu.SemaphoreType.DMA((2 * fams,)),
            ],
            compiler_params=params(24),
            name="arrange",
            cost_estimate=pl.CostEstimate(flops=0, bytes_accessed=20 * MIB, transcendentals=0),
        )(place, *page_operands, *[in_hbm(x) for x in before])

    def attend(recv, pages, own=None):
        owners = recv.shape[0]
        meta = recv[:, row_dev * width, :].astype(I32)
        span = GROUP * width
        rows = owners * row_dev
        keys, values = pages
        kernel = functools.partial(
            attend_kernel,
            rows_dev=row_dev,
            cap=cap,
            page_len=page_len,
            width=width,
        )
        last = [] if own is None else [own]
        body = kernel
        if own is None:
            body = lambda *refs: kernel(*refs[:7], None, *refs[7:])
        scratch = [
            pltpu.VMEM(keys.shape, BF16),
            pltpu.VMEM(values.shape, BF16),
            pltpu.VMEM(suffix_key_pools.shape[1:], BF16),
            pltpu.VMEM(suffix_value_pools.shape[1:], BF16),
            pltpu.VMEM((KEY_BLOCK, span), F32),
            pltpu.VMEM((KEY_BLOCK, span), F32),
            pltpu.VMEM((8, span), F32),
            pltpu.VMEM((8, span), F32),
            pltpu.VMEM((GROUP * UNIT * page_len, span), F32),
            pltpu.VMEM((8, span), F32),
            pltpu.VMEM((owners, 16, width), F32),
            pltpu.SMEM((rows // GROUP + fams + 1, 3), I32),
            pltpu.SMEM((2, fams), I32),
            pltpu.SMEM((rows + 1,), I32),
            pltpu.SemaphoreType.DMA((2,)),
            pltpu.SemaphoreType.DMA((fams,)),
            pltpu.SemaphoreType.DMA((fams,)),
        ]
        return pl.pallas_call(
            body,
            out_shape=jax.ShapeDtypeStruct((owners, row_dev * head_dim + 16, width), BF16),
            in_specs=[smem_spec()] * 2 + [vmem_spec()] + [any_spec()] * 4 + [vmem_spec()] * len(last),
            out_specs=vmem_spec(),
            scratch_shapes=scratch,
            compiler_params=params(40),
            name="attend_own" if own is None else "attend",
            cost_estimate=pl.CostEstimate(
                flops=8 * rows * width * prefix_dev * head_dim,
                bytes_accessed=14 * MIB,
                transcendentals=rows * width * prefix_dev,
            ),
        )(
            place,
            meta,
            recv,
            in_hbm(keys),
            in_hbm(values),
            in_hbm(suffix_key_pools[0]),
            in_hbm(suffix_value_pools[0]),
            *last,
        )

    def merge(returned):
        return pl.pallas_call(
            merge_kernel,
            out_shape=[
                jax.ShapeDtypeStruct((row_dev, steps, features), BF16),
                jax.ShapeDtypeStruct((devices, row_dev * steps, features), BF16),
            ],
            in_specs=[vmem_spec()] * 4,
            out_specs=[vmem_spec()] * 2,
            compiler_params=params(12),
            name="merge",
        )(returned, flat_query, new_keys[:, 0], incoming_values[:, 0])


    def project(tokens):
        block = sum(t.shape[2] * t.shape[3] for t in tokens)
        return pl.pallas_call(
            project_kernel,
            out_shape=[
                jax.ShapeDtypeStruct((chips, block, columns), BF16),
                jax.ShapeDtypeStruct((chips, block, columns), F32),
            ],
            in_specs=[smem_spec()] + [vmem_spec()] * (len(tokens) + 1),
            out_specs=[vmem_spec()] * 2,
            compiler_params=params(16),
            name="project",
        )(core.astype(I32).reshape(1), *tokens, out_weight)

    def chip_perm(shift):
        return [(y * 2 + c, (y + shift) % chips * 2 + c) for y in range(chips) for c in range(2)]

    def project_and_sum(tokens):
        away, own = project(
            [t.reshape(chips, 2, devices // heads, -1, features) for t in tokens]
        )
        partner = [(y * 2 + c, y * 2 + 1 - c) for y in range(chips) for c in range(2)]
        arrived = lax.ppermute(away, "kv", partner)
        both = own + arrived.astype(F32)
        total = lax.dynamic_index_in_dim(both, chip, 0, keepdims=False)
        for shift in sorted(range(1, chips), key=lambda d: -min(d, chips - d)):
            part = lax.dynamic_index_in_dim(both, (chip + shift) % chips, 0, keepdims=False)
            part = lax.ppermute(part.astype(BF16), "kv", chip_perm(shift))
            total = total + part.astype(F32)
        return total.astype(BF16)

    def exchange(x):
        return lax.all_to_all(x, "grp", 0, 0, tiled=True)

    packed, *pages = prepare()
    recv = exchange(packed)
    pages = arrange(pages)
    own = attend(lax.dynamic_slice_in_dim(packed, lax.axis_index("grp"), 1), pages)
    attended, spread = merge(exchange(attend(recv, pages, own)))
    mixed = project_and_sum([exchange(spread)])
    return (attended, mixed)


def solution(mesh):
    in_specs = (
        P("grp", "kv", None, None),
        P("grp", "kv", None, None),
        P("grp", "kv", None, None),
        P("grp"),
        P(None, "grp"),
        P("kv", "grp", None, None),
        P("kv", "grp", None, None),
        P("grp"),
        P("grp", None),
        P("grp", None),
        P("kv", "grp", None, None),
        P("kv", "grp", None, None),
        P("kv", "grp"),
    )
    out_specs = (P("grp", None, "kv"), P("kv", "grp"))
    return jax.shard_map(
        on_device, mesh=mesh, in_specs=in_specs, out_specs=out_specs, check_vma=False
    )
```

```python
import functools
import math

import jax
import jax.numpy as jnp
from jax import lax
from jax.experimental import pallas as pl
from jax.experimental.pallas import tpu as pltpu
from jax.sharding import PartitionSpec as P

F32 = jnp.float32
BF16 = jnp.bfloat16
I32 = jnp.int32
NT = (((1,), (1,)), ((), ()))
TN = (((0,), (0,)), ((), ()))
LOG2E = math.log2(math.e)
NEG = -1e30
MIB = 1024 * 1024
GROUP = 2
KEY_BLOCK = 1024
KEY_SUB = 512
UNIT = 4


def vmem_spec():
    return pl.BlockSpec(memory_space=pltpu.VMEM)


def smem_spec():
    return pl.BlockSpec(memory_space=pltpu.SMEM)


def any_spec():
    return pl.BlockSpec(memory_space=pl.ANY)


def in_hbm(x):
    return pltpu.with_memory_space_constraint(x, pltpu.HBM)


def params(mib):
    return pltpu.CompilerParams(vmem_limit_bytes=mib * MIB)


def list_pages(base, family_ref, length_ref, holder_ref, slot_ref, devices, cap, page_len):
    rows, pages = holder_ref.shape
    lanes = 128
    holder_of = lax.broadcasted_iota(I32, (devices, lanes), 0)
    lane = lax.broadcasted_iota(I32, (devices, lanes), 1)
    listed = jnp.full((devices, lanes), -1, I32)
    for r in range(rows):
        listed = jnp.where(lane == rows * cap + r, family_ref[r], listed)
        length = length_ref[r]

        def add_page(c, carry):
            listed, count = carry
            live = jnp.clip(length - c * page_len, 0, page_len)
            holder = jnp.where(live > 0, holder_ref[r, c], -1)
            entry = (slot_ref[r, c] - base) * page_len + live - 1
            here = holder_of == holder
            listed = jnp.where(here & (lane == count), entry, listed)
            return listed, count + here.astype(I32)

        start = jnp.full((devices, lanes), r * cap, I32)
        listed, _ = lax.fori_loop(0, pages, add_page, (listed, start), unroll=8)
    return listed


def arrange_pages(
    table_ref, loads, key_ref, value_ref, key_done, value_done, key_out, value_out, sems, unroll
):
    pages, page_len, head_dim = key_ref.shape
    fams = key_done.shape[0]
    per_fam = pages // fams
    span = 256
    block = span // page_len
    row = lax.broadcasted_iota(I32, (head_dim, head_dim), 0)
    column = lax.broadcasted_iota(I32, (head_dim, head_dim), 1)
    identity = (row == column).astype(F32).astype(BF16)
    stores = []
    loads[0].wait()
    for f in range(fams):

        def turn_block(b, carry):
            listed = [table_ref[f, b * block + i] for i in range(block)]
            values = jnp.concatenate([value_ref[page] for page in listed], axis=0)
            turned = lax.dot_general(identity, values, NT, preferred_element_type=F32)
            value_done[f, :, pl.ds(pl.multiple_of(b * span, span), span)] = turned.astype(BF16)
            return carry

        lax.fori_loop(0, per_fam // block, turn_block, 0, unroll=min(2 * unroll, per_fam // block))
        stores.append(pltpu.make_async_copy(value_done.at[f], value_out.at[f], sems.at[f]))
        stores[-1].start()
    loads[1].wait()
    for f in range(fams):

        def move_block(b, carry):
            for i in range(block):
                at = pl.multiple_of(b * span + i * page_len, page_len)
                key_done[f, pl.ds(at, page_len), :] = key_ref[table_ref[f, b * block + i]]
            return carry

        lax.fori_loop(0, per_fam // block, move_block, 0, unroll=unroll)
        stores.append(pltpu.make_async_copy(key_done.at[f], key_out.at[f], sems.at[fams + f]))
        stores[-1].start()
    for store in stores:
        store.wait()


def prepare_kernel(
    place_ref,
    table_hbm,
    key_hbm,
    value_hbm,
    family_hbm,
    length_hbm,
    holder_hbm,
    slot_hbm,
    query_hbm,
    packed_out,
    key_out,
    value_out,
    table_ref,
    key_ref,
    value_ref,
    key_done,
    value_done,
    family_ref,
    length_ref,
    holder_ref,
    slot_ref,
    query_ref,
    tile_ref,
    small_sems,
    sent_sems,
    in_sems,
    out_sems,
    *,
    cap,
    page_len,
):
    devices, _, lanes = packed_out.shape
    body = query_ref.shape[0]
    first = place_ref[0] == 0
    small = [
        pltpu.make_async_copy(src, dst, small_sems.at[i])
        for i, (src, dst) in enumerate(
            (
                (family_hbm, family_ref),
                (length_hbm, length_ref),
                (holder_hbm, holder_ref),
                (slot_hbm, slot_ref),
                (query_hbm, query_ref),
                (table_hbm, table_ref),
            )
        )
    ]
    for load in small:
        load.start()
    loads = [
        pltpu.make_async_copy(value_hbm, value_ref, in_sems.at[0]),
        pltpu.make_async_copy(key_hbm, key_ref, in_sems.at[1]),
    ]

    @pl.when(first)
    def _():
        for load in loads:
            load.start()

    sent = [
        pltpu.make_async_copy(
            query_ref, packed_out.at[g, pl.ds(0, body), :], sent_sems.at[g]
        )
        for g in range(devices)
    ]
    small[4].wait()
    for copy in sent:
        copy.start()
    for i in (0, 1, 2, 3, 5):
        small[i].wait()
    listed = list_pages(
        place_ref[1], family_ref, length_ref, holder_ref, slot_ref, devices, cap, page_len
    ).astype(F32)
    tile_row = lax.broadcasted_iota(I32, (16, lanes), 0)
    for g in range(devices):
        tile = jnp.where(tile_row == 0, jnp.broadcast_to(listed[g : g + 1, :], (16, lanes)), 0.0)
        tile_ref[g] = tile.astype(BF16)
    tiles = pltpu.make_async_copy(
        tile_ref, packed_out.at[:, pl.ds(body, 16), :], sent_sems.at[devices]
    )
    tiles.start()

    @pl.when(first)
    def _():
        arrange_pages(
            table_ref,
            loads,
            key_ref,
            value_ref,
            key_done,
            value_done,
            key_out,
            value_out,
            out_sems,
            2,
        )

    for copy in sent:
        copy.wait()
    tiles.wait()


def arrange_kernel(
    place_ref,
    table_ref,
    key_hbm,
    value_hbm,
    key_before,
    value_before,
    key_out,
    value_out,
    key_ref,
    value_ref,
    key_done,
    value_done,
    in_sems,
    out_sems,
):
    @pl.when(place_ref[0] == 1)
    def _():
        loads = [
            pltpu.make_async_copy(value_hbm, value_ref, in_sems.at[0]),
            pltpu.make_async_copy(key_hbm, key_ref, in_sems.at[1]),
        ]
        for load in loads:
            load.start()
        arrange_pages(
            table_ref,
            loads,
            key_ref,
            value_ref,
            key_done,
            value_done,
            key_out,
            value_out,
            out_sems,
            8,
        )


def attend_kernel(
    place_ref,
    meta_ref,
    recv_ref,
    key_hbm,
    value_hbm,
    suffix_key_hbm,
    suffix_value_hbm,
    own_ref,
    out_ref,
    key_ref,
    value_ref,
    suffix_key_ref,
    suffix_value_ref,
    score_a,
    score_b,
    top_a,
    top_b,
    score_s,
    top_s,
    lse_ref,
    pair_ref,
    count_ref,
    many_ref,
    sems,
    key_sems,
    value_sems,
    *,
    rows_dev,
    cap,
    page_len,
    width,
):
    devices = out_ref.shape[0]
    rows = devices * rows_dev
    me = place_ref[1] // cap
    owner_base = me if own_ref is None else 0
    fams, prefix, head_dim = key_ref.shape
    scale = LOG2E / math.sqrt(head_dim)
    blocks = prefix // KEY_BLOCK
    subs = KEY_BLOCK // KEY_SUB
    buffers = ((score_a, top_a), (score_b, top_b))

    def key_load(f):
        return pltpu.make_async_copy(key_hbm.at[f], key_ref.at[f], key_sems.at[f])

    def value_load(f):
        return pltpu.make_async_copy(value_hbm.at[f], value_ref.at[f], value_sems.at[f])

    suffix_loads = [
        pltpu.make_async_copy(suffix_key_hbm, suffix_key_ref, sems.at[0]),
        pltpu.make_async_copy(suffix_value_hbm, suffix_value_ref, sems.at[1]),
    ]
    key_load(0).start()
    suffix_loads[0].start()
    value_load(0).start()
    suffix_loads[1].start()
    for f in range(1, fams):
        key_load(f).start()
        value_load(f).start()

    def row_family(r):
        return meta_ref[r // rows_dev, rows_dev * cap + r % rows_dev]

    for f in range(fams):
        count_ref[0, f] = 0

    def is_taken(r):
        return True if own_ref is None else r // rows_dev != me

    def count_row(r, n):
        fam = row_family(r)
        taken = is_taken(r)
        count_ref[0, fam] = count_ref[0, fam] + jnp.int32(taken)
        many_ref[n] = r
        more = meta_ref[r // rows_dev, (r % rows_dev) * cap + UNIT] >= 0
        return n + (taken & more).astype(I32)

    many = lax.fori_loop(0, rows, count_row, 0, unroll=4)
    groups = 0
    for f in range(fams):
        count_ref[1, f] = 2 * groups
        groups = groups + (count_ref[0, f] + 1) // 2

    def place_row(r, carry):
        @pl.when(is_taken(r))
        def _():
            fam = row_family(r)
            at = count_ref[1, fam]
            count_ref[1, fam] = at + 1
            pair_ref[at // 2, 0] = fam
            pair_ref[at // 2, 1 + at % 2] = r

            @pl.when(at % 2 == 0)
            def _():
                pair_ref[at // 2, 2] = r

        return carry

    lax.fori_loop(0, rows, place_row, 0, unroll=4)
    count_ref[0, 0] = 0

    def families_to(fam):
        def one(f, carry):
            key_load(f).wait()
            value_load(f).wait()
            return carry

        lax.fori_loop(count_ref[0, 0], fam + 1, one, 0)
        count_ref[0, 0] = jnp.maximum(count_ref[0, 0], fam + 1)

    tail = rows_dev * head_dim
    lse_ref[...] = jnp.zeros_like(lse_ref)

    def load_queries(g):
        parts = []
        for i in range(GROUP):
            r = pair_ref[g, 1 + i]
            at = pl.multiple_of((r % rows_dev) * width, width)
            parts.append(recv_ref[r // rows_dev, pl.ds(at, width), :])
        return jnp.concatenate(parts, axis=0)

    def fold_max(scores):
        return jnp.max(scores.reshape(scores.shape[0] // 8, 8, scores.shape[1]), axis=0)

    def fold_sum(values):
        return jnp.sum(values.reshape(values.shape[0] // 8, 8, values.shape[1]), axis=0)

    def score_sub(query, fam, block, sub, into):
        at = block * KEY_BLOCK + sub * KEY_SUB
        scores = lax.dot_general(
            key_ref[fam, at : at + KEY_SUB, :], query, NT, preferred_element_type=F32
        )
        into[0][sub * KEY_SUB : (sub + 1) * KEY_SUB, :] = scores
        return fold_max(scores)

    token = lax.broadcasted_iota(I32, (page_len, width), 0)

    def listed_pages(r, unit):
        owner = r // rows_dev
        found = []
        for p in range(UNIT):
            entry = meta_ref[owner, (r % rows_dev) * cap + unit * UNIT + p]
            live = jnp.where(entry >= 0, entry % page_len + 1, 0)
            page = (owner_base + owner) * cap + jnp.maximum(entry, 0) // page_len
            found.append((page, live))
        return found

    def pair_pages(g):
        found = []
        for i in range(GROUP):
            found += listed_pages(pair_ref[g, 1 + i], 0)
        return found

    def suffix_scores(query, pages):
        keys = jnp.concatenate([suffix_key_ref[page] for page, _ in pages], axis=0)
        return lax.dot_general(keys, query, NT, preferred_element_type=F32)

    def suffix_part(weight, pages):
        values = jnp.concatenate([suffix_value_ref[page] for page, _ in pages], axis=0)
        return lax.dot_general(values, weight.astype(BF16), TN, preferred_element_type=F32)

    def score_suffix(query, pages):
        scores = suffix_scores(query, pages)
        dead = jnp.full((page_len, width), NEG, F32)
        tops = []
        for i in range(GROUP):
            cols = slice(i * width, (i + 1) * width)
            top = None
            for p, (_, live) in enumerate(pages):
                at = slice(p * page_len, (p + 1) * page_len)
                if p // UNIT != i:
                    score_s[at, cols] = dead
                    continue
                part = jnp.where(token < live, scores[at, cols], NEG)
                score_s[at, cols] = part
                sub_top = fold_max(part)
                top = sub_top if top is None else jnp.maximum(top, sub_top)
            tops.append(top)
        top_s[...] = jnp.concatenate(tops, axis=1)

    first_query = load_queries(0)
    first_fam = pair_ref[0, 0]
    families_to(first_fam)
    suffix_loads[0].wait()
    top = None
    for s in range(subs):
        sub_top = score_sub(first_query, first_fam, 0, s, buffers[0])
        top = sub_top if top is None else jnp.maximum(top, sub_top)
    top_a[...] = top
    score_suffix(first_query, pair_pages(0))
    suffix_loads[1].wait()

    def attend_group(g, carry):
        fam = pair_ref[g, 0]
        after = jnp.minimum(g + 1, groups - 1)
        next_fam = pair_ref[after, 0]
        families_to(next_fam)
        query = load_queries(g)
        next_query = load_queries(after)
        peak = total = acc = pending = None

        def value_part(at, weight):
            return jnp.dot(
                value_ref[fam, :, at : at + KEY_SUB], weight, preferred_element_type=F32
            )

        for b in range(blocks):
            now, later = buffers[b % 2], buffers[(b + 1) % 2]
            block_top = now[1][...]
            if b == 0:
                block_top = jnp.maximum(block_top, top_s[...])
            block_peak = jnp.max(block_top, axis=0, keepdims=True) * scale
            if peak is None:
                new_peak = block_peak
            else:
                new_peak = jnp.maximum(peak, block_peak)
                factor = jnp.exp2(peak - new_peak)
                total = total * factor
                acc = (acc + value_part(*pending)) * factor
                pending = None
            peak = new_peak
            if b == 0:
                weight = jnp.exp2(score_s[...] * scale - peak)
                total = fold_sum(weight)
                acc = suffix_part(weight, pair_pages(g))
            if b + 1 == blocks:
                score_suffix(next_query, pair_pages(after))
            top = None
            for s in range(subs):
                if b + 1 < blocks:
                    sub_top = score_sub(query, fam, b + 1, s, later)
                else:
                    sub_top = score_sub(next_query, next_fam, 0, s, later)
                top = sub_top if top is None else jnp.maximum(top, sub_top)
                if pending is not None:
                    acc = acc + value_part(*pending)
                weight = jnp.exp2(now[0][s * KEY_SUB : (s + 1) * KEY_SUB, :] * scale - peak)
                total = total + fold_sum(weight)
                pending = (b * KEY_BLOCK + s * KEY_SUB, weight.astype(BF16))
            later[1][...] = top
        acc = acc + value_part(*pending)
        total = jnp.sum(total, axis=0, keepdims=True)
        lse = peak + jnp.log2(total)
        acc = (acc * (1.0 / total)).astype(BF16)
        for i in range(GROUP):
            cols = slice(i * width, (i + 1) * width)
            put_row(pair_ref[g, 1 + i], acc[:, cols], lse[:, cols])
        return carry

    def row_place(r):
        return pl.ds(pl.multiple_of((r % rows_dev) * head_dim, head_dim), head_dim)

    def put_row(r, acc, lse):
        owner, at = r // rows_dev, r % rows_dev
        high = lse.astype(BF16).astype(F32)
        middle = (lse - high).astype(BF16).astype(F32)
        out_ref[owner, row_place(r), :] = acc
        lse_ref[owner, pl.ds(at, 1), :] = high
        lse_ref[owner, pl.ds(rows_dev + at, 1), :] = middle
        lse_ref[owner, pl.ds(2 * rows_dev + at, 1), :] = lse - high - middle

    def more_suffix(r, unit):
        owner, at = r // rows_dev, r % rows_dev
        begin = pl.multiple_of(at * width, width)
        pages = listed_pages(r, unit)
        scores = suffix_scores(recv_ref[owner, pl.ds(begin, width), :], pages)
        scores = jnp.concatenate(
            [
                jnp.where(token < live, scores[p * page_len : (p + 1) * page_len, :], NEG)
                for p, (_, live) in enumerate(pages)
            ],
            axis=0,
        )
        lse = (
            lse_ref[owner, pl.ds(at, 1), :]
            + lse_ref[owner, pl.ds(rows_dev + at, 1), :]
            + lse_ref[owner, pl.ds(2 * rows_dev + at, 1), :]
        )
        peak = jnp.maximum(lse, jnp.max(scores, axis=0, keepdims=True) * scale)
        weight = jnp.exp2(scores * scale - peak)
        factor = jnp.exp2(lse - peak)
        total = factor + jnp.sum(weight, axis=0, keepdims=True)
        acc = out_ref[owner, row_place(r), :].astype(F32) * factor + suffix_part(weight, pages)
        put_row(r, (acc * (1.0 / total)).astype(BF16), peak + jnp.log2(total))

    def finish_row(n, carry):
        r = many_ref[n]
        for unit in range(1, cap // UNIT):

            @pl.when(meta_ref[r // rows_dev, (r % rows_dev) * cap + unit * UNIT] >= 0)
            def _():
                more_suffix(r, unit)

        return carry

    lax.fori_loop(0, groups, attend_group, 0)
    families_to(fams - 1)
    lax.fori_loop(0, many, finish_row, 0)
    out_ref[:, tail:, :] = lse_ref[...].astype(BF16)
    if own_ref is not None:
        out_ref[me] = own_ref[0]


def merge_kernel(
    recv_ref,
    query_ref,
    key_ref,
    value_ref,
    out_ref,
    send_ref,
):
    devices, _, head_dim = recv_ref.shape
    rows, steps, _ = out_ref.shape
    width = query_ref.shape[0] // rows
    scale = LOG2E / math.sqrt(head_dim)
    tail = recv_ref[:, rows * head_dim :, :].astype(F32)
    fresh = lax.broadcasted_iota(I32, (steps, width), 0)
    step = lax.broadcasted_iota(I32, (steps, width), 1) % steps
    for r in range(rows):
        scores = lax.dot_general(
            key_ref[r],
            query_ref[r * width : (r + 1) * width, :],
            NT,
            preferred_element_type=F32,
        )
        scores = jnp.where(fresh <= step, scores * scale, NEG)
        new_peak = jnp.max(scores, axis=0, keepdims=True)
        weight = jnp.exp2(scores - new_peak)
        new_total = jnp.sum(weight, axis=0, keepdims=True)
        new_acc = lax.dot_general(
            value_ref[r], weight.astype(BF16), TN, preferred_element_type=F32
        )
        lse = tail[:, r, :] + tail[:, rows + r, :] + tail[:, 2 * rows + r, :]
        peak = jnp.maximum(jnp.max(lse, axis=0, keepdims=True), new_peak)
        share = jnp.exp2(lse - peak)
        new_share = jnp.exp2(new_peak - peak)
        total = jnp.sum(share, axis=0, keepdims=True) + new_share * new_total
        acc = new_acc * new_share
        for g in range(devices):
            part = recv_ref[g, r * head_dim : (r + 1) * head_dim, :].astype(F32)
            acc = acc + part * share[g : g + 1, :]
        turned = (acc * (1.0 / total)).T.astype(BF16)
        for h in range(width // steps):
            tile = turned[h * steps : (h + 1) * steps, :]
            cols = slice(h * head_dim, (h + 1) * head_dim)
            out_ref[r, :, cols] = tile
            for g in range(devices):
                send_ref[g, r * steps : (r + 1) * steps, cols] = tile


def project_kernel(core_ref, *refs):
    token_refs, weight_ref, away_ref, own_ref = refs[:-3], *refs[-3:]
    chips, tokens_out, columns = own_ref.shape
    groups = token_refs[0].shape[2]
    step = 256
    for side, out_ref in ((1 - core_ref[0], away_ref), (core_ref[0], own_ref)):
        for c in range(columns // step):
            cols = slice(c * step, (c + 1) * step)
            at = 0
            for token_ref in token_refs:
                steps, features = token_ref.shape[3:]
                tokens = jnp.concatenate([token_ref[y, side] for y in range(chips)], axis=0)
                part = jnp.dot(
                    tokens.reshape(-1, features), weight_ref[:, cols], preferred_element_type=F32
                )
                part = part.astype(out_ref.dtype).reshape(chips, groups, steps, step)
                for g in range(groups):
                    row = g * (tokens_out // groups) + at
                    out_ref[:, row : row + steps, cols] = part[:, g]
                at += steps


def on_device(
    queries,
    new_keys,
    incoming_values,
    family,
    prefix_table,
    prefix_key_pool,
    prefix_value_pool,
    suffix_len,
    suffix_holder,
    suffix_slot,
    suffix_key_pools,
    suffix_value_pools,
    out_weight,
):
    devices = lax.axis_size("grp")
    heads = lax.axis_size("kv")
    row_dev, local_heads, steps, head_dim = queries.shape
    width = local_heads * steps
    features = local_heads * head_dim
    fams, pages_dev = prefix_table.shape
    page_len = prefix_key_pool.shape[2]
    prefix_dev = pages_dev * page_len
    own_pages = suffix_key_pools.shape[1]
    cap = own_pages // devices
    columns = out_weight.shape[1]
    core = lax.axis_index("kv") % 2
    chip = lax.axis_index("kv") // 2
    chips = heads // 2
    flat_query = queries.reshape(row_dev * width, head_dim)

    place = jnp.stack([core, lax.axis_index("grp") * cap]).astype(I32)
    key_shape = (fams, prefix_dev, head_dim)
    value_shape = (fams, head_dim, prefix_dev)
    page_scratch = [
        pltpu.VMEM(prefix_key_pool.shape[1:], BF16),
        pltpu.VMEM(prefix_value_pool.shape[1:], BF16),
        pltpu.VMEM(key_shape, BF16),
        pltpu.VMEM(value_shape, BF16),
    ]
    page_operands = [
        in_hbm(prefix_table),
        in_hbm(prefix_key_pool[0]),
        in_hbm(prefix_value_pool[0]),
    ]

    def prepare():
        return pl.pallas_call(
            functools.partial(prepare_kernel, cap=cap, page_len=page_len),
            out_shape=[
                pltpu.HBM((devices, row_dev * width + 16, head_dim), BF16),
                pltpu.HBM(key_shape, BF16),
                pltpu.HBM(value_shape, BF16),
            ],
            in_specs=[smem_spec()] + [any_spec()] * 8,
            out_specs=[any_spec()] * 3,
            scratch_shapes=[pltpu.SMEM(prefix_table.shape, I32)]
            + page_scratch
            + [
                pltpu.SMEM(family.shape, I32),
                pltpu.SMEM(suffix_len.shape, I32),
                pltpu.SMEM(suffix_holder.shape, I32),
                pltpu.SMEM(suffix_slot.shape, I32),
                pltpu.VMEM(flat_query.shape, BF16),
                pltpu.VMEM((devices, 16, head_dim), BF16),
                pltpu.SemaphoreType.DMA((6,)),
                pltpu.SemaphoreType.DMA((devices + 1,)),
                pltpu.SemaphoreType.DMA((2,)),
                pltpu.SemaphoreType.DMA((2 * fams,)),
            ],
            compiler_params=params(24),
            name="prepare",
        )(
            place,
            *page_operands,
            in_hbm(family),
            in_hbm(suffix_len),
            in_hbm(suffix_holder),
            in_hbm(suffix_slot),
            in_hbm(flat_query),
        )

    def arrange(before):
        return pl.pallas_call(
            arrange_kernel,
            out_shape=[pltpu.HBM(key_shape, BF16), pltpu.HBM(value_shape, BF16)],
            in_specs=[smem_spec()] * 2 + [any_spec()] * 4,
            out_specs=[any_spec()] * 2,
            input_output_aliases={4: 0, 5: 1},
            scratch_shapes=page_scratch
            + [
                pltpu.SemaphoreType.DMA((2,)),
                pltpu.SemaphoreType.DMA((2 * fams,)),
            ],
            compiler_params=params(24),
            name="arrange",
            cost_estimate=pl.CostEstimate(flops=0, bytes_accessed=20 * MIB, transcendentals=0),
        )(place, *page_operands, *[in_hbm(x) for x in before])

    def attend(recv, pages, own=None):
        owners = recv.shape[0]
        meta = recv[:, row_dev * width, :].astype(I32)
        span = GROUP * width
        rows = owners * row_dev
        keys, values = pages
        kernel = functools.partial(
            attend_kernel,
            rows_dev=row_dev,
            cap=cap,
            page_len=page_len,
            width=width,
        )
        last = [] if own is None else [own]
        body = kernel
        if own is None:
            body = lambda *refs: kernel(*refs[:7], None, *refs[7:])
        scratch = [
            pltpu.VMEM(keys.shape, BF16),
            pltpu.VMEM(values.shape, BF16),
            pltpu.VMEM(suffix_key_pools.shape[1:], BF16),
            pltpu.VMEM(suffix_value_pools.shape[1:], BF16),
            pltpu.VMEM((KEY_BLOCK, span), F32),
            pltpu.VMEM((KEY_BLOCK, span), F32),
            pltpu.VMEM((8, span), F32),
            pltpu.VMEM((8, span), F32),
            pltpu.VMEM((GROUP * UNIT * page_len, span), F32),
            pltpu.VMEM((8, span), F32),
            pltpu.VMEM((owners, 16, width), F32),
            pltpu.SMEM((rows // GROUP + fams + 1, 3), I32),
            pltpu.SMEM((2, fams), I32),
            pltpu.SMEM((rows + 1,), I32),
            pltpu.SemaphoreType.DMA((2,)),
            pltpu.SemaphoreType.DMA((fams,)),
            pltpu.SemaphoreType.DMA((fams,)),
        ]
        return pl.pallas_call(
            body,
            out_shape=jax.ShapeDtypeStruct((owners, row_dev * head_dim + 16, width), BF16),
            in_specs=[smem_spec()] * 2 + [vmem_spec()] + [any_spec()] * 4 + [vmem_spec()] * len(last),
            out_specs=vmem_spec(),
            scratch_shapes=scratch,
            compiler_params=params(40),
            name="attend_own" if own is None else "attend",
            cost_estimate=pl.CostEstimate(
                flops=8 * rows * width * prefix_dev * head_dim,
                bytes_accessed=14 * MIB,
                transcendentals=rows * width * prefix_dev,
            ),
        )(
            place,
            meta,
            recv,
            in_hbm(keys),
            in_hbm(values),
            in_hbm(suffix_key_pools[0]),
            in_hbm(suffix_value_pools[0]),
            *last,
        )

    def merge(returned):
        return pl.pallas_call(
            merge_kernel,
            out_shape=[
                jax.ShapeDtypeStruct((row_dev, steps, features), BF16),
                jax.ShapeDtypeStruct((devices, row_dev * steps, features), BF16),
            ],
            in_specs=[vmem_spec()] * 4,
            out_specs=[vmem_spec()] * 2,
            compiler_params=params(12),
            name="merge",
        )(returned, flat_query, new_keys[:, 0], incoming_values[:, 0])


    def project(tokens):
        block = sum(t.shape[2] * t.shape[3] for t in tokens)
        return pl.pallas_call(
            project_kernel,
            out_shape=[
                jax.ShapeDtypeStruct((chips, block, columns), BF16),
                jax.ShapeDtypeStruct((chips, block, columns), F32),
            ],
            in_specs=[smem_spec()] + [vmem_spec()] * (len(tokens) + 1),
            out_specs=[vmem_spec()] * 2,
            compiler_params=params(16),
            name="project",
        )(core.astype(I32).reshape(1), *tokens, out_weight)

    def chip_perm(shift):
        return [(y * 2 + c, (y + shift) % chips * 2 + c) for y in range(chips) for c in range(2)]

    def project_and_sum(tokens):
        away, own = project(
            [t.reshape(chips, 2, devices // heads, -1, features) for t in tokens]
        )
        partner = [(y * 2 + c, y * 2 + 1 - c) for y in range(chips) for c in range(2)]
        arrived = lax.ppermute(away, "kv", partner)
        both = own + arrived.astype(F32)
        total = lax.dynamic_index_in_dim(both, chip, 0, keepdims=False)
        for shift in sorted(range(1, chips), key=lambda d: -min(d, chips - d)):
            part = lax.dynamic_index_in_dim(both, (chip + shift) % chips, 0, keepdims=False)
            part = lax.ppermute(part.astype(BF16), "kv", chip_perm(shift))
            total = total + part.astype(F32)
        return total.astype(BF16)

    def exchange(x):
        return lax.all_to_all(x, "grp", 0, 0, tiled=True)

    packed, *pages = prepare()
    recv = exchange(packed)
    pages = arrange(pages)
    own = attend(lax.dynamic_slice_in_dim(packed, lax.axis_index("grp"), 1), pages)
    attended, spread = merge(exchange(attend(recv, pages, own)))
    mixed = project_and_sum([exchange(spread)])
    return (attended, mixed)


def solution(mesh):
    in_specs = (
        P("grp", "kv", None, None),
        P("grp", "kv", None, None),
        P("grp", "kv", None, None),
        P("grp"),
        P(None, "grp"),
        P("kv", "grp", None, None),
        P("kv", "grp", None, None),
        P("grp"),
        P("grp", None),
        P("grp", None),
        P("kv", "grp", None, None),
        P("kv", "grp", None, None),
        P("kv", "grp"),
    )
    out_specs = (P("grp", None, "kv"), P("kv", "grp"))
    return jax.shard_map(
        on_device, mesh=mesh, in_specs=in_specs, out_specs=out_specs, check_vma=False
    )
```

```python
import functools
import math

import jax
import jax.numpy as jnp
from jax import lax
from jax.experimental import pallas as pl
from jax.experimental.pallas import tpu as pltpu
from jax.sharding import PartitionSpec as P

F32 = jnp.float32
BF16 = jnp.bfloat16
I32 = jnp.int32
NT = (((1,), (1,)), ((), ()))
TN = (((0,), (0,)), ((), ()))
LOG2E = math.log2(math.e)
NEG = -1e30
MIB = 1024 * 1024
GROUP = 2
KEY_BLOCK = 1024
KEY_SUB = 512
UNIT = 4


def vmem_spec():
    return pl.BlockSpec(memory_space=pltpu.VMEM)


def smem_spec():
    return pl.BlockSpec(memory_space=pltpu.SMEM)


def any_spec():
    return pl.BlockSpec(memory_space=pl.ANY)


def in_hbm(x):
    return pltpu.with_memory_space_constraint(x, pltpu.HBM)


def params(mib):
    return pltpu.CompilerParams(vmem_limit_bytes=mib * MIB)


def list_pages(base, family_ref, length_ref, holder_ref, slot_ref, devices, cap, page_len):
    rows, pages = holder_ref.shape
    lanes = 128
    holder_of = lax.broadcasted_iota(I32, (devices, lanes), 0)
    lane = lax.broadcasted_iota(I32, (devices, lanes), 1)
    listed = jnp.full((devices, lanes), -1, I32)
    for r in range(rows):
        listed = jnp.where(lane == rows * cap + r, family_ref[r], listed)
        length = length_ref[r]

        def add_page(c, carry):
            listed, count = carry
            live = jnp.clip(length - c * page_len, 0, page_len)
            holder = jnp.where(live > 0, holder_ref[r, c], -1)
            entry = (slot_ref[r, c] - base) * page_len + live - 1
            here = holder_of == holder
            listed = jnp.where(here & (lane == count), entry, listed)
            return listed, count + here.astype(I32)

        start = jnp.full((devices, lanes), r * cap, I32)
        listed, _ = lax.fori_loop(0, pages, add_page, (listed, start), unroll=8)
    return listed


def arrange_pages(
    table_ref, loads, key_ref, value_ref, key_done, value_done, key_out, value_out, sems, unroll
):
    pages, page_len, head_dim = key_ref.shape
    fams = key_done.shape[0]
    per_fam = pages // fams
    span = 256
    block = span // page_len
    row = lax.broadcasted_iota(I32, (head_dim, head_dim), 0)
    column = lax.broadcasted_iota(I32, (head_dim, head_dim), 1)
    identity = (row == column).astype(F32).astype(BF16)
    stores = []
    loads[0].wait()
    for f in range(fams):

        def turn_block(b, carry):
            listed = [table_ref[f, b * block + i] for i in range(block)]
            values = jnp.concatenate([value_ref[page] for page in listed], axis=0)
            turned = lax.dot_general(identity, values, NT, preferred_element_type=F32)
            value_done[f, :, pl.ds(pl.multiple_of(b * span, span), span)] = turned.astype(BF16)
            return carry

        lax.fori_loop(0, per_fam // block, turn_block, 0, unroll=min(2 * unroll, per_fam // block))
        stores.append(pltpu.make_async_copy(value_done.at[f], value_out.at[f], sems.at[f]))
        stores[-1].start()
    loads[1].wait()
    for f in range(fams):

        def move_block(b, carry):
            for i in range(block):
                at = pl.multiple_of(b * span + i * page_len, page_len)
                key_done[f, pl.ds(at, page_len), :] = key_ref[table_ref[f, b * block + i]]
            return carry

        lax.fori_loop(0, per_fam // block, move_block, 0, unroll=unroll)
        stores.append(pltpu.make_async_copy(key_done.at[f], key_out.at[f], sems.at[fams + f]))
        stores[-1].start()
    for store in stores:
        store.wait()


def prepare_kernel(
    place_ref,
    table_hbm,
    key_hbm,
    value_hbm,
    family_hbm,
    length_hbm,
    holder_hbm,
    slot_hbm,
    query_hbm,
    packed_out,
    key_out,
    value_out,
    table_ref,
    key_ref,
    value_ref,
    key_done,
    value_done,
    family_ref,
    length_ref,
    holder_ref,
    slot_ref,
    query_ref,
    tile_ref,
    small_sems,
    sent_sems,
    in_sems,
    out_sems,
    *,
    cap,
    page_len,
):
    devices, _, lanes = packed_out.shape
    body = query_ref.shape[0]
    first = place_ref[0] == 0
    small = [
        pltpu.make_async_copy(src, dst, small_sems.at[i])
        for i, (src, dst) in enumerate(
            (
                (family_hbm, family_ref),
                (length_hbm, length_ref),
                (holder_hbm, holder_ref),
                (slot_hbm, slot_ref),
                (query_hbm, query_ref),
                (table_hbm, table_ref),
            )
        )
    ]
    for load in small:
        load.start()
    loads = [
        pltpu.make_async_copy(value_hbm, value_ref, in_sems.at[0]),
        pltpu.make_async_copy(key_hbm, key_ref, in_sems.at[1]),
    ]

    @pl.when(first)
    def _():
        for load in loads:
            load.start()

    sent = [
        pltpu.make_async_copy(
            query_ref, packed_out.at[g, pl.ds(0, body), :], sent_sems.at[g]
        )
        for g in range(devices)
    ]
    small[4].wait()
    for copy in sent:
        copy.start()
    for i in (0, 1, 2, 3, 5):
        small[i].wait()
    listed = list_pages(
        place_ref[1], family_ref, length_ref, holder_ref, slot_ref, devices, cap, page_len
    ).astype(F32)
    tile_row = lax.broadcasted_iota(I32, (16, lanes), 0)
    for g in range(devices):
        tile = jnp.where(tile_row == 0, jnp.broadcast_to(listed[g : g + 1, :], (16, lanes)), 0.0)
        tile_ref[g] = tile.astype(BF16)
    tiles = pltpu.make_async_copy(
        tile_ref, packed_out.at[:, pl.ds(body, 16), :], sent_sems.at[devices]
    )
    tiles.start()

    @pl.when(first)
    def _():
        arrange_pages(
            table_ref,
            loads,
            key_ref,
            value_ref,
            key_done,
            value_done,
            key_out,
            value_out,
            out_sems,
            2,
        )

    for copy in sent:
        copy.wait()
    tiles.wait()


def arrange_kernel(
    place_ref,
    table_ref,
    key_hbm,
    value_hbm,
    key_before,
    value_before,
    key_out,
    value_out,
    key_ref,
    value_ref,
    key_done,
    value_done,
    in_sems,
    out_sems,
):
    @pl.when(place_ref[0] == 1)
    def _():
        loads = [
            pltpu.make_async_copy(value_hbm, value_ref, in_sems.at[0]),
            pltpu.make_async_copy(key_hbm, key_ref, in_sems.at[1]),
        ]
        for load in loads:
            load.start()
        arrange_pages(
            table_ref,
            loads,
            key_ref,
            value_ref,
            key_done,
            value_done,
            key_out,
            value_out,
            out_sems,
            8,
        )


def attend_kernel(
    place_ref,
    meta_ref,
    recv_ref,
    key_hbm,
    value_hbm,
    suffix_key_hbm,
    suffix_value_hbm,
    own_ref,
    out_ref,
    key_ref,
    value_ref,
    suffix_key_ref,
    suffix_value_ref,
    score_a,
    score_b,
    top_a,
    top_b,
    score_s,
    top_s,
    lse_ref,
    pair_ref,
    count_ref,
    many_ref,
    sems,
    key_sems,
    value_sems,
    *,
    rows_dev,
    cap,
    page_len,
    width,
):
    devices = out_ref.shape[0]
    rows = devices * rows_dev
    me = place_ref[1] // cap
    owner_base = me if own_ref is None else 0
    fams, prefix, head_dim = key_ref.shape
    scale = LOG2E / math.sqrt(head_dim)
    blocks = prefix // KEY_BLOCK
    subs = KEY_BLOCK // KEY_SUB
    buffers = ((score_a, top_a), (score_b, top_b))

    def key_load(f):
        return pltpu.make_async_copy(key_hbm.at[f], key_ref.at[f], key_sems.at[f])

    def value_load(f):
        return pltpu.make_async_copy(value_hbm.at[f], value_ref.at[f], value_sems.at[f])

    suffix_loads = [
        pltpu.make_async_copy(suffix_key_hbm, suffix_key_ref, sems.at[0]),
        pltpu.make_async_copy(suffix_value_hbm, suffix_value_ref, sems.at[1]),
    ]
    key_load(0).start()
    suffix_loads[0].start()
    value_load(0).start()
    suffix_loads[1].start()
    for f in range(1, fams):
        key_load(f).start()
        value_load(f).start()

    def row_family(r):
        return meta_ref[r // rows_dev, rows_dev * cap + r % rows_dev]

    for f in range(fams):
        count_ref[0, f] = 0

    def is_taken(r):
        return True if own_ref is None else r // rows_dev != me

    def count_row(r, n):
        fam = row_family(r)
        taken = is_taken(r)
        count_ref[0, fam] = count_ref[0, fam] + jnp.int32(taken)
        many_ref[n] = r
        more = meta_ref[r // rows_dev, (r % rows_dev) * cap + UNIT] >= 0
        return n + (taken & more).astype(I32)

    many = lax.fori_loop(0, rows, count_row, 0, unroll=4)
    groups = 0
    for f in range(fams):
        count_ref[1, f] = 2 * groups
        groups = groups + (count_ref[0, f] + 1) // 2

    def place_row(r, carry):
        @pl.when(is_taken(r))
        def _():
            fam = row_family(r)
            at = count_ref[1, fam]
            count_ref[1, fam] = at + 1
            pair_ref[at // 2, 0] = fam
            pair_ref[at // 2, 1 + at % 2] = r

            @pl.when(at % 2 == 0)
            def _():
                pair_ref[at // 2, 2] = r

        return carry

    lax.fori_loop(0, rows, place_row, 0, unroll=4)
    count_ref[0, 0] = 0

    def families_to(fam):
        def one(f, carry):
            key_load(f).wait()
            value_load(f).wait()
            return carry

        lax.fori_loop(count_ref[0, 0], fam + 1, one, 0)
        count_ref[0, 0] = jnp.maximum(count_ref[0, 0], fam + 1)

    tail = rows_dev * head_dim
    lse_ref[...] = jnp.zeros_like(lse_ref)

    def load_queries(g):
        parts = []
        for i in range(GROUP):
            r = pair_ref[g, 1 + i]
            at = pl.multiple_of((r % rows_dev) * width, width)
            parts.append(recv_ref[r // rows_dev, pl.ds(at, width), :])
        return jnp.concatenate(parts, axis=0)

    def fold_max(scores):
        return jnp.max(scores.reshape(scores.shape[0] // 8, 8, scores.shape[1]), axis=0)

    def fold_sum(values):
        return jnp.sum(values.reshape(values.shape[0] // 8, 8, values.shape[1]), axis=0)

    def score_sub(query, fam, block, sub, into):
        at = block * KEY_BLOCK + sub * KEY_SUB
        scores = lax.dot_general(
            key_ref[fam, at : at + KEY_SUB, :], query, NT, preferred_element_type=F32
        )
        into[0][sub * KEY_SUB : (sub + 1) * KEY_SUB, :] = scores
        return fold_max(scores)

    token = lax.broadcasted_iota(I32, (page_len, width), 0)

    def listed_pages(r, unit):
        owner = r // rows_dev
        found = []
        for p in range(UNIT):
            entry = meta_ref[owner, (r % rows_dev) * cap + unit * UNIT + p]
            live = jnp.where(entry >= 0, entry % page_len + 1, 0)
            page = (owner_base + owner) * cap + jnp.maximum(entry, 0) // page_len
            found.append((page, live))
        return found

    def pair_pages(g):
        found = []
        for i in range(GROUP):
            found += listed_pages(pair_ref[g, 1 + i], 0)
        return found

    def suffix_scores(query, pages):
        keys = jnp.concatenate([suffix_key_ref[page] for page, _ in pages], axis=0)
        return lax.dot_general(keys, query, NT, preferred_element_type=F32)

    def suffix_part(weight, pages):
        values = jnp.concatenate([suffix_value_ref[page] for page, _ in pages], axis=0)
        return lax.dot_general(values, weight.astype(BF16), TN, preferred_element_type=F32)

    def score_suffix(query, pages):
        scores = suffix_scores(query, pages)
        dead = jnp.full((page_len, width), NEG, F32)
        tops = []
        for i in range(GROUP):
            cols = slice(i * width, (i + 1) * width)
            top = None
            for p, (_, live) in enumerate(pages):
                at = slice(p * page_len, (p + 1) * page_len)
                if p // UNIT != i:
                    score_s[at, cols] = dead
                    continue
                part = jnp.where(token < live, scores[at, cols], NEG)
                score_s[at, cols] = part
                sub_top = fold_max(part)
                top = sub_top if top is None else jnp.maximum(top, sub_top)
            tops.append(top)
        top_s[...] = jnp.concatenate(tops, axis=1)

    first_query = load_queries(0)
    first_fam = pair_ref[0, 0]
    families_to(first_fam)
    suffix_loads[0].wait()
    top = None
    for s in range(subs):
        sub_top = score_sub(first_query, first_fam, 0, s, buffers[0])
        top = sub_top if top is None else jnp.maximum(top, sub_top)
    top_a[...] = top
    score_suffix(first_query, pair_pages(0))
    suffix_loads[1].wait()

    def attend_group(g, carry, loading=True):
        fam = pair_ref[g, 0]
        after = jnp.minimum(g + 1, groups - 1)
        next_fam = pair_ref[after, 0]
        if loading:
            families_to(next_fam)
        query = load_queries(g)
        next_query = load_queries(after)
        peak = total = acc = pending = None

        def value_part(at, weight):
            return jnp.dot(
                value_ref[fam, :, at : at + KEY_SUB], weight, preferred_element_type=F32
            )

        for b in range(blocks):
            now, later = buffers[b % 2], buffers[(b + 1) % 2]
            block_top = now[1][...]
            if b == 0:
                block_top = jnp.maximum(block_top, top_s[...])
            block_peak = jnp.max(block_top, axis=0, keepdims=True) * scale
            if peak is None:
                new_peak = block_peak
            else:
                new_peak = jnp.maximum(peak, block_peak)
                factor = jnp.exp2(peak - new_peak)
                total = total * factor
                acc = (acc + value_part(*pending)) * factor
                pending = None
            peak = new_peak
            if b == 0:
                weight = jnp.exp2(score_s[...] * scale - peak)
                total = fold_sum(weight)
                acc = suffix_part(weight, pair_pages(g))
            if b + 1 == blocks:
                score_suffix(next_query, pair_pages(after))
            top = None
            for s in range(subs):
                if b + 1 < blocks:
                    sub_top = score_sub(query, fam, b + 1, s, later)
                else:
                    sub_top = score_sub(next_query, next_fam, 0, s, later)
                top = sub_top if top is None else jnp.maximum(top, sub_top)
                if pending is not None:
                    acc = acc + value_part(*pending)
                weight = jnp.exp2(now[0][s * KEY_SUB : (s + 1) * KEY_SUB, :] * scale - peak)
                total = total + fold_sum(weight)
                pending = (b * KEY_BLOCK + s * KEY_SUB, weight.astype(BF16))
            later[1][...] = top
        acc = acc + value_part(*pending)
        total = jnp.sum(total, axis=0, keepdims=True)
        lse = peak + jnp.log2(total)
        acc = (acc * (1.0 / total)).astype(BF16)
        for i in range(GROUP):
            cols = slice(i * width, (i + 1) * width)
            put_row(pair_ref[g, 1 + i], acc[:, cols], lse[:, cols])
        return carry

    def row_place(r):
        return pl.ds(pl.multiple_of((r % rows_dev) * head_dim, head_dim), head_dim)

    def put_row(r, acc, lse):
        owner, at = r // rows_dev, r % rows_dev
        high = lse.astype(BF16).astype(F32)
        middle = (lse - high).astype(BF16).astype(F32)
        out_ref[owner, row_place(r), :] = acc
        lse_ref[owner, pl.ds(at, 1), :] = high
        lse_ref[owner, pl.ds(rows_dev + at, 1), :] = middle
        lse_ref[owner, pl.ds(2 * rows_dev + at, 1), :] = lse - high - middle

    def more_suffix(r, unit):
        owner, at = r // rows_dev, r % rows_dev
        begin = pl.multiple_of(at * width, width)
        pages = listed_pages(r, unit)
        scores = suffix_scores(recv_ref[owner, pl.ds(begin, width), :], pages)
        scores = jnp.concatenate(
            [
                jnp.where(token < live, scores[p * page_len : (p + 1) * page_len, :], NEG)
                for p, (_, live) in enumerate(pages)
            ],
            axis=0,
        )
        lse = (
            lse_ref[owner, pl.ds(at, 1), :]
            + lse_ref[owner, pl.ds(rows_dev + at, 1), :]
            + lse_ref[owner, pl.ds(2 * rows_dev + at, 1), :]
        )
        peak = jnp.maximum(lse, jnp.max(scores, axis=0, keepdims=True) * scale)
        weight = jnp.exp2(scores * scale - peak)
        factor = jnp.exp2(lse - peak)
        total = factor + jnp.sum(weight, axis=0, keepdims=True)
        acc = out_ref[owner, row_place(r), :].astype(F32) * factor + suffix_part(weight, pages)
        put_row(r, (acc * (1.0 / total)).astype(BF16), peak + jnp.log2(total))

    def finish_row(n, carry):
        r = many_ref[n]
        for unit in range(1, cap // UNIT):

            @pl.when(meta_ref[r // rows_dev, (r % rows_dev) * cap + unit * UNIT] >= 0)
            def _():
                more_suffix(r, unit)

        return carry

    early = jnp.minimum(groups, 6)
    lax.fori_loop(0, early, attend_group, 0)
    families_to(fams - 1)
    if own_ref is not None:
        lax.fori_loop(early, groups, functools.partial(attend_group, loading=False), 0)
    lax.fori_loop(0, many, finish_row, 0)
    out_ref[:, tail:, :] = lse_ref[...].astype(BF16)
    if own_ref is not None:
        out_ref[me] = own_ref[0]


def merge_kernel(
    recv_ref,
    query_ref,
    key_ref,
    value_ref,
    out_ref,
    send_ref,
):
    devices, _, head_dim = recv_ref.shape
    rows, steps, _ = out_ref.shape
    width = query_ref.shape[0] // rows
    scale = LOG2E / math.sqrt(head_dim)
    tail = recv_ref[:, rows * head_dim :, :].astype(F32)
    fresh = lax.broadcasted_iota(I32, (steps, width), 0)
    step = lax.broadcasted_iota(I32, (steps, width), 1) % steps
    results = []
    for r in range(rows):
        scores = lax.dot_general(
            key_ref[r],
            query_ref[r * width : (r + 1) * width, :],
            NT,
            preferred_element_type=F32,
        )
        scores = jnp.where(fresh <= step, scores * scale, NEG)
        new_peak = jnp.max(scores, axis=0, keepdims=True)
        weight = jnp.exp2(scores - new_peak)
        new_total = jnp.sum(weight, axis=0, keepdims=True)
        new_acc = lax.dot_general(
            value_ref[r], weight.astype(BF16), TN, preferred_element_type=F32
        )
        lse = tail[:, r, :] + tail[:, rows + r, :] + tail[:, 2 * rows + r, :]
        peak = jnp.maximum(jnp.max(lse, axis=0, keepdims=True), new_peak)
        share = jnp.exp2(lse - peak)
        new_share = jnp.exp2(new_peak - peak)
        total = jnp.sum(share, axis=0, keepdims=True) + new_share * new_total
        acc = new_acc * new_share
        for g in range(devices):
            part = recv_ref[g, r * head_dim : (r + 1) * head_dim, :].astype(F32)
            acc = acc + part * share[g : g + 1, :]
        results.append((acc * (1.0 / total)).T)
        if r % 2 == 0:
            continue
        for h in range(width // steps):
            cols = slice(h * head_dim, (h + 1) * head_dim)
            pair = [turned[h * steps : (h + 1) * steps, :] for turned in results[-2:]]
            for i, tile in enumerate(pair):
                out_ref[r - 1 + i, :, cols] = tile.astype(BF16)
            both = jnp.concatenate(pair, axis=0).astype(BF16)
            for g in range(devices):
                send_ref[g, (r - 1) * steps : (r + 1) * steps, cols] = both


def project_kernel(core_ref, *refs):
    token_refs, weight_ref, away_ref, own_ref = refs[:-3], *refs[-3:]
    chips, tokens_out, columns = own_ref.shape
    groups = token_refs[0].shape[2]
    step = 256
    for side, out_ref in ((1 - core_ref[0], away_ref), (core_ref[0], own_ref)):
        for c in range(columns // step):
            cols = slice(c * step, (c + 1) * step)
            at = 0
            for token_ref in token_refs:
                steps, features = token_ref.shape[3:]
                tokens = jnp.concatenate([token_ref[y, side] for y in range(chips)], axis=0)
                part = jnp.dot(
                    tokens.reshape(-1, features), weight_ref[:, cols], preferred_element_type=F32
                )
                part = part.astype(out_ref.dtype).reshape(chips, groups, steps, step)
                for g in range(groups):
                    row = g * (tokens_out // groups) + at
                    out_ref[:, row : row + steps, cols] = part[:, g]
                at += steps


def on_device(
    queries,
    new_keys,
    incoming_values,
    family,
    prefix_table,
    prefix_key_pool,
    prefix_value_pool,
    suffix_len,
    suffix_holder,
    suffix_slot,
    suffix_key_pools,
    suffix_value_pools,
    out_weight,
):
    devices = lax.axis_size("grp")
    heads = lax.axis_size("kv")
    row_dev, local_heads, steps, head_dim = queries.shape
    width = local_heads * steps
    features = local_heads * head_dim
    fams, pages_dev = prefix_table.shape
    page_len = prefix_key_pool.shape[2]
    prefix_dev = pages_dev * page_len
    own_pages = suffix_key_pools.shape[1]
    cap = own_pages // devices
    columns = out_weight.shape[1]
    core = lax.axis_index("kv") % 2
    chip = lax.axis_index("kv") // 2
    chips = heads // 2
    flat_query = queries.reshape(row_dev * width, head_dim)

    place = jnp.stack([core, lax.axis_index("grp") * cap]).astype(I32)
    key_shape = (fams, prefix_dev, head_dim)
    value_shape = (fams, head_dim, prefix_dev)
    page_scratch = [
        pltpu.VMEM(prefix_key_pool.shape[1:], BF16),
        pltpu.VMEM(prefix_value_pool.shape[1:], BF16),
        pltpu.VMEM(key_shape, BF16),
        pltpu.VMEM(value_shape, BF16),
    ]
    page_operands = [
        in_hbm(prefix_table),
        in_hbm(prefix_key_pool[0]),
        in_hbm(prefix_value_pool[0]),
    ]

    def prepare():
        return pl.pallas_call(
            functools.partial(prepare_kernel, cap=cap, page_len=page_len),
            out_shape=[
                pltpu.HBM((devices, row_dev * width + 16, head_dim), BF16),
                pltpu.HBM(key_shape, BF16),
                pltpu.HBM(value_shape, BF16),
            ],
            in_specs=[smem_spec()] + [any_spec()] * 8,
            out_specs=[any_spec()] * 3,
            scratch_shapes=[pltpu.SMEM(prefix_table.shape, I32)]
            + page_scratch
            + [
                pltpu.SMEM(family.shape, I32),
                pltpu.SMEM(suffix_len.shape, I32),
                pltpu.SMEM(suffix_holder.shape, I32),
                pltpu.SMEM(suffix_slot.shape, I32),
                pltpu.VMEM(flat_query.shape, BF16),
                pltpu.VMEM((devices, 16, head_dim), BF16),
                pltpu.SemaphoreType.DMA((6,)),
                pltpu.SemaphoreType.DMA((devices + 1,)),
                pltpu.SemaphoreType.DMA((2,)),
                pltpu.SemaphoreType.DMA((2 * fams,)),
            ],
            compiler_params=params(24),
            name="prepare",
        )(
            place,
            *page_operands,
            in_hbm(family),
            in_hbm(suffix_len),
            in_hbm(suffix_holder),
            in_hbm(suffix_slot),
            in_hbm(flat_query),
        )

    def arrange(before):
        return pl.pallas_call(
            arrange_kernel,
            out_shape=[pltpu.HBM(key_shape, BF16), pltpu.HBM(value_shape, BF16)],
            in_specs=[smem_spec()] * 2 + [any_spec()] * 4,
            out_specs=[any_spec()] * 2,
            input_output_aliases={4: 0, 5: 1},
            scratch_shapes=page_scratch
            + [
                pltpu.SemaphoreType.DMA((2,)),
                pltpu.SemaphoreType.DMA((2 * fams,)),
            ],
            compiler_params=params(24),
            name="arrange",
            cost_estimate=pl.CostEstimate(flops=0, bytes_accessed=20 * MIB, transcendentals=0),
        )(place, *page_operands, *[in_hbm(x) for x in before])

    def attend(recv, pages, own=None):
        owners = recv.shape[0]
        meta = recv[:, row_dev * width, :].astype(I32)
        span = GROUP * width
        rows = owners * row_dev
        keys, values = pages
        kernel = functools.partial(
            attend_kernel,
            rows_dev=row_dev,
            cap=cap,
            page_len=page_len,
            width=width,
        )
        last = [] if own is None else [own]
        body = kernel
        if own is None:
            body = lambda *refs: kernel(*refs[:7], None, *refs[7:])
        scratch = [
            pltpu.VMEM(keys.shape, BF16),
            pltpu.VMEM(values.shape, BF16),
            pltpu.VMEM(suffix_key_pools.shape[1:], BF16),
            pltpu.VMEM(suffix_value_pools.shape[1:], BF16),
            pltpu.VMEM((KEY_BLOCK, span), F32),
            pltpu.VMEM((KEY_BLOCK, span), F32),
            pltpu.VMEM((8, span), F32),
            pltpu.VMEM((8, span), F32),
            pltpu.VMEM((GROUP * UNIT * page_len, span), F32),
            pltpu.VMEM((8, span), F32),
            pltpu.VMEM((owners, 16, width), F32),
            pltpu.SMEM((rows // GROUP + fams + 1, 3), I32),
            pltpu.SMEM((2, fams), I32),
            pltpu.SMEM((rows + 1,), I32),
            pltpu.SemaphoreType.DMA((2,)),
            pltpu.SemaphoreType.DMA((fams,)),
            pltpu.SemaphoreType.DMA((fams,)),
        ]
        return pl.pallas_call(
            body,
            out_shape=jax.ShapeDtypeStruct((owners, row_dev * head_dim + 16, width), BF16),
            in_specs=[smem_spec()] * 2 + [vmem_spec()] + [any_spec()] * 4 + [vmem_spec()] * len(last),
            out_specs=vmem_spec(),
            scratch_shapes=scratch,
            compiler_params=params(40),
            name="attend_own" if own is None else "attend",
            cost_estimate=pl.CostEstimate(
                flops=8 * rows * width * prefix_dev * head_dim,
                bytes_accessed=14 * MIB,
                transcendentals=rows * width * prefix_dev,
            ),
        )(
            place,
            meta,
            recv,
            in_hbm(keys),
            in_hbm(values),
            in_hbm(suffix_key_pools[0]),
            in_hbm(suffix_value_pools[0]),
            *last,
        )

    def merge(returned):
        return pl.pallas_call(
            merge_kernel,
            out_shape=[
                jax.ShapeDtypeStruct((row_dev, steps, features), BF16),
                jax.ShapeDtypeStruct((devices, row_dev * steps, features), BF16),
            ],
            in_specs=[vmem_spec()] * 4,
            out_specs=[vmem_spec()] * 2,
            compiler_params=params(12),
            name="merge",
        )(returned, flat_query, new_keys[:, 0], incoming_values[:, 0])


    def project(tokens):
        block = sum(t.shape[2] * t.shape[3] for t in tokens)
        return pl.pallas_call(
            project_kernel,
            out_shape=[
                jax.ShapeDtypeStruct((chips, block, columns), BF16),
                jax.ShapeDtypeStruct((chips, block, columns), F32),
            ],
            in_specs=[smem_spec()] + [vmem_spec()] * (len(tokens) + 1),
            out_specs=[vmem_spec()] * 2,
            compiler_params=params(16),
            name="project",
        )(core.astype(I32).reshape(1), *tokens, out_weight)

    def chip_perm(shift):
        return [(y * 2 + c, (y + shift) % chips * 2 + c) for y in range(chips) for c in range(2)]

    def project_and_sum(tokens):
        away, own = project(
            [t.reshape(chips, 2, devices // heads, -1, features) for t in tokens]
        )
        partner = [(y * 2 + c, y * 2 + 1 - c) for y in range(chips) for c in range(2)]
        arrived = lax.ppermute(away, "kv", partner)
        both = own + arrived.astype(F32)
        total = lax.dynamic_index_in_dim(both, chip, 0, keepdims=False)
        for shift in sorted(range(1, chips), key=lambda d: -min(d, chips - d)):
            part = lax.dynamic_index_in_dim(both, (chip + shift) % chips, 0, keepdims=False)
            part = lax.ppermute(part.astype(BF16), "kv", chip_perm(shift))
            total = total + part.astype(F32)
        return total.astype(BF16)

    def exchange(x):
        return lax.all_to_all(x, "grp", 0, 0, tiled=True)

    packed, *pages = prepare()
    recv = exchange(packed)
    pages = arrange(pages)
    own = attend(lax.dynamic_slice_in_dim(packed, lax.axis_index("grp"), 1), pages)
    attended, spread = merge(exchange(attend(recv, pages, own)))
    mixed = project_and_sum([exchange(spread)])
    return (attended, mixed)


def solution(mesh):
    in_specs = (
        P("grp", "kv", None, None),
        P("grp", "kv", None, None),
        P("grp", "kv", None, None),
        P("grp"),
        P(None, "grp"),
        P("kv", "grp", None, None),
        P("kv", "grp", None, None),
        P("grp"),
        P("grp", None),
        P("grp", None),
        P("kv", "grp", None, None),
        P("kv", "grp", None, None),
        P("kv", "grp"),
    )
    out_specs = (P("grp", None, "kv"), P("kv", "grp"))
    return jax.shard_map(
        on_device, mesh=mesh, in_specs=in_specs, out_specs=out_specs, check_vma=False
    )
```
